128 devices in a mesh: rep: 16 (over x_lo, z, core), shard: 8 (over x_hi, y).
Axes of the slice: x: 4 (x_hi: 2, x_lo: 2; x = x_hi * 2 + x_lo), y: 4, z: 4, core: 2. Of those that a mesh axis runs over, the one named last changes fastest.
Arguments:
- latents: bfloat16 [16, 1024, 1024], P('rep', 'shard'), may hold values from -6 to 6
- cond: bfloat16 [16, 1024], P('rep'), may hold values from -6 to 6
- cotangent: bfloat16 [16, 1024, 1024], P('rep', 'shard'), may hold values from -6 to 6
- w_qkv: bfloat16 [1024, 3072], P('shard'), may hold values from -0.1875 to 0.1875
- bias_qv: bfloat16 [2048], P('shard'), may hold values from -3 to 3
- w_proj: bfloat16 [1024, 1024], P('shard'), may hold values from -1 to 1
- b_proj: bfloat16 [1024], P('shard'), may hold values from -3 to 3
- w_fc1: bfloat16 [1024, 4096], P('shard'), may hold values from -0.1875 to 0.1875
- b_fc1: bfloat16 [4096], P('shard'), may hold values from -3 to 3
- w_fc2: bfloat16 [4096, 1024], P('shard'), may hold values from -0.09375 to 0.09375
- b_fc2: bfloat16 [1024], P('shard'), may hold values from -3 to 3
- w_ada: bfloat16 [1024, 6144], P('shard'), may hold values from -0.1875 to 0.1875
- b_ada: bfloat16 [6144], P('shard'), may hold values from -3 to 3
Outputs:
- output: bfloat16 [16, 1024, 1024], P('rep', 'shard')
- grad_latents: bfloat16 [16, 1024, 1024], P('rep', 'shard')
- grad_cond: float32 [16, 1024], P('rep')
- grad_w_qkv: float32 [1024, 3072], P('shard')
- grad_bias_qv: float32 [2048], P('shard')
- grad_w_proj: float32 [1024, 1024], P('shard')
- grad_b_proj: float32 [1024], P('shard')
- grad_w_fc1: float32 [1024, 4096], P('shard')
- grad_b_fc1: float32 [4096], P('shard')
- grad_w_fc2: float32 [4096, 1024], P('shard')
- grad_b_fc2: float32 [1024], P('shard')
- grad_w_ada: float32 [1024, 6144], P('shard')
- grad_b_ada: float32 [6144], P('shard')
The draws below stay inside these ranges and needn't reach their ends.
All inputs are finite; a program needn't handle non-finite values.
Results may differ from the reference program's by a relative error of at most 0.025.
Values may be sent and summed in bfloat16 or wider, within the bound.
No kernel may reach another device: no remote copies, remote signals or barrier semaphores. Data moves between devices by JAX's collectives and lax.ppermute only.
A program may use at most 192 MiB of HBM per device.

```python
import jax
import jax.numpy as jnp
from jax import lax

D = 1024
HEADS = 16
HEAD = 64
FF = 4096
SEQ = 1024
LATENTS = 16


def block_levels(stream_key, shape, cuts, smallest, largest):
    def one(dim, shards_of):
        heights = jax.random.uniform(jax.random.fold_in(jax.random.fold_in(stream_key, 6), dim), (shards_of,), jnp.float32, smallest / len(cuts), largest / len(cuts))
        return jnp.repeat(jnp.exp(heights), shape[dim] // shards_of).reshape((-1,) + (1,) * (len(shape) - dim - 1))

    factor_of = one(*cuts[0])
    for cut in cuts[1:]:
        factor_of = factor_of * one(*cut)
    return factor_of


def centred(own_key, dims, width, bound, pieces=(), kind=jnp.bfloat16):
    drawn = jax.random.normal(own_key, dims, jnp.float32) * width
    if len(pieces) > 0:
        drawn = block_levels(own_key, dims, pieces, -0.22, 0.18) * drawn
    return jnp.clip(drawn, min=-bound, max=bound).astype(kind)


def setup_inputs(seed: int = 0) -> dict:
    keys = jax.random.split(jax.random.key(seed), 14)
    return {
        "latents": centred(keys[0], (LATENTS, SEQ, D), 1.0, 6.0, ((0, 16), (1, 8))),
        "cond": centred(keys[1], (LATENTS, D), 1.0, 6.0, ((0, 16),)),
        "cotangent": centred(keys[2], (LATENTS, SEQ, D), 1.0, 6.0, ((0, 16), (1, 8))),
        "w_qkv": centred(keys[3], (D, 3 * D), D ** -0.5, 0.1875, ((0, 8),)),
        "bias_qv": centred(keys[4], (2 * D,), 0.5, 3.0, ((0, 8),)),
        "w_proj": centred(keys[5], (D, D), (D * 32 // SEQ) ** -0.5, 1.0, ((0, 8),)),
        "b_proj": centred(keys[6], (D,), 0.5, 3.0, ((0, 8),)),
        "w_fc1": centred(keys[7], (D, FF), D ** -0.5, 0.1875, ((0, 8),)),
        "b_fc1": centred(keys[8], (FF,), 0.5, 3.0, ((0, 8),)),
        "w_fc2": centred(keys[9], (FF, D), FF ** -0.5, 0.09375, ((0, 8),)),
        "b_fc2": centred(keys[10], (D,), 0.5, 3.0, ((0, 8),)),
        "w_ada": centred(keys[11], (D, 6 * D), D ** -0.5, 0.1875, ((0, 8),)),
        "b_ada": centred(keys[12], (6 * D,), 0.5, 3.0, ((0, 8),)),
    }


@jax.custom_vjp
def low(v):
    return lax.optimization_barrier(v.astype(jnp.bfloat16)).astype(jnp.float32)

@jax.custom_vjp
def low_back(v):
    return v

def low_keep(v):
    return (low(v), None)

def low_pass(kept, grad):
    return (grad,)

def back_keep(v):
    return (v, None)

def back_low(kept, grad):
    return (low(grad),)
low.defvjp(low_keep, low_pass)
low_back.defvjp(back_keep, back_low)
epsilon = 1e-06
highest = lax.Precision.HIGHEST

def layer_norm(values):
    centered = values - lax.optimization_barrier(jnp.mean(values, axis=-1, keepdims=True))
    variance = lax.optimization_barrier(jnp.mean(centered * centered, axis=-1, keepdims=True))
    return centered * lax.rsqrt(variance + epsilon)

def sigmoid_linear(values):
    return values / (1.0 + jnp.exp(-values))

def gelu_tanh(values):
    return 0.5 * values * (1.0 + jnp.tanh(0.7978845608028654 * (values + 0.044715 * values * values * values)))

def matrix(left, right):
    return jnp.dot(left, right, precision=highest)

def block(latent, cond_row, w_qkv, bias_qv, w_proj, b_proj, w_fc1, b_fc1, w_fc2, b_fc2, w_ada, b_ada):
    length = latent.shape[0]
    features = latent.shape[1]
    cond_low = low(sigmoid_linear(cond_row))
    modulation = matrix(cond_low[None, :], w_ada)[0] + b_ada
    shift_first, scale_first, gate_first, shift_second, scale_second, gate_second = jnp.split(modulation, 6)
    attend_in = low(layer_norm(latent) * (1.0 + scale_first) + shift_first)
    packed = matrix(attend_in, w_qkv)
    queries = low(low_back(packed[:, :features] + bias_qv[:features]))
    keyset = low(low_back(packed[:, features:2 * features]))
    valueset = low(low_back(packed[:, 2 * features:] + bias_qv[features:]))
    query_heads = queries.reshape(length, HEADS, HEAD)
    key_heads = keyset.reshape(length, HEADS, HEAD)
    value_heads = valueset.reshape(length, HEADS, HEAD)
    scores = low_back(jnp.einsum('qhe,khe->hqk', query_heads, key_heads, precision=highest) * HEAD ** (-0.5))
    row_peak = lax.optimization_barrier(jnp.max(scores, axis=-1, keepdims=True))
    powered = jnp.exp(scores - row_peak)
    attention = low(powered / lax.optimization_barrier(jnp.sum(powered, axis=-1, keepdims=True)))
    mixed_heads = jnp.einsum('hqk,khe->qhe', attention, value_heads, precision=highest).reshape(length, features)
    mixed_heads = low(low_back(mixed_heads))
    branch = low_back(matrix(mixed_heads, w_proj) + b_proj)
    middle = latent + gate_first * branch
    feed_in = low(layer_norm(middle) * (1.0 + scale_second) + shift_second)
    hidden = low_back(matrix(feed_in, w_fc1) + b_fc1)
    active = low(gelu_tanh(hidden))
    branch_second = low_back(matrix(active, w_fc2) + b_fc2)
    return middle + gate_second * branch_second

def reference(latents, cond, cotangent, w_qkv, bias_qv, w_proj, b_proj, w_fc1, b_fc1, w_fc2, b_fc2, w_ada, b_ada):
    params = tuple((weight.astype(jnp.float32) for weight in (w_qkv, bias_qv, w_proj, b_proj, w_fc1, b_fc1, w_fc2, b_fc2, w_ada, b_ada)))

    def per_latent(totals, item):
        latent, cond_row, cot_row = item
        result, pull = jax.vjp(block, latent.astype(jnp.float32), cond_row.astype(jnp.float32), *params)
        grads = pull(cot_row.astype(jnp.float32))
        totals = tuple((total + grad_one for total, grad_one in zip(totals, grads[2:])))
        return (totals, (result.astype(jnp.bfloat16), grads[0].astype(jnp.bfloat16), grads[1]))
    start = tuple((jnp.zeros(weight.shape, jnp.float32) for weight in params))
    totals, (output, grad_latents, grad_cond) = lax.scan(per_latent, start, (latents, cond, cotangent))
    return (output, grad_latents, grad_cond, totals[0], totals[1], totals[2], totals[3], totals[4], totals[5], totals[6], totals[7], totals[8], totals[9])
```

```python
import jax
import jax.numpy as jnp
from jax import lax
from jax.sharding import Mesh, PartitionSpec as P

HEAD = 64
SHARD = ("xh", "y")
CHIPS = ("xl", "z")
REP = ("xl", "z", "core")
OFFSETS = ((0, 0), (0, 1), (0, 3), (0, 2), (1, 0), (1, 1), (1, 3), (1, 2))

epsilon = 1e-06
highest = lax.Precision.HIGHEST
low = jnp.bfloat16
wide = jnp.float32


def shift(value, dx, dy):
    pairs = [(x * 4 + y, ((x + dx) % 2) * 4 + (y + dy) % 4) for x in range(2) for y in range(4)]
    return lax.ppermute(value, SHARD, pairs)


def gather_turned(value):
    return [value] + [shift(value, dx, dy) for dx, dy in OFFSETS[1:]]


def scatter_turned(parts):
    total = parts[0]
    for part, (dx, dy) in zip(parts[1:], OFFSETS[1:]):
        total = total + shift(part.astype(low), dx, (4 - dy) % 4).astype(wide)
    return total


def swap_core(value):
    return lax.ppermute(value, "core", [(0, 1), (1, 0)])


def exchange(value, axes=SHARD):
    return lax.all_to_all(value, axes, 0, 0, tiled=True)


def spread(value, axes=SHARD, count=8):
    return exchange(jnp.broadcast_to(value[None], (count,) + value.shape), axes)


def normalize(values):
    centered = values - jnp.mean(values, axis=-1, keepdims=True)
    inverse = lax.rsqrt(jnp.mean(centered * centered, axis=-1, keepdims=True) + epsilon)
    return centered * inverse, inverse


def normalize_back(norm, inverse, grad):
    return inverse * (
        grad
        - jnp.mean(grad, axis=-1, keepdims=True)
        - norm * jnp.mean(grad * norm, axis=-1, keepdims=True)
    )


def silu(values):
    return values / (1.0 + jnp.exp(-values))


def gelu_tanh(values):
    return (
        0.5
        * values
        * (1.0 + jnp.tanh(0.7978845608028654 * (values + 0.044715 * values * values * values)))
    )


def mul(left, right):
    return lax.dot_general(left, right, (((1,), (0,)), ((), ())), preferred_element_type=wide)


def mul_t(left, right):
    return lax.dot_general(left, right, (((1,), (1,)), ((), ())), preferred_element_type=wide)


def t_mul(left, right):
    return lax.dot_general(left, right, (((0,), (0,)), ((), ())), preferred_element_type=wide)


def core_half(value, core):
    half = value.shape[0] // 2
    keep = lax.dynamic_slice_in_dim(value, core * half, half, 0)
    give = lax.dynamic_slice_in_dim(value, (1 - core) * half, half, 0).astype(low)
    return keep + swap_core(give).astype(wide)


def core_join(value, core):
    other = swap_core(value)
    first = jnp.where(core == 0, value, other)
    second = jnp.where(core == 0, other, value)
    return jnp.concatenate([first, second], axis=0)


def on_device(
    latents, cond, cotangent, w_qkv, bias_qv, w_proj, b_proj, w_fc1, b_fc1, w_fc2, b_fc2, w_ada, b_ada
):
    stream_low = latents[0]
    upstream_low = cotangent[0]
    rows, features = stream_low.shape
    shards = 8
    own = features // shards
    units = w_fc2.shape[0]
    heads = own // HEAD
    place = lax.axis_index(SHARD)
    core = lax.axis_index("core")
    score_scale = HEAD ** (-0.5)

    cond_value = cond.astype(wide)
    cond_silu, silu_pull = jax.vjp(silu, cond_value)
    cond_low = cond_silu.astype(low)
    cond_own = lax.dynamic_slice_in_dim(cond_low, place * own, own, 1)
    mod_part = mul(cond_own, w_ada)[0]
    ada_width = w_ada.shape[1]
    blocks = jnp.arange(shards)[:, None] == place
    mod_part = mod_part + jnp.where(blocks, b_ada.astype(wide)[None, :], 0.0).reshape(ada_width)
    small = jnp.concatenate(
        [mod_part, bias_qv.astype(wide), b_proj.astype(wide), b_fc2.astype(wide)]
    )
    small_all = spread(small)
    modulation = jnp.sum(small_all[:, :ada_width], axis=0)
    shift_first, scale_first, gate_first, shift_second, scale_second, gate_second = jnp.split(
        modulation[None, :], 6, axis=1
    )
    at = ada_width
    bias_wide = small_all[:, at : at + 2 * own].reshape(1, 2 * features)
    at += 2 * own
    proj_bias = small_all[:, at : at + own].reshape(1, features)
    at += own
    second_bias = small_all[:, at : at + own].reshape(1, features)

    tokens = spread(stream_low).reshape(shards * rows, features)
    wq = exchange(
        w_qkv.reshape(own, 3, shards, own).transpose(2, 0, 1, 3).reshape(shards, own, 3 * own)
    ).reshape(features, 3 * own)
    w1 = exchange(w_fc1.reshape(own, shards, units).transpose(1, 0, 2)).reshape(features, units)
    wp = spread(w_proj).reshape(features, features)
    upstream_all = jnp.concatenate(gather_turned(upstream_low), axis=0)

    norm_first, inverse_first = normalize(tokens.astype(wide))
    attend_in = (norm_first * (1.0 + scale_first) + shift_first).astype(low)
    packed = mul(attend_in, wq)
    query_bias = lax.dynamic_slice_in_dim(bias_wide, place * own, own, 1)
    value_bias = lax.dynamic_slice_in_dim(bias_wide, features + place * own, own, 1)
    queries = (packed[:, :own] + query_bias).astype(low)
    keyset = packed[:, own : 2 * own].astype(low)
    valueset = (packed[:, 2 * own :] + value_bias).astype(low)
    length = shards * rows

    def split(value):
        return value.reshape(length, heads, HEAD)

    query_heads, key_heads, value_heads = split(queries), split(keyset), split(valueset)
    scores = (
        jnp.einsum("qhe,khe->hqk", query_heads, key_heads, preferred_element_type=wide)
        * score_scale
    )
    row_peak = jnp.max(scores, axis=-1, keepdims=True)
    powered = jnp.exp(scores - row_peak)
    row_total = jnp.sum(powered, axis=-1, keepdims=True)
    attention = powered / row_total
    log_total = row_peak + jnp.log(row_total)
    mixed = (
        jnp.einsum("hqk,khe->qhe", attention.astype(low), value_heads, preferred_element_type=wide)
        .reshape(length, own)
        .astype(low)
    )
    mixed_tok = exchange(mixed.reshape(shards, rows, own))
    mixed_tok = mixed_tok.transpose(1, 0, 2).reshape(rows, features)
    branch = mul(mixed_tok, wp) + proj_bias
    stream = stream_low.astype(wide)
    middle = stream + gate_first * branch
    norm_second, inverse_second = normalize(middle)
    feed_in = (norm_second * (1.0 + scale_second) + shift_second).astype(low)
    feed_all = jnp.concatenate(gather_turned(feed_in), axis=0)
    hidden = mul(feed_all, w1) + b_fc1.astype(wide)[None, :]
    active_value, gelu_pull = jax.vjp(gelu_tanh, hidden)
    active = active_value.astype(low)
    branch_second_part = mul(active, w_fc2)

    def turned_parts(value):
        return [value[k * rows : (k + 1) * rows] for k in range(shards)]

    grad_branch_second = (upstream_all.astype(wide) * gate_second).astype(low)
    grad_active = mul_t(grad_branch_second, w_fc2)
    grad_hidden = gelu_pull(grad_active)[0].astype(low)
    grad_feed = scatter_turned(turned_parts(mul_t(grad_hidden, w1)))

    branch_second = scatter_turned(turned_parts(branch_second_part)) + second_bias
    output = (middle + gate_second * branch_second).astype(low)

    upstream = upstream_low.astype(wide)
    grad_gate_second = jnp.sum(upstream * branch_second, axis=0)
    grad_scale_second = jnp.sum(grad_feed * norm_second, axis=0)
    grad_shift_second = jnp.sum(grad_feed, axis=0)
    grad_middle = upstream + normalize_back(
        norm_second, inverse_second, grad_feed * (1.0 + scale_second)
    )
    grad_gate_first = jnp.sum(grad_middle * branch, axis=0)
    grad_branch = (grad_middle * gate_first).astype(low)
    grad_mixed_tok = mul_t(grad_branch, wp).astype(low)
    grad_mixed = exchange(grad_mixed_tok.reshape(rows, shards, own).transpose(1, 0, 2))
    grad_mixed = split(grad_mixed.reshape(length, own))

    again_scores = (
        jnp.einsum("qhe,khe->hqk", query_heads, key_heads, preferred_element_type=wide)
        * score_scale
    )
    again = jnp.exp(again_scores - log_total)
    grad_probs = jnp.einsum("qhe,khe->hqk", grad_mixed, value_heads, preferred_element_type=wide)
    grad_value = jnp.einsum(
        "hqk,qhe->khe", again.astype(low), grad_mixed, preferred_element_type=wide
    )
    row_delta = jnp.sum(again * grad_probs, axis=-1, keepdims=True)
    grad_scores = (again * (grad_probs - row_delta)).astype(low)
    grad_query = (
        jnp.einsum("hqk,khe->qhe", grad_scores, key_heads, preferred_element_type=wide)
        * score_scale
    )
    grad_key = (
        jnp.einsum("hqk,qhe->khe", grad_scores, query_heads, preferred_element_type=wide)
        * score_scale
    )
    grad_packed = jnp.concatenate(
        [part.reshape(length, own).astype(low) for part in (grad_query, grad_key, grad_value)],
        axis=1,
    )
    attend_part = mul_t(grad_packed, wq)
    grad_scale_first = jnp.sum(attend_part * norm_first, axis=0)
    grad_shift_first = jnp.sum(attend_part, axis=0)
    attend_sent = exchange(attend_part.astype(low).reshape(shards, rows, features))
    grad_attend = jnp.sum(attend_sent.astype(wide), axis=0)
    norm_own, inverse_own = normalize(stream)
    grad_stream = grad_middle + normalize_back(
        norm_own, inverse_own, grad_attend * (1.0 + scale_first)
    )
    grad_latents = grad_stream.astype(low)

    mod_terms = jnp.concatenate(
        [
            grad_shift_first,
            grad_scale_first,
            grad_gate_first,
            grad_shift_second,
            grad_scale_second,
            grad_gate_second,
            jnp.sum(grad_branch.astype(wide), axis=0),
        ]
    )
    mod_sums = jnp.sum(spread(mod_terms), axis=0)
    grad_modulation = mod_sums[:ada_width]
    proj_bias_term = lax.dynamic_slice_in_dim(mod_sums, ada_width + place * own, own, 0)
    cond_term = jnp.sum(w_ada.astype(wide) * grad_modulation[None, :], axis=1)
    cond_total = spread(cond_term).reshape(1, features)
    grad_cond = silu_pull(cond_total)[0]

    packed_sums = jnp.sum(grad_packed.astype(wide), axis=0)
    second_bias_sums = jnp.sum(grad_branch_second.astype(wide), axis=0)
    rep_terms = jnp.concatenate(
        [
            grad_modulation,
            cond_own[0].astype(wide),
            proj_bias_term,
            jnp.sum(grad_hidden.astype(wide), axis=0),
            lax.dynamic_slice_in_dim(second_bias_sums, place * own, own, 0),
            packed_sums,
        ]
    )
    rep_all = spread(rep_terms, REP, 16)
    grad_w_ada = lax.dot_general(
        rep_all[:, ada_width : ada_width + own],
        rep_all[:, :ada_width],
        (((0,), (0,)), ((), ())),
        precision=highest,
        preferred_element_type=wide,
    )
    rep_sums = jnp.sum(rep_all, axis=0)
    ada_own = ada_width // shards
    grad_b_ada = lax.dynamic_slice_in_dim(rep_sums, place * ada_own, ada_own, 0)
    at = ada_width + own
    grad_b_proj = rep_sums[at : at + own]
    at += own
    grad_b_fc1 = rep_sums[at : at + units]
    at += units
    grad_b_fc2 = rep_sums[at : at + own]
    at += own
    bias_all = spread(jnp.concatenate([rep_sums[at : at + own], rep_sums[at + 2 * own :]]))
    bias_all = jnp.concatenate(
        [bias_all[:, :own].reshape(features), bias_all[:, own:].reshape(features)]
    )
    grad_bias_qv = lax.dynamic_slice_in_dim(bias_all, place * 2 * own, 2 * own, 0)

    def over_rep(value):
        owned = lax.psum_scatter(value.astype(low), CHIPS, scatter_dimension=0, tiled=True)
        return core_join(lax.all_gather(owned, CHIPS, axis=0, tiled=True), core).astype(wide)

    term_second = core_half(t_mul(active, grad_branch_second), core)
    grad_w_fc2 = over_rep(term_second)

    term_first = core_half(t_mul(feed_all, grad_hidden).reshape(shards, own, units).transpose(1, 0, 2).reshape(own, shards * units), core)
    term_first = exchange(
        term_first.astype(low).reshape(own // 2, shards, units).transpose(1, 0, 2)
    )
    term_first = term_first.transpose(1, 0, 2).reshape(own // 2, shards * units)
    grad_w_fc1 = over_rep(term_first)

    term_proj = t_mul(mixed_tok, grad_branch).reshape(shards, own, features)
    term_proj = core_half(term_proj.transpose(1, 0, 2), core)
    term_proj = exchange(term_proj.astype(low).transpose(1, 0, 2))
    grad_w_proj = over_rep(jnp.sum(term_proj.astype(wide), axis=0))

    term_qkv = t_mul(attend_in, grad_packed).reshape(shards, own, 3 * own)
    term_qkv = core_half(term_qkv.transpose(1, 0, 2), core)
    term_qkv = exchange(term_qkv.astype(low).transpose(1, 0, 2))
    term_qkv = (
        term_qkv.reshape(shards, own // 2, 3, own)
        .transpose(1, 2, 0, 3)
        .reshape(own // 2, 3 * features)
    )
    grad_w_qkv = over_rep(term_qkv)

    return (
        output[None],
        grad_latents[None],
        grad_cond,
        grad_w_qkv,
        grad_bias_qv,
        grad_w_proj,
        grad_b_proj,
        grad_w_fc1,
        grad_b_fc1,
        grad_w_fc2,
        grad_b_fc2,
        grad_w_ada,
        grad_b_ada,
    )


def solution(mesh):
    fine = Mesh(mesh.devices.reshape(2, 4, 2, 2, 4), REP + SHARD)
    tokens = P(REP, SHARD, None)
    matrix = P(SHARD, None)
    vector = P(SHARD)
    params = (matrix, vector) * 5
    return jax.shard_map(
        on_device,
        mesh=fine,
        in_specs=(tokens, P(REP, None), tokens) + params,
        out_specs=(tokens, tokens, P(REP, None)) + params,
        check_vma=False,
    )
```

```python
import jax
import jax.numpy as jnp
from jax import lax
from jax.sharding import Mesh, PartitionSpec as P

HEAD = 64
SHARD = ("xh", "y")
CHIPS = ("xl", "z")
REP = ("xl", "z", "core")
LANES = 128

epsilon = 1e-06
highest = lax.Precision.HIGHEST
low = jnp.bfloat16
wide = jnp.float32


def swap_core(value):
    return lax.ppermute(value, "core", [(0, 1), (1, 0)])


def exchange(value, axes=SHARD):
    return lax.all_to_all(value, axes, 0, 0, tiled=True)


def copies(value):
    return jnp.broadcast_to(value[None], (8,) + value.shape)


def as_rows(value, count):
    rows = value.reshape(-1, LANES)
    return jnp.pad(rows, ((0, count - rows.shape[0]), (0, 0)))


def normalize(values):
    centered = values - jnp.mean(values, axis=-1, keepdims=True)
    inverse = lax.rsqrt(jnp.mean(centered * centered, axis=-1, keepdims=True) + epsilon)
    return centered * inverse, inverse


def normalize_back(norm, inverse, grad):
    return inverse * (
        grad
        - jnp.mean(grad, axis=-1, keepdims=True)
        - norm * jnp.mean(grad * norm, axis=-1, keepdims=True)
    )


def silu(values):
    return values / (1.0 + jnp.exp(-values))


def gelu_tanh(values):
    return (
        0.5
        * values
        * (1.0 + jnp.tanh(0.7978845608028654 * (values + 0.044715 * values * values * values)))
    )


def mul(left, right):
    return lax.dot_general(left, right, (((1,), (0,)), ((), ())), preferred_element_type=wide)


def mul_t(left, right):
    return lax.dot_general(left, right, (((1,), (1,)), ((), ())), preferred_element_type=wide)


def t_mul(left, right):
    return lax.dot_general(left, right, (((0,), (0,)), ((), ())), preferred_element_type=wide)


def core_half(value, core):
    keep = lax.dynamic_index_in_dim(value, core, 1, keepdims=False)
    give = lax.dynamic_index_in_dim(value, 1 - core, 1, keepdims=False).astype(low)
    return (keep.astype(wide) + swap_core(give).astype(wide)).astype(low)


def on_device(
    latents, cond, cotangent, w_qkv, bias_qv, w_proj, b_proj, w_fc1, b_fc1, w_fc2, b_fc2, w_ada, b_ada
):
    stream_low = latents[0]
    upstream_low = cotangent[0]
    rows, features = stream_low.shape
    shards = 8
    length = shards * rows
    own = features // shards
    half = own // 2
    units = w_fc2.shape[0]
    heads = own // HEAD
    ada_width = w_ada.shape[1]
    ada_rows = ada_width // LANES
    place = lax.axis_index(SHARD)
    core = lax.axis_index("core")
    score_scale = HEAD ** (-0.5)

    upstream_all = lax.all_gather(upstream_low, SHARD, axis=0, tiled=True)
    wp = lax.all_gather(w_proj, SHARD, axis=0, tiled=True)

    cond_value = cond.astype(wide)
    cond_silu, silu_pull = jax.vjp(silu, cond_value)
    cond_low = cond_silu.astype(low)
    cond_own = lax.dynamic_slice_in_dim(cond_low, place * own, own, 1)
    mod_part = mul(cond_own, w_ada)[0]
    blocks = jnp.arange(shards)[:, None] == place
    mod_part = mod_part + jnp.where(blocks, b_ada.astype(wide)[None, :], 0.0).reshape(ada_width)
    mod_high = lax.reduce_precision(mod_part, 8, 7)
    mod_rest = mod_part - mod_high
    small = jnp.concatenate(
        [mod_high.astype(low), mod_rest.astype(low), bias_qv, b_proj, b_fc2]
    )
    first_sent = jnp.concatenate(
        [
            copies(stream_low),
            w_qkv.reshape(own, 3, shards, own).transpose(2, 0, 1, 3).reshape(shards, own, 3 * own),
            copies(as_rows(small, rows)),
        ],
        axis=2,
    )
    first_got = exchange(first_sent)
    tokens = first_got[:, :, :features].reshape(length, features)
    wq = first_got[:, :, features : features + 3 * own].reshape(features, 3 * own)
    small_got = first_got[:, :, features + 3 * own :].astype(wide)
    mod_sums = jnp.sum(small_got[:, : 2 * ada_rows], axis=0)
    modulation = (mod_sums[:ada_rows] + mod_sums[ada_rows:]).reshape(1, ada_width)
    shift_first, scale_first, gate_first, shift_second, scale_second, gate_second = jnp.split(
        modulation, 6, axis=1
    )
    at = 2 * ada_rows
    bias_wide = small_got[:, at : at + 2].reshape(1, 2 * features)
    proj_bias = small_got[:, at + 2].reshape(1, features)
    second_bias = small_got[:, at + 3].reshape(1, features)

    w1 = exchange(w_fc1.reshape(own, shards, units).transpose(1, 0, 2)).reshape(features, units)

    norm_first, inverse_first = normalize(tokens.astype(wide))
    attend_in = (norm_first * (1.0 + scale_first) + shift_first).astype(low)
    packed = mul(attend_in, wq)
    query_bias = lax.dynamic_slice_in_dim(bias_wide, place * own, own, 1)
    value_bias = lax.dynamic_slice_in_dim(bias_wide, features + place * own, own, 1)
    queries = (packed[:, :own] + query_bias).astype(low)
    keyset = packed[:, own : 2 * own].astype(low)
    valueset = (packed[:, 2 * own :] + value_bias).astype(low)
    def split(value):
        return value.reshape(length, heads, HEAD)

    query_heads, key_heads, value_heads = split(queries), split(keyset), split(valueset)
    scores = (
        jnp.einsum("qhe,khe->hqk", query_heads, key_heads, preferred_element_type=wide)
        * score_scale
    )
    row_peak = jnp.max(scores, axis=-1, keepdims=True)
    powered = jnp.exp(scores - row_peak)
    row_total = jnp.sum(powered, axis=-1, keepdims=True)
    attention = powered / row_total
    log_total = row_peak + jnp.log(row_total)
    mixed = (
        jnp.einsum("hqk,khe->qhe", attention.astype(low), value_heads, preferred_element_type=wide)
        .reshape(length, own)
        .astype(low)
    )
    mixed_tok = exchange(mixed.reshape(shards, rows, own))
    mixed_tok = mixed_tok.transpose(1, 0, 2).reshape(rows, features)
    branch = mul(mixed_tok, wp) + proj_bias
    stream = stream_low.astype(wide)
    middle = stream + gate_first * branch
    norm_second, inverse_second = normalize(middle)
    feed_in = (norm_second * (1.0 + scale_second) + shift_second).astype(low)
    feed_all = exchange(copies(feed_in)).reshape(length, features)
    hidden = mul(feed_all, w1) + b_fc1.astype(wide)[None, :]
    active_value, gelu_pull = jax.vjp(gelu_tanh, hidden)
    active = active_value.astype(low)
    branch_second_part = mul(active, w_fc2)

    def scatter(value):
        sent = value.astype(low).reshape(shards, rows, features)
        return jnp.sum(exchange(sent).astype(wide), axis=0)

    grad_branch_second = (upstream_all.astype(wide) * gate_second).astype(low)
    grad_active = mul_t(grad_branch_second, w_fc2)
    grad_hidden = gelu_pull(grad_active)[0].astype(low)
    grad_feed = scatter(mul_t(grad_hidden, w1))

    branch_second = scatter(branch_second_part) + second_bias
    output = (middle + gate_second * branch_second).astype(low)

    upstream = upstream_low.astype(wide)
    grad_gate_second = jnp.sum(upstream * branch_second, axis=0)
    grad_scale_second = jnp.sum(grad_feed * norm_second, axis=0)
    grad_shift_second = jnp.sum(grad_feed, axis=0)
    grad_middle = upstream + normalize_back(
        norm_second, inverse_second, grad_feed * (1.0 + scale_second)
    )
    grad_gate_first = jnp.sum(grad_middle * branch, axis=0)
    grad_branch = (grad_middle * gate_first).astype(low)
    grad_mixed_tok = mul_t(grad_branch, wp).astype(low)
    grad_mixed = exchange(grad_mixed_tok.reshape(rows, shards, own).transpose(1, 0, 2))
    grad_mixed = split(grad_mixed.reshape(length, own))

    again_scores = (
        jnp.einsum("qhe,khe->hqk", query_heads, key_heads, preferred_element_type=wide)
        * score_scale
    )
    again = jnp.exp(again_scores - log_total)
    grad_probs = jnp.einsum("qhe,khe->hqk", grad_mixed, value_heads, preferred_element_type=wide)
    grad_value = jnp.einsum(
        "hqk,qhe->khe", again.astype(low), grad_mixed, preferred_element_type=wide
    )
    row_delta = jnp.sum(again * grad_probs, axis=-1, keepdims=True)
    grad_scores = (again * (grad_probs - row_delta)).astype(low)
    grad_query = (
        jnp.einsum("hqk,khe->qhe", grad_scores, key_heads, preferred_element_type=wide)
        * score_scale
    )
    grad_key = (
        jnp.einsum("hqk,qhe->khe", grad_scores, query_heads, preferred_element_type=wide)
        * score_scale
    )
    grad_packed = jnp.concatenate(
        [part.reshape(length, own).astype(low) for part in (grad_query, grad_key, grad_value)],
        axis=1,
    )
    attend_part = mul_t(grad_packed, wq)
    grad_scale_first = jnp.sum(attend_part * norm_first, axis=0)
    grad_shift_first = jnp.sum(attend_part, axis=0)
    packed_sums = jnp.sum(grad_packed.astype(wide), axis=0)
    mod_terms = jnp.concatenate(
        [
            grad_shift_first,
            grad_scale_first,
            grad_gate_first,
            grad_shift_second,
            grad_scale_second,
            grad_gate_second,
            jnp.sum(grad_branch.astype(wide), axis=0),
            packed_sums[:own],
            packed_sums[2 * own :],
        ]
    ).astype(low)
    term_qkv = core_half(
        t_mul(attend_in, grad_packed).reshape(shards, 2, half, 3 * own), core
    )
    last_sent = jnp.concatenate(
        [
            attend_part.astype(low).reshape(shards, rows, features),
            jnp.concatenate([term_qkv[:, :, :own], term_qkv[:, :, own : 2 * own]], axis=1),
            jnp.concatenate(
                [term_qkv[:, :, 2 * own :], copies(as_rows(mod_terms, half))], axis=1
            ),
        ],
        axis=2,
    )
    last_got = exchange(last_sent)
    grad_attend = jnp.sum(last_got[:, :, :features].astype(wide), axis=0)
    near = last_got[:, :, features : features + own]
    far = last_got[:, :, features + own :]
    term_qkv = jnp.concatenate([near[:, :half], near[:, half:], far[:, :half]], axis=2)
    mod_got = far[:, half:].astype(wide)
    head_rows = ada_rows + features // LANES
    mod_sums = jnp.sum(mod_got[:, :head_rows], axis=0)
    bias_qv_all = jnp.concatenate(
        [mod_got[:, head_rows].reshape(features), mod_got[:, head_rows + 1].reshape(features)]
    )
    norm_own, inverse_own = normalize(stream)
    grad_stream = grad_middle + normalize_back(
        norm_own, inverse_own, grad_attend * (1.0 + scale_first)
    )
    grad_latents = grad_stream.astype(low)

    grad_modulation = mod_sums[:ada_rows].reshape(ada_width)
    proj_bias_term = lax.dynamic_slice_in_dim(mod_sums, ada_rows + place, 1, 0)
    cond_term = jnp.sum(w_ada.astype(wide) * grad_modulation[None, :], axis=1)
    cond_total = exchange(copies(cond_term)).reshape(1, features)
    grad_cond = silu_pull(cond_total)[0]

    second_bias_sums = jnp.sum(grad_branch_second.astype(wide), axis=0)
    rep_terms = jnp.concatenate(
        [
            mod_sums[:ada_rows],
            cond_own.astype(wide),
            proj_bias_term,
            jnp.sum(grad_hidden.astype(wide), axis=0).reshape(units // LANES, LANES),
            lax.dynamic_slice_in_dim(second_bias_sums, place * own, own, 0)[None],
            lax.dynamic_slice_in_dim(bias_qv_all, place * 2 * own, 2 * own, 0).reshape(2, own),
        ]
    )
    rep_terms = jnp.pad(rep_terms, ((0, half - rep_terms.shape[0]), (0, 0))).astype(low)
    rep_terms = jnp.concatenate([rep_terms, swap_core(rep_terms)], axis=1)

    term_pair = jnp.concatenate(
        [t_mul(feed_all, grad_hidden).astype(low), t_mul(mixed_tok, grad_branch).astype(low)],
        axis=1,
    )
    term_pair = core_half(term_pair.reshape(shards, 2, half, units + features), core)
    pair_got = exchange(term_pair)
    term_first = pair_got[:, :, :units]
    term_proj = jnp.sum(pair_got[:, :, units:].astype(wide), axis=0).astype(low)
    term_second = core_half(
        t_mul(active, grad_branch_second).reshape(1, 2, units // 2, features), core
    )[0]
    piece = units // 2 // shards
    term_second = term_second.reshape(shards, piece, features)
    fold = features // 2

    rep_sent = jnp.concatenate(
        [
            term_first,
            jnp.concatenate([term_second[:, :, :fold], term_second[:, :, fold:]], axis=1),
            term_qkv,
            term_proj.reshape(half, shards, own).transpose(1, 0, 2),
            copies(rep_terms),
        ],
        axis=2,
    )
    rep_got = exchange(rep_sent, CHIPS)
    width = units + fold + 4 * own
    owned = jnp.sum(rep_got[:, :, :width].astype(wide), axis=0).astype(low)
    rep_small = jnp.concatenate(
        [rep_got[:, :, width : width + own], rep_got[:, :, width + own :]], axis=0
    )
    grad_w_ada = t_mul(
        rep_small[:, ada_rows], rep_small[:, :ada_rows].reshape(2 * shards, ada_width)
    )
    rep_sums = jnp.sum(rep_small.astype(wide), axis=0)
    ada_own = ada_rows // shards
    grad_b_ada = lax.dynamic_slice_in_dim(rep_sums, place * ada_own, ada_own, 0)
    grad_b_ada = grad_b_ada.reshape(ada_width // shards)
    at = ada_rows + 1
    grad_b_proj = rep_sums[at]
    at += 1
    grad_b_fc1 = rep_sums[at : at + units // LANES].reshape(units)
    at += units // LANES
    grad_b_fc2 = rep_sums[at]
    grad_bias_qv = rep_sums[at + 1 : at + 3].reshape(2 * own)

    whole_mine = exchange(copies(owned), CHIPS)
    whole_other = swap_core(whole_mine)
    whole = [
        jnp.where(core == 0, whole_mine, whole_other).astype(wide),
        jnp.where(core == 0, whole_other, whole_mine).astype(wide),
    ]

    def side(value):
        return jnp.concatenate([value[k] for k in range(shards)], axis=1)

    grad_w_fc1 = jnp.concatenate([side(part[:, :, :units]) for part in whole], axis=0)
    at = units
    grad_w_fc2 = jnp.concatenate(
        [
            jnp.concatenate(
                [part[:, :piece, at : at + fold], part[:, piece:, at : at + fold]], axis=2
            ).reshape(units // 2, features)
            for part in whole
        ],
        axis=0,
    )
    at += fold
    grad_w_qkv = jnp.concatenate(
        [
            jnp.concatenate(
                [side(part[:, :, at + k * own : at + (k + 1) * own]) for k in range(3)], axis=1
            )
            for part in whole
        ],
        axis=0,
    )
    at += 3 * own
    grad_w_proj = jnp.concatenate([side(part[:, :, at:]) for part in whole], axis=0)

    return (
        output[None],
        grad_latents[None],
        grad_cond,
        grad_w_qkv,
        grad_bias_qv,
        grad_w_proj,
        grad_b_proj,
        grad_w_fc1,
        grad_b_fc1,
        grad_w_fc2,
        grad_b_fc2,
        grad_w_ada,
        grad_b_ada,
    )


def solution(mesh):
    fine = Mesh(mesh.devices.reshape(2, 4, 2, 2, 4), REP + SHARD)
    tokens = P(REP, SHARD, None)
    matrix = P(SHARD, None)
    vector = P(SHARD)
    params = (matrix, vector) * 5
    return jax.shard_map(
        on_device,
        mesh=fine,
        in_specs=(tokens, P(REP, None), tokens) + params,
        out_specs=(tokens, tokens, P(REP, None)) + params,
        check_vma=False,
    )
```

```python
import jax
import jax.numpy as jnp
from jax import lax
from jax.experimental import pallas as pl
from jax.experimental.pallas import tpu as pltpu
from jax.sharding import Mesh, PartitionSpec as P

HEAD = 64
SHARD = ("xh", "y")
CHIPS = ("xl", "z")
REP = ("xl", "z", "core")
LANES = 128
QUERY_BLOCK = 256
SCALE = HEAD ** (-0.5)

epsilon = 1e-06
highest = lax.Precision.HIGHEST
low = jnp.bfloat16
wide = jnp.float32


def swap_core(value):
    return lax.ppermute(value, "core", [(0, 1), (1, 0)])


def exchange(value, axes=SHARD):
    return lax.all_to_all(value, axes, 0, 0, tiled=True)


def copies(value):
    return jnp.broadcast_to(value[None], (8,) + value.shape)


def as_rows(value, count):
    rows = value.reshape(-1, LANES)
    return jnp.pad(rows, ((0, count - rows.shape[0]), (0, 0)))


def normalize(values):
    centered = values - jnp.mean(values, axis=-1, keepdims=True)
    inverse = lax.rsqrt(jnp.mean(centered * centered, axis=-1, keepdims=True) + epsilon)
    return centered * inverse, inverse


def normalize_back(norm, inverse, grad):
    return inverse * (
        grad
        - jnp.mean(grad, axis=-1, keepdims=True)
        - norm * jnp.mean(grad * norm, axis=-1, keepdims=True)
    )


def silu(values):
    return values / (1.0 + jnp.exp(-values))


def gelu_tanh(values):
    return (
        0.5
        * values
        * (1.0 + jnp.tanh(0.7978845608028654 * (values + 0.044715 * values * values * values)))
    )


def mul(left, right):
    return lax.dot_general(left, right, (((1,), (0,)), ((), ())), preferred_element_type=wide)


def mul_t(left, right):
    return lax.dot_general(left, right, (((1,), (1,)), ((), ())), preferred_element_type=wide)


def t_mul(left, right):
    return lax.dot_general(left, right, (((0,), (0,)), ((), ())), preferred_element_type=wide)


def head_of(value, index):
    lane = lax.broadcasted_iota(jnp.int32, value.shape, 1)
    return jnp.where((lane >= HEAD) == (index == 1), value, jnp.zeros_like(value))


def attend_kernel(q_ref, k_ref, v_ref, mixed_ref, log_ref):
    total = None
    logs = None
    for index in range(2):
        scores = mul_t(head_of(q_ref[...], index), k_ref[...]) * SCALE
        peak = jnp.max(scores, axis=1, keepdims=True)
        powered = jnp.exp(scores - peak)
        row_total = jnp.sum(powered, axis=1, keepdims=True)
        probs = (powered / row_total).astype(low)
        part = mul(probs, head_of(v_ref[...], index))
        log = head_of(jnp.broadcast_to(peak + jnp.log(row_total), part.shape), index)
        total = part if total is None else total + part
        logs = log if logs is None else logs + log
    mixed_ref[...] = total.astype(low)
    log_ref[...] = logs


def attend(queries, keyset, valueset):
    length, own = queries.shape
    block = pl.BlockSpec((QUERY_BLOCK, own), lambda i: (i, 0))
    fixed = pl.BlockSpec((length, own), lambda i: (0, 0))
    return pl.pallas_call(
        attend_kernel,
        grid=(length // QUERY_BLOCK,),
        in_specs=[block, fixed, fixed],
        out_specs=[block, block],
        out_shape=[
            jax.ShapeDtypeStruct((length, own), low),
            jax.ShapeDtypeStruct((length, own), wide),
        ],
        compiler_params=pltpu.CompilerParams(vmem_limit_bytes=32 * 1024 * 1024),
        cost_estimate=pl.CostEstimate(
            flops=8 * length * length * own,
            transcendentals=2 * length * length,
            bytes_accessed=12 * length * own,
        ),
        name="attend",
    )(queries, keyset, valueset)


def attend_back_kernel(q_ref, g_ref, log_ref, k_ref, v_ref, out_ref, key_acc, value_acc):
    step = pl.program_id(0)
    own = q_ref.shape[1]

    @pl.when(step == 0)
    def _():
        key_acc[...] = jnp.zeros_like(key_acc)
        value_acc[...] = jnp.zeros_like(value_acc)

    grad_query = None
    for index in range(2):
        query = head_of(q_ref[...], index)
        grad = head_of(g_ref[...], index)
        log = log_ref[:, index * HEAD : index * HEAD + 1]
        probs = jnp.exp(mul_t(query, k_ref[...]) * SCALE - log)
        grad_probs = mul_t(grad, v_ref[...])
        delta = jnp.sum(probs * grad_probs, axis=1, keepdims=True)
        grad_scores = (probs * (grad_probs - delta)).astype(low)
        part = mul(grad_scores, head_of(k_ref[...], index))
        grad_query = part if grad_query is None else grad_query + part
        key_acc[...] += t_mul(grad_scores, query)
        value_acc[...] += t_mul(probs.astype(low), grad)
    at = pl.multiple_of(step * QUERY_BLOCK, QUERY_BLOCK)
    out_ref[pl.ds(at, QUERY_BLOCK), 0:own] = (grad_query * SCALE).astype(low)

    @pl.when(step == pl.num_programs(0) - 1)
    def _():
        out_ref[:, own : 2 * own] = (key_acc[...] * SCALE).astype(low)
        out_ref[:, 2 * own : 3 * own] = value_acc[...].astype(low)


def attend_back(queries, grad_mixed, logs, keyset, valueset):
    length, own = queries.shape
    block = pl.BlockSpec((QUERY_BLOCK, own), lambda i: (i, 0))
    fixed = pl.BlockSpec((length, own), lambda i: (0, 0))
    return pl.pallas_call(
        attend_back_kernel,
        grid=(length // QUERY_BLOCK,),
        in_specs=[block, block, block, fixed, fixed],
        out_specs=pl.BlockSpec((length, 3 * own), lambda i: (0, 0)),
        out_shape=jax.ShapeDtypeStruct((length, 3 * own), low),
        scratch_shapes=[pltpu.VMEM((length, own), wide), pltpu.VMEM((length, own), wide)],
        compiler_params=pltpu.CompilerParams(vmem_limit_bytes=32 * 1024 * 1024),
        cost_estimate=pl.CostEstimate(
            flops=20 * length * length * own,
            transcendentals=2 * length * length,
            bytes_accessed=20 * length * own,
        ),
        name="attend_back",
    )(queries, grad_mixed, logs, keyset, valueset)


def gather_small(value, place):
    for bit in (1, 2, 4):
        other = lax.ppermute(value, SHARD, [(k, k ^ bit) for k in range(8)])
        upper = (place // bit) % 2 == 1
        value = jnp.concatenate(
            [jnp.where(upper, other, value), jnp.where(upper, value, other)], axis=0
        )
    return value


def join_rows(mine, other, core):
    first = jnp.where(core == 0, mine, other)
    second = jnp.where(core == 0, other, mine)
    return jnp.concatenate([first, second], axis=1).reshape(-1, mine.shape[-1])


def core_half(value, core):
    keep = lax.dynamic_index_in_dim(value, core, 1, keepdims=False)
    give = lax.dynamic_index_in_dim(value, 1 - core, 1, keepdims=False).astype(low)
    return (keep.astype(wide) + swap_core(give).astype(wide)).astype(low)


def on_device(
    latents, cond, cotangent, w_qkv, bias_qv, w_proj, b_proj, w_fc1, b_fc1, w_fc2, b_fc2, w_ada, b_ada
):
    stream_low = latents[0]
    upstream_low = cotangent[0]
    rows, features = stream_low.shape
    shards = 8
    length = shards * rows
    own = features // shards
    half = own // 2
    units = w_fc2.shape[0]
    ada_width = w_ada.shape[1]
    ada_rows = ada_width // LANES
    place = lax.axis_index(SHARD)
    core = lax.axis_index("core")

    upstream_all = lax.all_gather(upstream_low, SHARD, axis=0, tiled=True)
    proj_mine = lax.dynamic_slice_in_dim(w_proj, core * half, half, 0)
    proj_mine = lax.all_gather(proj_mine, SHARD, axis=0, tiled=True).reshape(shards, half, features)
    wp = join_rows(proj_mine, swap_core(proj_mine), core)

    cond_value = cond.astype(wide)
    cond_silu, silu_pull = jax.vjp(silu, cond_value)
    cond_low = cond_silu.astype(low)
    cond_own = lax.dynamic_slice_in_dim(cond_low, place * own, own, 1)
    mod_part = mul(cond_own, w_ada)[0]
    blocks = jnp.arange(shards)[:, None] == place
    mod_part = mod_part + jnp.where(blocks, b_ada.astype(wide)[None, :], 0.0).reshape(ada_width)
    mod_high = lax.reduce_precision(mod_part, 8, 7)
    mod_rest = mod_part - mod_high
    small = jnp.concatenate(
        [mod_high.astype(low), mod_rest.astype(low), bias_qv, b_proj, b_fc2]
    )

    def halved(value):
        return lax.dynamic_slice_in_dim(value, core * half, half, 0)

    fc1_mine = halved(w_fc1).reshape(half, shards, units).transpose(1, 0, 2)
    qkv_mine = halved(w_qkv)
    qkv_mine = jnp.stack(
        [
            jnp.concatenate(
                [
                    qkv_mine[:, part * features + k * own : part * features + (k + 1) * own]
                    for part in range(3)
                ]
                + [jnp.zeros((half, own), low)],
                axis=1,
            )
            for k in range(shards)
        ]
    )
    first_sent = jnp.concatenate(
        [
            copies(stream_low),
            jnp.concatenate([fc1_mine, qkv_mine], axis=1),
            copies(as_rows(small, rows)),
        ],
        axis=2,
    )
    first_got = exchange(first_sent)
    tokens = first_got[:, :, :features].reshape(length, features)
    pair_mine = first_got[:, :, features : features + units]
    pair_other = swap_core(pair_mine)
    w1 = join_rows(pair_mine[:, :half], pair_other[:, :half], core)
    wq = join_rows(pair_mine[:, half:, : 3 * own], pair_other[:, half:, : 3 * own], core)
    small_got = first_got[:, :, features + units :].astype(wide)
    mod_sums = jnp.sum(small_got[:, : 2 * ada_rows], axis=0)
    modulation = (mod_sums[:ada_rows] + mod_sums[ada_rows:]).reshape(1, ada_width)
    shift_first, scale_first, gate_first, shift_second, scale_second, gate_second = jnp.split(
        modulation, 6, axis=1
    )
    at = 2 * ada_rows
    bias_wide = small_got[:, at : at + 2].reshape(1, 2 * features)
    proj_bias = small_got[:, at + 2].reshape(1, features)
    second_bias = small_got[:, at + 3].reshape(1, features)

    norm_first, inverse_first = normalize(tokens.astype(wide))
    attend_in = (norm_first * (1.0 + scale_first) + shift_first).astype(low)
    packed = mul(attend_in, wq)
    query_bias = lax.dynamic_slice_in_dim(bias_wide, place * own, own, 1)
    value_bias = lax.dynamic_slice_in_dim(bias_wide, features + place * own, own, 1)
    queries = (packed[:, :own] + query_bias).astype(low)
    keyset = packed[:, own : 2 * own].astype(low)
    valueset = (packed[:, 2 * own :] + value_bias).astype(low)
    mixed, log_total = attend(queries, keyset, valueset)
    mixed_tok = exchange(mixed.reshape(shards, rows, own))
    mixed_tok = mixed_tok.transpose(1, 0, 2).reshape(rows, features)
    branch = mul(mixed_tok, wp) + proj_bias
    stream = stream_low.astype(wide)
    middle = stream + gate_first * branch
    norm_second, inverse_second = normalize(middle)
    feed_in = (norm_second * (1.0 + scale_second) + shift_second).astype(low)
    feed_all = exchange(copies(feed_in)).reshape(length, features)
    hidden = mul(feed_all, w1) + b_fc1.astype(wide)[None, :]
    active_value, gelu_pull = jax.vjp(gelu_tanh, hidden)
    active = active_value.astype(low)
    branch_second_part = mul(active, w_fc2)

    def scatter(value):
        sent = value.astype(low).reshape(shards, rows, features)
        return jnp.sum(exchange(sent).astype(wide), axis=0)

    grad_branch_second = (upstream_all.astype(wide) * gate_second).astype(low)
    grad_active = mul_t(grad_branch_second, w_fc2)
    grad_hidden = gelu_pull(grad_active)[0].astype(low)
    grad_feed = scatter(mul_t(grad_hidden, w1))

    branch_second = (
        lax.psum_scatter(
            branch_second_part.astype(low), SHARD, scatter_dimension=0, tiled=True
        ).astype(wide)
        + second_bias
    )
    output = (middle + gate_second * branch_second).astype(low)

    upstream = upstream_low.astype(wide)
    grad_gate_second = jnp.sum(
        upstream_all.astype(wide) * branch_second_part, axis=0
    ) + second_bias[0] * jnp.sum(upstream, axis=0)
    grad_scale_second = jnp.sum(grad_feed * norm_second, axis=0)
    grad_shift_second = jnp.sum(grad_feed, axis=0)
    grad_middle = upstream + normalize_back(
        norm_second, inverse_second, grad_feed * (1.0 + scale_second)
    )
    grad_gate_first = jnp.sum(grad_middle * branch, axis=0)
    grad_branch = (grad_middle * gate_first).astype(low)
    grad_mixed_tok = mul_t(grad_branch, wp).astype(low)
    grad_mixed = exchange(grad_mixed_tok.reshape(rows, shards, own).transpose(1, 0, 2))
    grad_packed = attend_back(
        queries, grad_mixed.reshape(length, own), log_total, keyset, valueset
    )
    attend_part = mul_t(grad_packed, wq)
    grad_scale_first = jnp.sum(attend_part * norm_first, axis=0)
    grad_shift_first = jnp.sum(attend_part, axis=0)
    packed_sums = jnp.sum(grad_packed.astype(wide), axis=0)
    mod_terms = jnp.concatenate(
        [
            grad_shift_first,
            grad_scale_first,
            grad_gate_first,
            grad_shift_second,
            grad_scale_second,
            grad_gate_second,
            jnp.sum(grad_branch.astype(wide), axis=0),
            packed_sums[:own],
            packed_sums[2 * own :],
        ]
    ).astype(low)
    term_qkv = core_half(
        t_mul(attend_in, grad_packed).reshape(shards, 2, half, 3 * own), core
    )
    last_sent = jnp.concatenate(
        [
            attend_part.astype(low).reshape(shards, rows, features),
            jnp.concatenate([term_qkv[:, :, :own], term_qkv[:, :, own : 2 * own]], axis=1),
            jnp.concatenate(
                [term_qkv[:, :, 2 * own :], copies(as_rows(mod_terms, half))], axis=1
            ),
        ],
        axis=2,
    )
    last_got = exchange(last_sent)
    grad_attend = jnp.sum(last_got[:, :, :features].astype(wide), axis=0)
    near = last_got[:, :, features : features + own]
    far = last_got[:, :, features + own :]
    term_qkv = jnp.concatenate([near[:, :half], near[:, half:], far[:, :half]], axis=2)
    mod_got = far[:, half:].astype(wide)
    head_rows = ada_rows + features // LANES
    mod_sums = jnp.sum(mod_got[:, :head_rows], axis=0)
    bias_qv_all = jnp.concatenate(
        [mod_got[:, head_rows].reshape(features), mod_got[:, head_rows + 1].reshape(features)]
    )
    norm_own, inverse_own = normalize(stream)
    grad_stream = grad_middle + normalize_back(
        norm_own, inverse_own, grad_attend * (1.0 + scale_first)
    )
    grad_latents = grad_stream.astype(low)

    grad_modulation = mod_sums[:ada_rows].reshape(ada_width)
    proj_bias_term = lax.dynamic_slice_in_dim(mod_sums, ada_rows + place, 1, 0)
    cond_term = jnp.sum(w_ada.astype(wide) * grad_modulation[None, :], axis=1)
    cond_total = gather_small(cond_term[None], place).reshape(1, features)
    grad_cond = silu_pull(cond_total)[0]

    second_bias_sums = jnp.sum(grad_branch_second.astype(wide), axis=0)
    rep_terms = jnp.concatenate(
        [
            mod_sums[:ada_rows],
            cond_own.astype(wide),
            proj_bias_term,
            jnp.sum(grad_hidden.astype(wide), axis=0).reshape(units // LANES, LANES),
            lax.dynamic_slice_in_dim(second_bias_sums, place * own, own, 0)[None],
            lax.dynamic_slice_in_dim(bias_qv_all, place * 2 * own, 2 * own, 0).reshape(2, own),
        ]
    )
    rep_terms = jnp.pad(rep_terms, ((0, half - rep_terms.shape[0]), (0, 0))).astype(low)
    rep_terms = jnp.concatenate([rep_terms, swap_core(rep_terms)], axis=1)

    term_pair = jnp.concatenate(
        [t_mul(feed_all, grad_hidden).astype(low), t_mul(mixed_tok, grad_branch).astype(low)],
        axis=1,
    )
    term_pair = core_half(term_pair.reshape(shards, 2, half, units + features), core)
    pair_got = exchange(term_pair)
    term_first = pair_got[:, :, :units]
    term_proj = jnp.sum(pair_got[:, :, units:].astype(wide), axis=0).astype(low)
    term_second = core_half(
        t_mul(active, grad_branch_second).reshape(1, 2, units // 2, features), core
    )[0]
    piece = units // 2 // shards
    term_second = term_second.reshape(shards, piece, features)
    fold = features // 2

    rep_sent = jnp.concatenate(
        [
            term_first,
            jnp.concatenate([term_second[:, :, :fold], term_second[:, :, fold:]], axis=1),
            term_qkv,
            term_proj.reshape(half, shards, own).transpose(1, 0, 2),
            copies(rep_terms),
        ],
        axis=2,
    )
    rep_got = exchange(rep_sent, CHIPS)
    width = units + fold + 4 * own
    owned = jnp.sum(rep_got[:, :, :width].astype(wide), axis=0).astype(low)
    rep_small = jnp.concatenate(
        [rep_got[:, :, width : width + own], rep_got[:, :, width + own :]], axis=0
    )
    grad_w_ada = t_mul(
        rep_small[:, ada_rows], rep_small[:, :ada_rows].reshape(2 * shards, ada_width)
    )
    rep_sums = jnp.sum(rep_small.astype(wide), axis=0)
    ada_own = ada_rows // shards
    grad_b_ada = lax.dynamic_slice_in_dim(rep_sums, place * ada_own, ada_own, 0)
    grad_b_ada = grad_b_ada.reshape(ada_width // shards)
    at = ada_rows + 1
    grad_b_proj = rep_sums[at]
    at += 1
    grad_b_fc1 = rep_sums[at : at + units // LANES].reshape(units)
    at += units // LANES
    grad_b_fc2 = rep_sums[at]
    grad_bias_qv = rep_sums[at + 1 : at + 3].reshape(2 * own)

    whole_mine = exchange(copies(owned), CHIPS)
    whole_other = swap_core(whole_mine)
    whole = [
        jnp.where(core == 0, whole_mine, whole_other).astype(wide),
        jnp.where(core == 0, whole_other, whole_mine).astype(wide),
    ]

    def side(value):
        return jnp.concatenate([value[k] for k in range(shards)], axis=1)

    grad_w_fc1 = jnp.concatenate([side(part[:, :, :units]) for part in whole], axis=0)
    at = units
    grad_w_fc2 = jnp.concatenate(
        [
            jnp.concatenate(
                [part[:, :piece, at : at + fold], part[:, piece:, at : at + fold]], axis=2
            ).reshape(units // 2, features)
            for part in whole
        ],
        axis=0,
    )
    at += fold
    grad_w_qkv = jnp.concatenate(
        [
            jnp.concatenate(
                [side(part[:, :, at + k * own : at + (k + 1) * own]) for k in range(3)], axis=1
            )
            for part in whole
        ],
        axis=0,
    )
    at += 3 * own
    grad_w_proj = jnp.concatenate([side(part[:, :, at:]) for part in whole], axis=0)

    return (
        output[None],
        grad_latents[None],
        grad_cond,
        grad_w_qkv,
        grad_bias_qv,
        grad_w_proj,
        grad_b_proj,
        grad_w_fc1,
        grad_b_fc1,
        grad_w_fc2,
        grad_b_fc2,
        grad_w_ada,
        grad_b_ada,
    )


def solution(mesh):
    fine = Mesh(mesh.devices.reshape(2, 4, 2, 2, 4), REP + SHARD)
    tokens = P(REP, SHARD, None)
    matrix = P(SHARD, None)
    vector = P(SHARD)
    params = (matrix, vector) * 5
    return jax.shard_map(
        on_device,
        mesh=fine,
        in_specs=(tokens, P(REP, None), tokens) + params,
        out_specs=(tokens, tokens, P(REP, None)) + params,
        check_vma=False,
    )
```

```python
import jax
import jax.numpy as jnp
from jax import lax
from jax.experimental import pallas as pl
from jax.experimental.pallas import tpu as pltpu
from jax.sharding import Mesh, PartitionSpec as P

HEAD = 64
SHARD = ("xh", "y")
CHIPS = ("xl", "z")
REP = ("xl", "z", "core")
LANES = 128
QUERY_BLOCK = 256
SCALE = HEAD ** (-0.5)

epsilon = 1e-06
highest = lax.Precision.HIGHEST
low = jnp.bfloat16
wide = jnp.float32


def swap_core(value):
    return lax.ppermute(value, "core", [(0, 1), (1, 0)])


def exchange(value, axes=SHARD):
    return lax.all_to_all(value, axes, 0, 0, tiled=True)


def copies(value):
    return jnp.broadcast_to(value[None], (8,) + value.shape)


def as_rows(value, count):
    rows = value.reshape(-1, LANES)
    return jnp.pad(rows, ((0, count - rows.shape[0]), (0, 0)))


def normalize(values):
    centered = values - jnp.mean(values, axis=-1, keepdims=True)
    inverse = lax.rsqrt(jnp.mean(centered * centered, axis=-1, keepdims=True) + epsilon)
    return centered * inverse, inverse


def normalize_back(norm, inverse, grad):
    return inverse * (
        grad
        - jnp.mean(grad, axis=-1, keepdims=True)
        - norm * jnp.mean(grad * norm, axis=-1, keepdims=True)
    )


def silu(values):
    return values / (1.0 + jnp.exp(-values))


def gelu_tanh(values):
    return (
        0.5
        * values
        * (1.0 + jnp.tanh(0.7978845608028654 * (values + 0.044715 * values * values * values)))
    )


def mul(left, right):
    return lax.dot_general(left, right, (((1,), (0,)), ((), ())), preferred_element_type=wide)


def mul_t(left, right):
    return lax.dot_general(left, right, (((1,), (1,)), ((), ())), preferred_element_type=wide)


def t_mul(left, right):
    return lax.dot_general(left, right, (((0,), (0,)), ((), ())), preferred_element_type=wide)


def head_of(value, index):
    lane = lax.broadcasted_iota(jnp.int32, value.shape, 1)
    return jnp.where((lane >= HEAD) == (index == 1), value, jnp.zeros_like(value))


def attend_kernel(
    got_ref, wq_ref, scale_ref, shift_ref, qb_ref, vb_ref, in_ref, q_ref, k_ref, v_ref, mixed_ref, log_ref
):
    count, rows, _ = got_ref.shape
    features = scale_ref.shape[1]
    own = qb_ref.shape[1]
    gain = 1.0 + scale_ref[...]
    for block in range(count):
        at = pl.ds(block * rows, rows)
        norm, _ = normalize(got_ref[block, :, 0:features].astype(wide))
        attend_in = (norm * gain + shift_ref[...]).astype(low)
        in_ref[at, :] = attend_in
        packed = mul(attend_in, wq_ref[...])
        q_ref[at, :] = (packed[:, :own] + qb_ref[...]).astype(low)
        k_ref[at, :] = packed[:, own : 2 * own].astype(low)
        v_ref[at, :] = (packed[:, 2 * own :] + vb_ref[...]).astype(low)
    for block in range(count * rows // QUERY_BLOCK):
        at = pl.ds(block * QUERY_BLOCK, QUERY_BLOCK)
        total = None
        logs = None
        for index in range(2):
            scores = mul_t(head_of(q_ref[at, :], index), k_ref[...]) * SCALE
            peak = jnp.max(scores, axis=1, keepdims=True)
            powered = jnp.exp(scores - peak)
            row_total = jnp.sum(powered, axis=1, keepdims=True)
            probs = (powered / row_total).astype(low)
            part = mul(probs, head_of(v_ref[...], index))
            log = head_of(jnp.broadcast_to(peak + jnp.log(row_total), part.shape), index)
            total = part if total is None else total + part
            logs = log if logs is None else logs + log
        mixed_ref[at, :] = total.astype(low)
        log_ref[at, :] = logs


def attend(got, wq, scale, shift, query_bias, value_bias):
    length, features = wq.shape
    length = got.shape[0] * got.shape[1]
    features = wq.shape[0]
    own = wq.shape[1] // 3
    head = jax.ShapeDtypeStruct((length, own), low)
    return pl.pallas_call(
        attend_kernel,
        out_shape=[
            jax.ShapeDtypeStruct((length, features), low),
            head,
            head,
            head,
            head,
            jax.ShapeDtypeStruct((length, own), wide),
        ],
        compiler_params=pltpu.CompilerParams(vmem_limit_bytes=40 * 1024 * 1024),
        cost_estimate=pl.CostEstimate(
            flops=16 * length * length * own,
            transcendentals=2 * length * length,
            bytes_accessed=8 * length * features,
        ),
        name="attend",
    )(got, wq, scale, shift, query_bias, value_bias)


def attend_back_kernel(
    q_ref, g_ref, log_ref, k_ref, v_ref, wq_ref, in_ref, got_ref,
    part_ref, term_ref, sums_ref, packed_sums_ref, packed, key_acc, value_acc,
):
    length, own = q_ref.shape
    count, rows, _ = got_ref.shape
    features = in_ref.shape[1]
    for block in range(length // QUERY_BLOCK):
        at = pl.ds(block * QUERY_BLOCK, QUERY_BLOCK)
        grad_query = None
        for index in range(2):
            query = head_of(q_ref[at, :], index)
            grad = head_of(g_ref[at, :], index)
            log = log_ref[at, index * HEAD : index * HEAD + 1]
            probs = jnp.exp(mul_t(query, k_ref[...]) * SCALE - log)
            grad_probs = mul_t(grad, v_ref[...])
            delta = jnp.sum(probs * grad_probs, axis=1, keepdims=True)
            grad_scores = (probs * (grad_probs - delta)).astype(low)
            part = mul(grad_scores, head_of(k_ref[...], index))
            grad_query = part if grad_query is None else grad_query + part
            key_part = t_mul(grad_scores, query)
            value_part = t_mul(probs.astype(low), grad)
            if block == 0 and index == 0:
                key_acc[...] = key_part
                value_acc[...] = value_part
            else:
                key_acc[...] += key_part
                value_acc[...] += value_part
        packed[at, 0:own] = (grad_query * SCALE).astype(low)
    packed[:, own : 2 * own] = (key_acc[...] * SCALE).astype(low)
    packed[:, 2 * own : 3 * own] = value_acc[...].astype(low)
    packed_sums_ref[...] = jnp.sum(packed[...].astype(wide), axis=0, keepdims=True)
    shift_sum = None
    scale_sum = None
    for block in range(count):
        at = pl.ds(block * rows, rows)
        part = mul_t(packed[at, :], wq_ref[...])
        norm, _ = normalize(got_ref[block, :, 0:features].astype(wide))
        part_ref[block] = part.astype(low)
        one = jnp.sum(part, axis=0, keepdims=True)
        two = jnp.sum(part * norm, axis=0, keepdims=True)
        shift_sum = one if shift_sum is None else shift_sum + one
        scale_sum = two if scale_sum is None else scale_sum + two
    sums_ref[0:1, :] = shift_sum
    sums_ref[1:2, :] = scale_sum
    for block in range(features // QUERY_BLOCK):
        at = pl.ds(block * QUERY_BLOCK, QUERY_BLOCK)
        term_ref[at, :] = t_mul(in_ref[:, at], packed[...]).astype(low)


def attend_back(queries, grad_mixed, logs, keyset, valueset, wq, attend_in, got):
    length, own = queries.shape
    features = attend_in.shape[1]
    count, rows, _ = got.shape
    return pl.pallas_call(
        attend_back_kernel,
        out_shape=[
            jax.ShapeDtypeStruct((count, rows, features), low),
            jax.ShapeDtypeStruct((features, 3 * own), low),
            jax.ShapeDtypeStruct((2, features), wide),
            jax.ShapeDtypeStruct((1, 3 * own), wide),
        ],
        scratch_shapes=[
            pltpu.VMEM((length, 3 * own), low),
            pltpu.VMEM((length, own), wide),
            pltpu.VMEM((length, own), wide),
        ],
        compiler_params=pltpu.CompilerParams(vmem_limit_bytes=40 * 1024 * 1024),
        cost_estimate=pl.CostEstimate(
            flops=32 * length * length * own,
            transcendentals=2 * length * length,
            bytes_accessed=12 * length * features,
        ),
        name="attend_back",
    )(queries, grad_mixed, logs, keyset, valueset, wq, attend_in, got)


def shift_to(value, dx, dy):
    pairs = [(x * 4 + y, ((x + dx) % 2) * 4 + (y + dy) % 4) for x in range(2) for y in range(4)]
    return lax.ppermute(value, SHARD, pairs)


def scatter_sum(value, place):
    total = lax.dynamic_index_in_dim(value, place, 0, keepdims=False).astype(wide)
    for dx, dy in ((0, 1), (0, 3), (1, 0), (0, 2), (1, 1), (1, 3), (1, 2)):
        target = ((place // 4 + dx) % 2) * 4 + (place + dy) % 4
        block = lax.dynamic_index_in_dim(value, target, 0, keepdims=False)
        total = total + shift_to(block, dx, dy).astype(wide)
    return total


def gather_small(value, place):
    for bit in (1, 2, 4):
        other = lax.ppermute(value, SHARD, [(k, k ^ bit) for k in range(8)])
        upper = (place // bit) % 2 == 1
        value = jnp.concatenate(
            [jnp.where(upper, other, value), jnp.where(upper, value, other)], axis=0
        )
    return value


def join_rows(mine, other, core):
    first = jnp.where(core == 0, mine, other)
    second = jnp.where(core == 0, other, mine)
    return jnp.concatenate([first, second], axis=1).reshape(-1, mine.shape[-1])


def core_half(value, core):
    keep = lax.dynamic_index_in_dim(value, core, 1, keepdims=False)
    give = lax.dynamic_index_in_dim(value, 1 - core, 1, keepdims=False).astype(low)
    return (keep.astype(wide) + swap_core(give).astype(wide)).astype(low)


def on_device(
    latents, cond, cotangent, w_qkv, bias_qv, w_proj, b_proj, w_fc1, b_fc1, w_fc2, b_fc2, w_ada, b_ada
):
    stream_low = latents[0]
    upstream_low = cotangent[0]
    rows, features = stream_low.shape
    shards = 8
    length = shards * rows
    own = features // shards
    half = own // 2
    units = w_fc2.shape[0]
    ada_width = w_ada.shape[1]
    ada_rows = ada_width // LANES
    place = lax.axis_index(SHARD)
    core = lax.axis_index("core")

    cond_value = cond.astype(wide)
    cond_silu, silu_pull = jax.vjp(silu, cond_value)
    cond_low = cond_silu.astype(low)
    cond_own = lax.dynamic_slice_in_dim(cond_low, place * own, own, 1)
    mod_part = mul(cond_own, w_ada)[0]
    blocks = jnp.arange(shards)[:, None] == place
    mod_part = mod_part + jnp.where(blocks, b_ada.astype(wide)[None, :], 0.0).reshape(ada_width)
    small = jnp.concatenate([mod_part.astype(low), bias_qv, b_proj, b_fc2])

    def halved(value):
        return lax.dynamic_slice_in_dim(value, core * half, half, 0)

    qkv_mine = halved(w_qkv)

    def qkv_part(part):
        return jnp.stack(
            [
                qkv_mine[:, part * features + k * own : part * features + (k + 1) * own]
                for k in range(shards)
            ]
        )

    first_sent = jnp.concatenate(
        [
            copies(stream_low),
            jnp.concatenate([qkv_part(0), qkv_part(1)], axis=1),
            jnp.concatenate([qkv_part(2), copies(as_rows(small, half))], axis=1),
        ],
        axis=2,
    )
    first_got = exchange(first_sent)
    weights_sent = jnp.concatenate(
        [
            halved(w_fc1).reshape(half, shards, units).transpose(1, 0, 2),
            copies(halved(w_proj)),
        ],
        axis=2,
    )
    weights_sent, first_got = lax.optimization_barrier((weights_sent, first_got))
    weights_got = exchange(weights_sent)
    near = first_got[:, :, features : features + own]
    far = first_got[:, :, features + own :]
    qkv_got = jnp.concatenate([near[:, :half], near[:, half:], far[:, :half]], axis=2)
    wq = join_rows(qkv_got, swap_core(qkv_got), core)
    small_got = far[:, half:].astype(wide)
    modulation = jnp.sum(small_got[:, :ada_rows], axis=0).reshape(1, ada_width)
    shift_first, scale_first, gate_first, shift_second, scale_second, gate_second = jnp.split(
        modulation, 6, axis=1
    )
    at = ada_rows
    bias_wide = small_got[:, at : at + 2].reshape(1, 2 * features)
    proj_bias = small_got[:, at + 2].reshape(1, features)
    second_bias = small_got[:, at + 3].reshape(1, features)

    query_bias = lax.dynamic_slice_in_dim(bias_wide, place * own, own, 1)
    value_bias = lax.dynamic_slice_in_dim(bias_wide, features + place * own, own, 1)
    attend_in, queries, keyset, valueset, mixed, log_total = attend(
        first_got, wq, scale_first, shift_first, query_bias, value_bias
    )
    mixed, weights_got = lax.optimization_barrier((mixed, weights_got))
    mixed_got = exchange(
        jnp.concatenate([mixed.reshape(shards, rows, own), copies(upstream_low)], axis=2)
    )
    weights_other = swap_core(weights_got)
    w1 = join_rows(weights_got[:, :, :units], weights_other[:, :, :units], core)
    wp = join_rows(weights_got[:, :, units:], weights_other[:, :, units:], core)
    mixed_tok = mixed_got[:, :, :own].transpose(1, 0, 2).reshape(rows, features)
    upstream_all = mixed_got[:, :, own:].reshape(length, features)
    branch = mul(mixed_tok, wp) + proj_bias
    stream = stream_low.astype(wide)
    middle = stream + gate_first * branch
    norm_second, inverse_second = normalize(middle)
    feed_in = (norm_second * (1.0 + scale_second) + shift_second).astype(low)
    feed_all = exchange(copies(feed_in)).reshape(length, features)
    hidden = mul(feed_all, w1) + b_fc1.astype(wide)[None, :]
    active_value, gelu_pull = jax.vjp(gelu_tanh, hidden)
    active = active_value.astype(low)
    branch_second_part = mul(active, w_fc2)

    def scatter(value):
        sent = value.astype(low).reshape(shards, rows, features)
        return jnp.sum(exchange(sent).astype(wide), axis=0)

    grad_branch_second = (upstream_all.astype(wide) * gate_second).astype(low)
    grad_active = mul_t(grad_branch_second, w_fc2)
    grad_hidden = gelu_pull(grad_active)[0].astype(low)
    grad_feed = scatter(mul_t(grad_hidden, w1))

    upstream = upstream_low.astype(wide)
    grad_gate_second = jnp.sum(
        upstream_all.astype(wide) * branch_second_part, axis=0
    ) + second_bias[0] * jnp.sum(upstream, axis=0)
    grad_scale_second = jnp.sum(grad_feed * norm_second, axis=0)
    grad_shift_second = jnp.sum(grad_feed, axis=0)
    grad_middle = upstream + normalize_back(
        norm_second, inverse_second, grad_feed * (1.0 + scale_second)
    )
    grad_gate_first = jnp.sum(grad_middle * branch, axis=0)
    grad_branch = (grad_middle * gate_first).astype(low)
    grad_mixed_tok = mul_t(grad_branch, wp).astype(low)
    grad_mixed = exchange(grad_mixed_tok.reshape(rows, shards, own).transpose(1, 0, 2))
    term_pair = jnp.concatenate(
        [t_mul(feed_all, grad_hidden).astype(low), t_mul(mixed_tok, grad_branch).astype(low)],
        axis=1,
    )
    term_pair = core_half(term_pair.reshape(shards, 2, half, units + features), core)
    term_pair, grad_mixed = lax.optimization_barrier((term_pair, grad_mixed))
    pair_got = exchange(term_pair)
    attend_part, term_qkv, attend_sums, packed_sums = attend_back(
        queries, grad_mixed.reshape(length, own), log_total, keyset, valueset, wq, attend_in, first_got
    )
    attend_part, term_qkv, attend_sums, packed_sums, pair_got = lax.optimization_barrier(
        (attend_part, term_qkv, attend_sums, packed_sums, pair_got)
    )
    packed_sums = packed_sums[0]
    grad_shift_first = attend_sums[0]
    grad_scale_first = attend_sums[1]
    mod_terms = jnp.concatenate(
        [
            grad_shift_first,
            grad_scale_first,
            grad_gate_first,
            grad_shift_second,
            grad_scale_second,
            grad_gate_second,
            jnp.sum(grad_branch.astype(wide), axis=0),
            packed_sums[:own],
            packed_sums[2 * own :],
        ]
    ).astype(low)
    term_qkv = core_half(term_qkv.reshape(shards, 2, half, 3 * own), core)
    last_sent = jnp.concatenate(
        [
            attend_part,
            jnp.concatenate([term_qkv[:, :, :own], term_qkv[:, :, own : 2 * own]], axis=1),
            jnp.concatenate(
                [term_qkv[:, :, 2 * own :], copies(as_rows(mod_terms, half))], axis=1
            ),
        ],
        axis=2,
    )
    last_got = exchange(last_sent)
    second_low = branch_second_part.astype(low).reshape(shards, rows, features)
    second_low, last_got = lax.optimization_barrier((second_low, last_got))
    branch_second = scatter_sum(second_low, place) + second_bias
    output = (middle + gate_second * branch_second).astype(low)
    grad_attend = jnp.sum(last_got[:, :, :features].astype(wide), axis=0)
    near = last_got[:, :, features : features + own]
    far = last_got[:, :, features + own :]
    term_qkv = jnp.concatenate([near[:, :half], near[:, half:], far[:, :half]], axis=2)
    mod_got = far[:, half:].astype(wide)
    head_rows = ada_rows + features // LANES
    mod_sums = jnp.sum(mod_got[:, :head_rows], axis=0)
    bias_qv_all = jnp.concatenate(
        [mod_got[:, head_rows].reshape(features), mod_got[:, head_rows + 1].reshape(features)]
    )
    norm_own, inverse_own = normalize(stream)
    grad_stream = grad_middle + normalize_back(
        norm_own, inverse_own, grad_attend * (1.0 + scale_first)
    )
    grad_latents = grad_stream.astype(low)

    grad_modulation = mod_sums[:ada_rows].reshape(ada_width)
    proj_bias_term = lax.dynamic_slice_in_dim(mod_sums, ada_rows + place, 1, 0)
    cond_term = jnp.sum(w_ada.astype(wide) * grad_modulation[None, :], axis=1)
    cond_total = gather_small(cond_term[None], place).reshape(1, features)
    grad_cond = silu_pull(cond_total)[0]

    second_bias_sums = jnp.sum(grad_branch_second.astype(wide), axis=0)
    rep_terms = jnp.concatenate(
        [
            mod_sums[:ada_rows],
            cond_own.astype(wide),
            proj_bias_term,
            jnp.sum(grad_hidden.astype(wide), axis=0).reshape(units // LANES, LANES),
            lax.dynamic_slice_in_dim(second_bias_sums, place * own, own, 0)[None],
            lax.dynamic_slice_in_dim(bias_qv_all, place * 2 * own, 2 * own, 0).reshape(2, own),
        ]
    )
    rep_terms = jnp.pad(rep_terms, ((0, half - rep_terms.shape[0]), (0, 0))).astype(low)
    rep_terms = jnp.concatenate([rep_terms, swap_core(rep_terms)], axis=1)

    term_first = pair_got[:, :, :units]
    term_proj = jnp.sum(pair_got[:, :, units:].astype(wide), axis=0).astype(low)
    term_second = core_half(
        t_mul(active, grad_branch_second).reshape(1, 2, units // 2, features), core
    )[0]
    piece = units // 2 // shards
    term_second = term_second.reshape(shards, piece, features)
    fold = features // 2

    rep_sent = jnp.concatenate(
        [
            term_first,
            jnp.concatenate([term_second[:, :, :fold], term_second[:, :, fold:]], axis=1),
            term_qkv,
            term_proj.reshape(half, shards, own).transpose(1, 0, 2),
            copies(rep_terms),
        ],
        axis=2,
    )
    rep_got = exchange(rep_sent, CHIPS)
    width = units + fold + 4 * own
    owned = jnp.sum(rep_got[:, :, :width].astype(wide), axis=0).astype(low)
    rep_small = jnp.concatenate(
        [rep_got[:, :, width : width + own], rep_got[:, :, width + own :]], axis=0
    )
    grad_w_ada = t_mul(
        rep_small[:, ada_rows], rep_small[:, :ada_rows].reshape(2 * shards, ada_width)
    )
    rep_sums = jnp.sum(rep_small.astype(wide), axis=0)
    ada_own = ada_rows // shards
    grad_b_ada = lax.dynamic_slice_in_dim(rep_sums, place * ada_own, ada_own, 0)
    grad_b_ada = grad_b_ada.reshape(ada_width // shards)
    at = ada_rows + 1
    grad_b_proj = rep_sums[at]
    at += 1
    grad_b_fc1 = rep_sums[at : at + units // LANES].reshape(units)
    at += units // LANES
    grad_b_fc2 = rep_sums[at]
    grad_bias_qv = rep_sums[at + 1 : at + 3].reshape(2 * own)

    whole_mine = exchange(copies(owned), CHIPS)
    whole_other = swap_core(whole_mine)
    whole = [
        jnp.where(core == 0, whole_mine, whole_other).astype(wide),
        jnp.where(core == 0, whole_other, whole_mine).astype(wide),
    ]

    def side(value):
        return jnp.concatenate([value[k] for k in range(shards)], axis=1)

    grad_w_fc1 = jnp.concatenate([side(part[:, :, :units]) for part in whole], axis=0)
    at = units
    grad_w_fc2 = jnp.concatenate(
        [
            jnp.concatenate(
                [part[:, :piece, at : at + fold], part[:, piece:, at : at + fold]], axis=2
            ).reshape(units // 2, features)
            for part in whole
        ],
        axis=0,
    )
    at += fold
    grad_w_qkv = jnp.concatenate(
        [
            jnp.concatenate(
                [side(part[:, :, at + k * own : at + (k + 1) * own]) for k in range(3)], axis=1
            )
            for part in whole
        ],
        axis=0,
    )
    at += 3 * own
    grad_w_proj = jnp.concatenate([side(part[:, :, at:]) for part in whole], axis=0)

    return (
        output[None],
        grad_latents[None],
        grad_cond,
        grad_w_qkv,
        grad_bias_qv,
        grad_w_proj,
        grad_b_proj,
        grad_w_fc1,
        grad_b_fc1,
        grad_w_fc2,
        grad_b_fc2,
        grad_w_ada,
        grad_b_ada,
    )


def solution(mesh):
    fine = Mesh(mesh.devices.reshape(2, 4, 2, 2, 4), REP + SHARD)
    tokens = P(REP, SHARD, None)
    matrix = P(SHARD, None)
    vector = P(SHARD)
    params = (matrix, vector) * 5
    return jax.shard_map(
        on_device,
        mesh=fine,
        in_specs=(tokens, P(REP, None), tokens) + params,
        out_specs=(tokens, tokens, P(REP, None)) + params,
        check_vma=False,
    )
```

```python
import jax
import jax.numpy as jnp
from jax import lax
from jax.experimental import pallas as pl
from jax.experimental.pallas import tpu as pltpu
from jax.sharding import Mesh, PartitionSpec as P

HEAD = 64
SHARD = ("xh", "y")
CHIPS = ("xl", "z")
REP = ("xl", "z", "core")
LANES = 128
QUERY_BLOCK = 256
SCALE = HEAD ** (-0.5)

epsilon = 1e-06
highest = lax.Precision.HIGHEST
low = jnp.bfloat16
wide = jnp.float32


def swap_core(value):
    return lax.ppermute(value, "core", [(0, 1), (1, 0)])


def exchange(value, axes=SHARD):
    return lax.all_to_all(value, axes, 0, 0, tiled=True)


def copies(value):
    return jnp.broadcast_to(value[None], (8,) + value.shape)


def as_rows(value, count):
    rows = value.reshape(-1, LANES)
    return jnp.pad(rows, ((0, count - rows.shape[0]), (0, 0)))


def normalize(values):
    centered = values - jnp.mean(values, axis=-1, keepdims=True)
    inverse = lax.rsqrt(jnp.mean(centered * centered, axis=-1, keepdims=True) + epsilon)
    return centered * inverse, inverse


def normalize_back(norm, inverse, grad):
    return inverse * (
        grad
        - jnp.mean(grad, axis=-1, keepdims=True)
        - norm * jnp.mean(grad * norm, axis=-1, keepdims=True)
    )


def silu(values):
    return values / (1.0 + jnp.exp(-values))


def gelu_tanh(values):
    return (
        0.5
        * values
        * (1.0 + jnp.tanh(0.7978845608028654 * (values + 0.044715 * values * values * values)))
    )


def mul(left, right):
    return lax.dot_general(left, right, (((1,), (0,)), ((), ())), preferred_element_type=wide)


def mul_t(left, right):
    return lax.dot_general(left, right, (((1,), (1,)), ((), ())), preferred_element_type=wide)


def t_mul(left, right):
    return lax.dot_general(left, right, (((0,), (0,)), ((), ())), preferred_element_type=wide)


def head_of(value, index):
    lane = lax.broadcasted_iota(jnp.int32, value.shape, 1)
    return jnp.where((lane >= HEAD) == (index == 1), value, jnp.zeros_like(value))


def attend_kernel(
    got_ref, wq_ref, scale_ref, shift_ref, qb_ref, vb_ref, in_ref, q_ref, k_ref, v_ref, mixed_ref, log_ref
):
    count, rows, _ = got_ref.shape
    features = scale_ref.shape[1]
    own = qb_ref.shape[1]
    gain = 1.0 + scale_ref[...]
    for block in range(count):
        at = pl.ds(block * rows, rows)
        norm, _ = normalize(got_ref[block, :, 0:features].astype(wide))
        attend_in = (norm * gain + shift_ref[...]).astype(low)
        in_ref[at, :] = attend_in
        packed = mul(attend_in, wq_ref[...])
        q_ref[at, :] = (packed[:, :own] + qb_ref[...]).astype(low)
        k_ref[at, :] = packed[:, own : 2 * own].astype(low)
        v_ref[at, :] = (packed[:, 2 * own :] + vb_ref[...]).astype(low)
    for block in range(count * rows // QUERY_BLOCK):
        at = pl.ds(block * QUERY_BLOCK, QUERY_BLOCK)
        total = None
        logs = None
        for index in range(2):
            scores = mul_t(head_of(q_ref[at, :], index), k_ref[...]) * SCALE
            peak = jnp.max(scores, axis=1, keepdims=True)
            powered = jnp.exp(scores - peak)
            row_total = jnp.sum(powered, axis=1, keepdims=True)
            probs = (powered / row_total).astype(low)
            part = mul(probs, head_of(v_ref[...], index))
            log = head_of(jnp.broadcast_to(peak + jnp.log(row_total), part.shape), index)
            total = part if total is None else total + part
            logs = log if logs is None else logs + log
        mixed_ref[at, :] = total.astype(low)
        log_ref[at, :] = logs


def attend(got, wq, scale, shift, query_bias, value_bias):
    length, features = wq.shape
    length = got.shape[0] * got.shape[1]
    features = wq.shape[0]
    own = wq.shape[1] // 3
    head = jax.ShapeDtypeStruct((length, own), low)
    return pl.pallas_call(
        attend_kernel,
        out_shape=[
            jax.ShapeDtypeStruct((length, features), low),
            head,
            head,
            head,
            head,
            jax.ShapeDtypeStruct((length, own), wide),
        ],
        compiler_params=pltpu.CompilerParams(vmem_limit_bytes=40 * 1024 * 1024),
        cost_estimate=pl.CostEstimate(
            flops=16 * length * length * own,
            transcendentals=2 * length * length,
            bytes_accessed=8 * length * features,
        ),
        name="attend",
    )(got, wq, scale, shift, query_bias, value_bias)


def attend_back_kernel(
    q_ref, g_ref, log_ref, k_ref, v_ref, wq_ref, in_ref, got_ref,
    part_ref, term_ref, sums_ref, packed_sums_ref, packed, key_acc, value_acc,
):
    length, own = q_ref.shape
    count, rows, _ = got_ref.shape
    features = in_ref.shape[1]
    for block in range(length // QUERY_BLOCK):
        at = pl.ds(block * QUERY_BLOCK, QUERY_BLOCK)
        grad_query = None
        for index in range(2):
            query = head_of(q_ref[at, :], index)
            grad = head_of(g_ref[at, :], index)
            log = log_ref[at, index * HEAD : index * HEAD + 1]
            probs = jnp.exp(mul_t(query, k_ref[...]) * SCALE - log)
            grad_probs = mul_t(grad, v_ref[...])
            delta = jnp.sum(probs * grad_probs, axis=1, keepdims=True)
            grad_scores = (probs * (grad_probs - delta)).astype(low)
            part = mul(grad_scores, head_of(k_ref[...], index))
            grad_query = part if grad_query is None else grad_query + part
            key_part = t_mul(grad_scores, query)
            value_part = t_mul(probs.astype(low), grad)
            if block == 0 and index == 0:
                key_acc[...] = key_part
                value_acc[...] = value_part
            else:
                key_acc[...] += key_part
                value_acc[...] += value_part
        packed[at, 0:own] = (grad_query * SCALE).astype(low)
    packed[:, own : 2 * own] = (key_acc[...] * SCALE).astype(low)
    packed[:, 2 * own : 3 * own] = value_acc[...].astype(low)
    packed_sums_ref[...] = jnp.sum(packed[...].astype(wide), axis=0, keepdims=True)
    shift_sum = None
    scale_sum = None
    for block in range(count):
        at = pl.ds(block * rows, rows)
        part = mul_t(packed[at, :], wq_ref[...])
        norm, _ = normalize(got_ref[block, :, 0:features].astype(wide))
        part_ref[block] = part.astype(low)
        one = jnp.sum(part, axis=0, keepdims=True)
        two = jnp.sum(part * norm, axis=0, keepdims=True)
        shift_sum = one if shift_sum is None else shift_sum + one
        scale_sum = two if scale_sum is None else scale_sum + two
    sums_ref[0:1, :] = shift_sum
    sums_ref[1:2, :] = scale_sum
    for block in range(features // QUERY_BLOCK):
        at = pl.ds(block * QUERY_BLOCK, QUERY_BLOCK)
        term_ref[at, :] = t_mul(in_ref[:, at], packed[...]).astype(low)


def attend_back(queries, grad_mixed, logs, keyset, valueset, wq, attend_in, got):
    length, own = queries.shape
    features = attend_in.shape[1]
    count, rows, _ = got.shape
    return pl.pallas_call(
        attend_back_kernel,
        out_shape=[
            jax.ShapeDtypeStruct((count, rows, features), low),
            jax.ShapeDtypeStruct((features, 3 * own), low),
            jax.ShapeDtypeStruct((2, features), wide),
            jax.ShapeDtypeStruct((1, 3 * own), wide),
        ],
        scratch_shapes=[
            pltpu.VMEM((length, 3 * own), low),
            pltpu.VMEM((length, own), wide),
            pltpu.VMEM((length, own), wide),
        ],
        compiler_params=pltpu.CompilerParams(vmem_limit_bytes=40 * 1024 * 1024),
        cost_estimate=pl.CostEstimate(
            flops=32 * length * length * own,
            transcendentals=2 * length * length,
            bytes_accessed=12 * length * features,
        ),
        name="attend_back",
    )(queries, grad_mixed, logs, keyset, valueset, wq, attend_in, got)


def gated_kernel(
    feed_ref, w1_ref, b1_ref, w2_ref, got_ref, gate_ref,
    grad_ref, second_ref, active_ref, hidden_ref, branch_ref, gate_sum, branch_sum, hidden_sum,
):
    count, rows, features = feed_ref.shape
    units = w1_ref.shape[1]
    skip = got_ref.shape[2] - features
    sums = [None, None, None]

    def add(slot, value):
        one = jnp.sum(value, axis=0, keepdims=True)
        sums[slot] = one if sums[slot] is None else sums[slot] + one

    pair = 2
    for block in range(count // pair):
        at = pl.ds(block * pair * rows, pair * rows)
        both = slice(block * pair, (block + 1) * pair)
        feed = feed_ref[both].reshape(pair * rows, features)
        upstream = got_ref[both, :, skip:].reshape(pair * rows, features).astype(wide)
        hidden = mul(feed, w1_ref[...]) + b1_ref[...]
        square = hidden * hidden
        bent = jnp.tanh(0.7978845608028654 * (hidden + 0.044715 * square * hidden))
        rise = 0.5 * (1.0 + bent)
        slope = rise + 0.5 * hidden * (1.0 - bent * bent) * (
            0.7978845608028654 * (1.0 + 3.0 * 0.044715 * square)
        )
        active = (hidden * rise).astype(low)
        active_ref[at, :] = active
        second = mul(active, w2_ref[...])
        second_ref[both] = second.astype(low).reshape(pair, rows, features)
        add(0, upstream * second)
        grad_branch = (upstream * gate_ref[...]).astype(low)
        branch_ref[at, :] = grad_branch
        add(1, grad_branch.astype(wide))
        grad_hidden = (mul_t(grad_branch, w2_ref[...]) * slope).astype(low)
        hidden_ref[at, :] = grad_hidden
        add(2, grad_hidden.astype(wide))
        grad_feed = mul_t(grad_hidden, w1_ref[...]).astype(low)
        grad_ref[both] = grad_feed.reshape(pair, rows, features)
    gate_sum[...] = sums[0]
    branch_sum[...] = sums[1]
    hidden_sum[...] = sums[2]


def gated(feed, w1, b1, w2, got, gate):
    count, rows, features = feed.shape
    units = w1.shape[1]
    length = count * rows
    return pl.pallas_call(
        gated_kernel,
        out_shape=[
            jax.ShapeDtypeStruct((count, rows, features), low),
            jax.ShapeDtypeStruct((count, rows, features), low),
            jax.ShapeDtypeStruct((length, units), low),
            jax.ShapeDtypeStruct((length, units), low),
            jax.ShapeDtypeStruct((length, features), low),
            jax.ShapeDtypeStruct((1, features), wide),
            jax.ShapeDtypeStruct((1, features), wide),
            jax.ShapeDtypeStruct((1, units), wide),
        ],
        compiler_params=pltpu.CompilerParams(vmem_limit_bytes=40 * 1024 * 1024),
        cost_estimate=pl.CostEstimate(
            flops=8 * length * features * units,
            transcendentals=length * units,
            bytes_accessed=16 * length * features,
        ),
        name="gated",
    )(feed, w1, b1, w2, got, gate)


def weights_kernel(feed_ref, hidden_ref, active_ref, branch_ref, first_ref, second_ref):
    features = feed_ref.shape[1]
    units = hidden_ref.shape[1]
    own = 2 * first_ref.shape[2]
    half = own // 2
    for block in range(features // QUERY_BLOCK):
        at = pl.ds(block * QUERY_BLOCK, QUERY_BLOCK)
        term = t_mul(feed_ref[:, at], hidden_ref[...]).astype(low)
        for piece in range(QUERY_BLOCK // own):
            target = block * (QUERY_BLOCK // own) + piece
            first_ref[0, target] = term[piece * own : piece * own + half]
            first_ref[1, target] = term[piece * own + half : (piece + 1) * own]
    for block in range(units // QUERY_BLOCK):
        at = pl.ds(block * QUERY_BLOCK, QUERY_BLOCK)
        second_ref[at, :] = t_mul(active_ref[:, at], branch_ref[...]).astype(low)


def weights_back(feed, grad_hidden, active, grad_branch, shards):
    length, features = feed.shape
    units = active.shape[1]
    return pl.pallas_call(
        weights_kernel,
        out_shape=[
            jax.ShapeDtypeStruct((2, shards, features // shards // 2, units), low),
            jax.ShapeDtypeStruct((units, features), low),
        ],
        compiler_params=pltpu.CompilerParams(vmem_limit_bytes=40 * 1024 * 1024),
        cost_estimate=pl.CostEstimate(
            flops=4 * length * features * units,
            transcendentals=0,
            bytes_accessed=10 * length * features,
        ),
        name="weights_back",
    )(feed, grad_hidden, active, grad_branch)


def proj_kernel(got_ref, grad_ref, out_ref):
    count = got_ref.shape[0]
    half = out_ref.shape[2]
    for block in range(count):
        term = t_mul(got_ref[block, :, 0 : 2 * half], grad_ref[...]).astype(low)
        out_ref[0, block] = term[:half]
        out_ref[1, block] = term[half:]


def proj_back(got, grad, own):
    count, rows, _ = got.shape
    features = grad.shape[1]
    return pl.pallas_call(
        proj_kernel,
        out_shape=jax.ShapeDtypeStruct((2, count, own // 2, features), low),
        compiler_params=pltpu.CompilerParams(vmem_limit_bytes=40 * 1024 * 1024),
        name="proj_back",
    )(got, grad)


def unpack_kernel(core_ref, mine_ref, other_ref, first_ref, second_ref, qkv_ref, proj_ref):
    count, half, _ = mine_ref.shape
    units = first_ref.shape[1] // count
    features = second_ref.shape[1]
    fold = features // 2
    own = proj_ref.shape[1] // count
    piece = half // 2
    for side in range(2):
        rows = pl.ds(side * half, half)
        for block in range(count):
            value = jnp.where(
                core_ref[0] == side, mine_ref[block], other_ref[block]
            ).astype(wide)
            first_ref[rows, block * units : (block + 1) * units] = value[:, :units]
            at = pl.ds((side * count + block) * piece, piece)
            second_ref[at, :fold] = value[:piece, units : units + fold]
            second_ref[at, fold:] = value[piece:, units : units + fold]
            for part in range(3):
                lane = part * features + block * own
                start = units + fold + part * own
                qkv_ref[rows, lane : lane + own] = value[:, start : start + own]
            proj_ref[rows, block * own : (block + 1) * own] = value[:, units + fold + 3 * own :]


def unpack(core, mine, other, units, features):
    count, half, _ = mine.shape
    return pl.pallas_call(
        unpack_kernel,
        in_specs=[
            pl.BlockSpec(memory_space=pltpu.SMEM),
            pl.BlockSpec(memory_space=pltpu.VMEM),
            pl.BlockSpec(memory_space=pltpu.VMEM),
        ],
        out_shape=[
            jax.ShapeDtypeStruct((2 * half, count * units), wide),
            jax.ShapeDtypeStruct((units, features), wide),
            jax.ShapeDtypeStruct((2 * half, 3 * features), wide),
            jax.ShapeDtypeStruct((2 * half, features), wide),
        ],
        compiler_params=pltpu.CompilerParams(vmem_limit_bytes=40 * 1024 * 1024),
        name="unpack",
    )(core, mine, other)


def swap_add(value, core):
    keep = lax.dynamic_index_in_dim(value, core, 0, keepdims=False)
    give = lax.dynamic_index_in_dim(value, 1 - core, 0, keepdims=False)
    return (keep.astype(wide) + swap_core(give).astype(wide)).astype(low)


def shift_to(value, dx, dy):
    pairs = [(x * 4 + y, ((x + dx) % 2) * 4 + (y + dy) % 4) for x in range(2) for y in range(4)]
    return lax.ppermute(value, SHARD, pairs)


def scatter_sum(total, value, place, offsets):
    for dx, dy in offsets:
        target = ((place // 4 + dx) % 2) * 4 + (place + dy) % 4
        block = lax.dynamic_index_in_dim(value, target, 0, keepdims=False)
        total = total + shift_to(block, dx, dy).astype(wide)
    return total


def gather_small(value, place):
    for bit in (1, 2, 4):
        other = lax.ppermute(value, SHARD, [(k, k ^ bit) for k in range(8)])
        upper = (place // bit) % 2 == 1
        value = jnp.concatenate(
            [jnp.where(upper, other, value), jnp.where(upper, value, other)], axis=0
        )
    return value


def join_rows(mine, other, core):
    first = jnp.where(core == 0, mine, other)
    second = jnp.where(core == 0, other, mine)
    return jnp.concatenate([first, second], axis=1).reshape(-1, mine.shape[-1])


def core_half(value, core):
    keep = lax.dynamic_index_in_dim(value, core, 1, keepdims=False)
    give = lax.dynamic_index_in_dim(value, 1 - core, 1, keepdims=False).astype(low)
    return (keep.astype(wide) + swap_core(give).astype(wide)).astype(low)


def on_device(
    latents, cond, cotangent, w_qkv, bias_qv, w_proj, b_proj, w_fc1, b_fc1, w_fc2, b_fc2, w_ada, b_ada
):
    stream_low = latents[0]
    upstream_low = cotangent[0]
    rows, features = stream_low.shape
    shards = 8
    length = shards * rows
    own = features // shards
    half = own // 2
    units = w_fc2.shape[0]
    ada_width = w_ada.shape[1]
    ada_rows = ada_width // LANES
    place = lax.axis_index(SHARD)
    core = lax.axis_index("core")

    cond_value = cond.astype(wide)
    cond_silu, silu_pull = jax.vjp(silu, cond_value)
    cond_low = cond_silu.astype(low)
    cond_own = lax.dynamic_slice_in_dim(cond_low, place * own, own, 1)
    mod_part = mul(cond_own, w_ada)[0]
    blocks = jnp.arange(shards)[:, None] == place
    mod_part = mod_part + jnp.where(blocks, b_ada.astype(wide)[None, :], 0.0).reshape(ada_width)
    small = jnp.concatenate([mod_part.astype(low), bias_qv, b_proj, b_fc2])

    def halved(value):
        return lax.dynamic_slice_in_dim(value, core * half, half, 0)

    qkv_mine = halved(w_qkv)

    def qkv_part(part):
        return jnp.stack(
            [
                qkv_mine[:, part * features + k * own : part * features + (k + 1) * own]
                for k in range(shards)
            ]
        )

    first_sent = jnp.concatenate(
        [
            copies(stream_low),
            jnp.concatenate([qkv_part(0), qkv_part(1)], axis=1),
            jnp.concatenate([qkv_part(2), copies(as_rows(small, half))], axis=1),
        ],
        axis=2,
    )
    first_got = exchange(first_sent)
    weights_sent = jnp.concatenate(
        [
            halved(w_fc1).reshape(half, shards, units).transpose(1, 0, 2),
            copies(halved(w_proj)),
        ],
        axis=2,
    )
    weights_sent, first_got = lax.optimization_barrier((weights_sent, first_got))
    weights_got = exchange(weights_sent)
    near = first_got[:, :, features : features + own]
    far = first_got[:, :, features + own :]
    qkv_got = jnp.concatenate([near[:, :half], near[:, half:], far[:, :half]], axis=2)
    wq = join_rows(qkv_got, swap_core(qkv_got), core)
    small_got = far[:, half:].astype(wide)
    modulation = jnp.sum(small_got[:, :ada_rows], axis=0).reshape(1, ada_width)
    shift_first, scale_first, gate_first, shift_second, scale_second, gate_second = jnp.split(
        modulation, 6, axis=1
    )
    at = ada_rows
    bias_wide = small_got[:, at : at + 2].reshape(1, 2 * features)
    proj_bias = small_got[:, at + 2].reshape(1, features)
    second_bias = small_got[:, at + 3].reshape(1, features)

    query_bias = lax.dynamic_slice_in_dim(bias_wide, place * own, own, 1)
    value_bias = lax.dynamic_slice_in_dim(bias_wide, features + place * own, own, 1)
    attend_in, queries, keyset, valueset, mixed, log_total = attend(
        first_got, wq, scale_first, shift_first, query_bias, value_bias
    )
    mixed, weights_got = lax.optimization_barrier((mixed, weights_got))
    mixed_got = exchange(
        jnp.concatenate([mixed.reshape(shards, rows, own), copies(upstream_low)], axis=2)
    )
    weights_other = swap_core(weights_got)
    w1 = join_rows(weights_got[:, :, :units], weights_other[:, :, :units], core)
    wp = join_rows(weights_got[:, :, units:], weights_other[:, :, units:], core)
    mixed_tok = mixed_got[:, :, :own].transpose(1, 0, 2).reshape(rows, features)
    upstream_all = mixed_got[:, :, own:].reshape(length, features)
    branch = mul(mixed_tok, wp) + proj_bias
    stream = stream_low.astype(wide)
    middle = stream + gate_first * branch
    norm_second, inverse_second = normalize(middle)
    feed_in = (norm_second * (1.0 + scale_second) + shift_second).astype(low)
    feed_got = exchange(copies(feed_in))
    (
        feed_part,
        second_low,
        active,
        grad_hidden,
        grad_branch_second,
        gate_sums,
        second_bias_sums,
        hidden_sums,
    ) = gated(feed_got, w1, b_fc1.astype(wide)[None, :], w_fc2, mixed_got, gate_second)
    feed_back = exchange(feed_part)
    term_first, term_second = weights_back(
        feed_got.reshape(length, features), grad_hidden, active, grad_branch_second, shards
    )
    term_first = swap_add(term_first, core)
    feed_back, term_first, term_second = lax.optimization_barrier(
        (feed_back, term_first, term_second)
    )
    grad_feed = jnp.sum(feed_back.astype(wide), axis=0)

    upstream = upstream_low.astype(wide)
    grad_gate_second = gate_sums[0] + second_bias[0] * jnp.sum(upstream, axis=0)
    grad_scale_second = jnp.sum(grad_feed * norm_second, axis=0)
    grad_shift_second = jnp.sum(grad_feed, axis=0)
    grad_middle = upstream + normalize_back(
        norm_second, inverse_second, grad_feed * (1.0 + scale_second)
    )
    grad_gate_first = jnp.sum(grad_middle * branch, axis=0)
    grad_branch = (grad_middle * gate_first).astype(low)
    grad_mixed_tok = mul_t(grad_branch, wp).astype(low)
    grad_mixed = exchange(grad_mixed_tok.reshape(rows, shards, own).transpose(1, 0, 2))
    term_proj = proj_back(mixed_got, grad_branch, own)
    term_proj, grad_mixed = lax.optimization_barrier((term_proj, grad_mixed))
    pair_got = exchange(jnp.concatenate([term_first, swap_add(term_proj, core)], axis=2))
    attend_part, term_qkv, attend_sums, packed_sums = attend_back(
        queries, grad_mixed.reshape(length, own), log_total, keyset, valueset, wq, attend_in, first_got
    )
    attend_part, term_qkv, attend_sums, packed_sums, pair_got = lax.optimization_barrier(
        (attend_part, term_qkv, attend_sums, packed_sums, pair_got)
    )
    packed_sums = packed_sums[0]
    grad_shift_first = attend_sums[0]
    grad_scale_first = attend_sums[1]
    mod_terms = jnp.concatenate(
        [
            grad_shift_first,
            grad_scale_first,
            grad_gate_first,
            grad_shift_second,
            grad_scale_second,
            grad_gate_second,
            jnp.sum(grad_branch.astype(wide), axis=0),
            packed_sums[:own],
            packed_sums[2 * own :],
        ]
    ).astype(low)
    term_qkv = core_half(term_qkv.reshape(shards, 2, half, 3 * own), core)
    last_sent = jnp.concatenate(
        [
            attend_part,
            jnp.concatenate([term_qkv[:, :, :own], term_qkv[:, :, own : 2 * own]], axis=1),
            jnp.concatenate(
                [term_qkv[:, :, 2 * own :], copies(as_rows(mod_terms, half))], axis=1
            ),
        ],
        axis=2,
    )
    last_got = exchange(last_sent)
    second_low, last_got = lax.optimization_barrier((second_low, last_got))
    second_own = lax.dynamic_index_in_dim(second_low, place, 0, keepdims=False).astype(wide)
    second_near = scatter_sum(second_own, second_low, place, ((0, 1), (0, 3), (0, 2)))
    grad_attend = jnp.sum(last_got[:, :, :features].astype(wide), axis=0)
    near = last_got[:, :, features : features + own]
    far = last_got[:, :, features + own :]
    term_qkv = jnp.concatenate([near[:, :half], near[:, half:], far[:, :half]], axis=2)
    mod_got = far[:, half:].astype(wide)
    head_rows = ada_rows + features // LANES
    mod_sums = jnp.sum(mod_got[:, :head_rows], axis=0)
    bias_qv_all = jnp.concatenate(
        [mod_got[:, head_rows].reshape(features), mod_got[:, head_rows + 1].reshape(features)]
    )
    norm_own, inverse_own = normalize(stream)
    grad_stream = grad_middle + normalize_back(
        norm_own, inverse_own, grad_attend * (1.0 + scale_first)
    )
    grad_latents = grad_stream.astype(low)

    grad_modulation = mod_sums[:ada_rows].reshape(ada_width)
    proj_bias_term = lax.dynamic_slice_in_dim(mod_sums, ada_rows + place, 1, 0)
    cond_term = jnp.sum(w_ada.astype(wide) * grad_modulation[None, :], axis=1)
    cond_total = gather_small(cond_term[None], place).reshape(1, features)
    grad_cond = silu_pull(cond_total)[0]

    second_bias_sums = second_bias_sums[0]
    rep_terms = jnp.concatenate(
        [
            mod_sums[:ada_rows],
            cond_own.astype(wide),
            proj_bias_term,
            hidden_sums.reshape(units // LANES, LANES),
            lax.dynamic_slice_in_dim(second_bias_sums, place * own, own, 0)[None],
            lax.dynamic_slice_in_dim(bias_qv_all, place * 2 * own, 2 * own, 0).reshape(2, own),
        ]
    )
    rep_terms = jnp.pad(rep_terms, ((0, half - rep_terms.shape[0]), (0, 0))).astype(low)
    rep_terms = jnp.concatenate([rep_terms, swap_core(rep_terms)], axis=1)

    term_first = pair_got[:, :, :units]
    term_proj = jnp.sum(pair_got[:, :, units:].astype(wide), axis=0).astype(low)
    term_second = swap_add(term_second.reshape(2, units // 2, features), core)
    piece = units // 2 // shards
    term_second = term_second.reshape(shards, piece, features)
    fold = features // 2

    rep_sent = jnp.concatenate(
        [
            term_first,
            jnp.concatenate([term_second[:, :, :fold], term_second[:, :, fold:]], axis=1),
            term_qkv,
            term_proj.reshape(half, shards, own).transpose(1, 0, 2),
            copies(rep_terms),
        ],
        axis=2,
    )
    rep_got = exchange(rep_sent, CHIPS)
    width = units + fold + 4 * own
    owned = jnp.sum(rep_got[:, :, :width].astype(wide), axis=0).astype(low)
    rep_small = jnp.concatenate(
        [rep_got[:, :, width : width + own], rep_got[:, :, width + own :]], axis=0
    )
    grad_w_ada = t_mul(
        rep_small[:, ada_rows], rep_small[:, :ada_rows].reshape(2 * shards, ada_width)
    )
    rep_sums = jnp.sum(rep_small.astype(wide), axis=0)
    ada_own = ada_rows // shards
    grad_b_ada = lax.dynamic_slice_in_dim(rep_sums, place * ada_own, ada_own, 0)
    grad_b_ada = grad_b_ada.reshape(ada_width // shards)
    at = ada_rows + 1
    grad_b_proj = rep_sums[at]
    at += 1
    grad_b_fc1 = rep_sums[at : at + units // LANES].reshape(units)
    at += units // LANES
    grad_b_fc2 = rep_sums[at]
    grad_bias_qv = rep_sums[at + 1 : at + 3].reshape(2 * own)

    owned, second_near = lax.optimization_barrier((owned, second_near))
    whole_mine = exchange(copies(owned), CHIPS)
    branch_second = (
        scatter_sum(second_near, second_low, place, ((1, 0), (1, 1), (1, 3), (1, 2)))
        + second_bias
    )
    output = (middle + gate_second * branch_second).astype(low)
    whole_mine, grad_w_ada = lax.optimization_barrier((whole_mine, grad_w_ada))
    grad_w_fc1, grad_w_fc2, grad_w_qkv, grad_w_proj = unpack(
        core.astype(jnp.int32)[None], whole_mine, swap_core(whole_mine), units, features
    )

    return (
        output[None],
        grad_latents[None],
        grad_cond,
        grad_w_qkv,
        grad_bias_qv,
        grad_w_proj,
        grad_b_proj,
        grad_w_fc1,
        grad_b_fc1,
        grad_w_fc2,
        grad_b_fc2,
        grad_w_ada,
        grad_b_ada,
    )


def solution(mesh):
    fine = Mesh(mesh.devices.reshape(2, 4, 2, 2, 4), REP + SHARD)
    tokens = P(REP, SHARD, None)
    matrix = P(SHARD, None)
    vector = P(SHARD)
    params = (matrix, vector) * 5
    return jax.shard_map(
        on_device,
        mesh=fine,
        in_specs=(tokens, P(REP, None), tokens) + params,
        out_specs=(tokens, tokens, P(REP, None)) + params,
        check_vma=False,
    )
```

```python
import jax
import jax.numpy as jnp
from jax import lax
from jax.experimental import pallas as pl
from jax.experimental.pallas import tpu as pltpu
from jax.sharding import Mesh, PartitionSpec as P

HEAD = 64
SHARD = ("xh", "y")
CHIPS = ("xl", "z")
REP = ("xl", "z", "core")
LANES = 128
QUERY_BLOCK = 256
SCALE = HEAD ** (-0.5)

epsilon = 1e-06
highest = lax.Precision.HIGHEST
low = jnp.bfloat16
wide = jnp.float32


def swap_core(value):
    return lax.ppermute(value, "core", [(0, 1), (1, 0)])


def exchange(value, axes=SHARD):
    return lax.all_to_all(value, axes, 0, 0, tiled=True)


def copies(value):
    return jnp.broadcast_to(value[None], (8,) + value.shape)


def as_rows(value, count):
    rows = value.reshape(-1, LANES)
    return jnp.pad(rows, ((0, count - rows.shape[0]), (0, 0)))


def normalize(values):
    centered = values - jnp.mean(values, axis=-1, keepdims=True)
    inverse = lax.rsqrt(jnp.mean(centered * centered, axis=-1, keepdims=True) + epsilon)
    return centered * inverse, inverse


def normalize_back(norm, inverse, grad):
    return inverse * (
        grad
        - jnp.mean(grad, axis=-1, keepdims=True)
        - norm * jnp.mean(grad * norm, axis=-1, keepdims=True)
    )


def silu(values):
    return values / (1.0 + jnp.exp(-values))


def gelu_tanh(values):
    return (
        0.5
        * values
        * (1.0 + jnp.tanh(0.7978845608028654 * (values + 0.044715 * values * values * values)))
    )


def mul(left, right):
    return lax.dot_general(left, right, (((1,), (0,)), ((), ())), preferred_element_type=wide)


def mul_t(left, right):
    return lax.dot_general(left, right, (((1,), (1,)), ((), ())), preferred_element_type=wide)


def t_mul(left, right):
    return lax.dot_general(left, right, (((0,), (0,)), ((), ())), preferred_element_type=wide)


def head_of(value, index):
    lane = lax.broadcasted_iota(jnp.int32, value.shape, 1)
    return jnp.where((lane >= HEAD) == (index == 1), value, jnp.zeros_like(value))


def attend_kernel(
    got_ref, wq_ref, scale_ref, shift_ref, qb_ref, vb_ref, in_ref, q_ref, k_ref, v_ref, mixed_ref, log_ref
):
    count, rows, _ = got_ref.shape
    features = scale_ref.shape[1]
    own = qb_ref.shape[1]
    gain = 1.0 + scale_ref[...]
    for block in range(count):
        at = pl.ds(block * rows, rows)
        norm, _ = normalize(got_ref[block, :, 0:features].astype(wide))
        attend_in = (norm * gain + shift_ref[...]).astype(low)
        in_ref[at, :] = attend_in
        packed = mul(attend_in, wq_ref[...])
        q_ref[at, :] = (packed[:, :own] + qb_ref[...]).astype(low)
        k_ref[at, :] = packed[:, own : 2 * own].astype(low)
        v_ref[at, :] = (packed[:, 2 * own :] + vb_ref[...]).astype(low)
    for block in range(count * rows // QUERY_BLOCK):
        at = pl.ds(block * QUERY_BLOCK, QUERY_BLOCK)
        total = None
        logs = None
        for index in range(2):
            scores = mul_t(head_of(q_ref[at, :], index), k_ref[...]) * SCALE
            peak = jnp.max(scores, axis=1, keepdims=True)
            powered = jnp.exp(scores - peak)
            row_total = jnp.sum(powered, axis=1, keepdims=True)
            probs = (powered / row_total).astype(low)
            part = mul(probs, head_of(v_ref[...], index))
            log = head_of(jnp.broadcast_to(peak + jnp.log(row_total), part.shape), index)
            total = part if total is None else total + part
            logs = log if logs is None else logs + log
        mixed_ref[at, :] = total.astype(low)
        log_ref[at, :] = logs


def attend(got, wq, scale, shift, query_bias, value_bias):
    length, features = wq.shape
    length = got.shape[0] * got.shape[1]
    features = wq.shape[0]
    own = wq.shape[1] // 3
    head = jax.ShapeDtypeStruct((length, own), low)
    return pl.pallas_call(
        attend_kernel,
        out_shape=[
            jax.ShapeDtypeStruct((length, features), low),
            head,
            head,
            head,
            head,
            jax.ShapeDtypeStruct((length, own), wide),
        ],
        compiler_params=pltpu.CompilerParams(vmem_limit_bytes=40 * 1024 * 1024),
        cost_estimate=pl.CostEstimate(
            flops=16 * length * length * own,
            transcendentals=2 * length * length,
            bytes_accessed=8 * length * features,
        ),
        name="attend",
    )(got, wq, scale, shift, query_bias, value_bias)


def attend_back_kernel(
    q_ref, g_ref, log_ref, k_ref, v_ref, wq_ref, in_ref, got_ref,
    part_ref, term_ref, sums_ref, packed_sums_ref, packed, key_acc, value_acc,
):
    length, own = q_ref.shape
    count, rows, _ = got_ref.shape
    features = in_ref.shape[1]
    for block in range(length // QUERY_BLOCK):
        at = pl.ds(block * QUERY_BLOCK, QUERY_BLOCK)
        grad_query = None
        for index in range(2):
            query = head_of(q_ref[at, :], index)
            grad = head_of(g_ref[at, :], index)
            log = log_ref[at, index * HEAD : index * HEAD + 1]
            probs = jnp.exp(mul_t(query, k_ref[...]) * SCALE - log)
            grad_probs = mul_t(grad, v_ref[...])
            delta = jnp.sum(probs * grad_probs, axis=1, keepdims=True)
            grad_scores = (probs * (grad_probs - delta)).astype(low)
            part = mul(grad_scores, head_of(k_ref[...], index))
            grad_query = part if grad_query is None else grad_query + part
            key_part = t_mul(grad_scores, query)
            value_part = t_mul(probs.astype(low), grad)
            if block == 0 and index == 0:
                key_acc[...] = key_part
                value_acc[...] = value_part
            else:
                key_acc[...] += key_part
                value_acc[...] += value_part
        packed[at, 0:own] = (grad_query * SCALE).astype(low)
    packed[:, own : 2 * own] = (key_acc[...] * SCALE).astype(low)
    packed[:, 2 * own : 3 * own] = value_acc[...].astype(low)
    packed_sums_ref[...] = jnp.sum(packed[...].astype(wide), axis=0, keepdims=True)
    shift_sum = None
    scale_sum = None
    for block in range(count):
        at = pl.ds(block * rows, rows)
        part = mul_t(packed[at, :], wq_ref[...])
        norm, _ = normalize(got_ref[block, :, 0:features].astype(wide))
        part_ref[block] = part.astype(low)
        one = jnp.sum(part, axis=0, keepdims=True)
        two = jnp.sum(part * norm, axis=0, keepdims=True)
        shift_sum = one if shift_sum is None else shift_sum + one
        scale_sum = two if scale_sum is None else scale_sum + two
    sums_ref[0:1, :] = shift_sum
    sums_ref[1:2, :] = scale_sum
    for block in range(features // QUERY_BLOCK):
        at = pl.ds(block * QUERY_BLOCK, QUERY_BLOCK)
        term_ref[at, :] = t_mul(in_ref[:, at], packed[...]).astype(low)


def attend_back(queries, grad_mixed, logs, keyset, valueset, wq, attend_in, got):
    length, own = queries.shape
    features = attend_in.shape[1]
    count, rows, _ = got.shape
    return pl.pallas_call(
        attend_back_kernel,
        out_shape=[
            jax.ShapeDtypeStruct((count, rows, features), low),
            jax.ShapeDtypeStruct((features, 3 * own), low),
            jax.ShapeDtypeStruct((2, features), wide),
            jax.ShapeDtypeStruct((1, 3 * own), wide),
        ],
        scratch_shapes=[
            pltpu.VMEM((length, 3 * own), low),
            pltpu.VMEM((length, own), wide),
            pltpu.VMEM((length, own), wide),
        ],
        compiler_params=pltpu.CompilerParams(vmem_limit_bytes=40 * 1024 * 1024),
        cost_estimate=pl.CostEstimate(
            flops=32 * length * length * own,
            transcendentals=2 * length * length,
            bytes_accessed=12 * length * features,
        ),
        name="attend_back",
    )(queries, grad_mixed, logs, keyset, valueset, wq, attend_in, got)


def gated_kernel(
    feed_ref, w1_ref, b1_ref, w2_ref, got_ref, gate_ref,
    grad_ref, second_ref, active_ref, hidden_ref, branch_ref, gate_sum, branch_sum, hidden_sum,
):
    count, rows, features = feed_ref.shape
    units = w1_ref.shape[1]
    skip = got_ref.shape[2] - features
    sums = [None, None, None]

    def add(slot, value):
        one = jnp.sum(value, axis=0, keepdims=True)
        sums[slot] = one if sums[slot] is None else sums[slot] + one

    pair = 2
    for block in range(count // pair):
        at = pl.ds(block * pair * rows, pair * rows)
        both = slice(block * pair, (block + 1) * pair)
        feed = feed_ref[both].reshape(pair * rows, features)
        upstream = got_ref[both, :, skip:].reshape(pair * rows, features).astype(wide)
        hidden = mul(feed, w1_ref[...]) + b1_ref[...]
        square = hidden * hidden
        bent = jnp.tanh(0.7978845608028654 * (hidden + 0.044715 * square * hidden))
        rise = 0.5 * (1.0 + bent)
        slope = rise + 0.5 * hidden * (1.0 - bent * bent) * (
            0.7978845608028654 * (1.0 + 3.0 * 0.044715 * square)
        )
        active = (hidden * rise).astype(low)
        active_ref[at, :] = active
        second = mul(active, w2_ref[...])
        second_ref[both] = second.astype(low).reshape(pair, rows, features)
        add(0, upstream * second)
        grad_branch = (upstream * gate_ref[...]).astype(low)
        branch_ref[at, :] = grad_branch
        add(1, grad_branch.astype(wide))
        grad_hidden = (mul_t(grad_branch, w2_ref[...]) * slope).astype(low)
        hidden_ref[at, :] = grad_hidden
        add(2, grad_hidden.astype(wide))
        grad_feed = mul_t(grad_hidden, w1_ref[...]).astype(low)
        grad_ref[both] = grad_feed.reshape(pair, rows, features)
    gate_sum[...] = sums[0]
    branch_sum[...] = sums[1]
    hidden_sum[...] = sums[2]


def gated(feed, w1, b1, w2, got, gate):
    count, rows, features = feed.shape
    units = w1.shape[1]
    length = count * rows
    return pl.pallas_call(
        gated_kernel,
        out_shape=[
            pltpu.HBM((count, rows, features), low),
            pltpu.HBM((count, rows, features), low),
            pltpu.HBM((length, units), low),
            pltpu.HBM((length, units), low),
            pltpu.HBM((length, features), low),
            jax.ShapeDtypeStruct((1, features), wide),
            jax.ShapeDtypeStruct((1, features), wide),
            jax.ShapeDtypeStruct((1, units), wide),
        ],
        compiler_params=pltpu.CompilerParams(vmem_limit_bytes=40 * 1024 * 1024),
        cost_estimate=pl.CostEstimate(
            flops=8 * length * features * units,
            transcendentals=length * units,
            bytes_accessed=16 * length * features,
        ),
        name="gated",
    )(feed, w1, b1, w2, got, gate)


def weights_kernel(feed_ref, hidden_ref, active_ref, branch_ref, first_ref, second_ref):
    features = feed_ref.shape[1]
    units = hidden_ref.shape[1]
    own = 2 * first_ref.shape[2]
    half = own // 2
    for block in range(features // QUERY_BLOCK):
        at = pl.ds(block * QUERY_BLOCK, QUERY_BLOCK)
        term = t_mul(feed_ref[:, at], hidden_ref[...]).astype(low)
        for piece in range(QUERY_BLOCK // own):
            target = block * (QUERY_BLOCK // own) + piece
            first_ref[0, target] = term[piece * own : piece * own + half]
            first_ref[1, target] = term[piece * own + half : (piece + 1) * own]
    for block in range(units // QUERY_BLOCK):
        at = pl.ds(block * QUERY_BLOCK, QUERY_BLOCK)
        second_ref[at, :] = t_mul(active_ref[:, at], branch_ref[...]).astype(low)


def weights_back(feed, grad_hidden, active, grad_branch, shards):
    length, features = feed.shape
    units = active.shape[1]
    return pl.pallas_call(
        weights_kernel,
        out_shape=[
            jax.ShapeDtypeStruct((2, shards, features // shards // 2, units), low),
            jax.ShapeDtypeStruct((units, features), low),
        ],
        compiler_params=pltpu.CompilerParams(vmem_limit_bytes=40 * 1024 * 1024),
        cost_estimate=pl.CostEstimate(
            flops=4 * length * features * units,
            transcendentals=0,
            bytes_accessed=10 * length * features,
        ),
        name="weights_back",
    )(feed, grad_hidden, active, grad_branch)


def proj_kernel(got_ref, grad_ref, out_ref):
    count = got_ref.shape[0]
    half = out_ref.shape[2]
    for block in range(count):
        term = t_mul(got_ref[block, :, 0 : 2 * half], grad_ref[...]).astype(low)
        out_ref[0, block] = term[:half]
        out_ref[1, block] = term[half:]


def proj_back(got, grad, own):
    count, rows, _ = got.shape
    features = grad.shape[1]
    return pl.pallas_call(
        proj_kernel,
        out_shape=jax.ShapeDtypeStruct((2, count, own // 2, features), low),
        compiler_params=pltpu.CompilerParams(vmem_limit_bytes=40 * 1024 * 1024),
        name="proj_back",
    )(got, grad)


def unpack_kernel(
    at_ref, mine_ref, other_ref, mine_qkv_ref, other_qkv_ref, first_ref, second_ref, qkv_ref, proj_ref
):
    count, half, _ = mine_ref.shape
    units = first_ref.shape[1] // count
    features = second_ref.shape[1]
    fold = features // 2
    own = proj_ref.shape[1] // count
    piece = half // 2
    core, far, deep = at_ref[0], at_ref[1], at_ref[2]
    for side in range(2):
        rows = pl.ds(side * half, half)
        here = core == side
        for block in range(count):
            turn = ((far + 2 - block // 4) % 2) * 4 + (deep + 4 - block % 4) % 4
            value = jnp.where(here, mine_ref[turn], other_ref[turn]).astype(wide)
            first_ref[rows, block * units : (block + 1) * units] = value[:, :units]
            at = pl.ds((side * count + block) * piece, piece)
            second_ref[at, :fold] = value[:piece, units : units + fold]
            second_ref[at, fold:] = value[piece:, units : units + fold]
            proj_ref[rows, block * own : (block + 1) * own] = value[:, units + fold :]
            value = jnp.where(here, mine_qkv_ref[block], other_qkv_ref[block]).astype(wide)
            for part in range(3):
                lane = part * features + block * own
                qkv_ref[rows, lane : lane + own] = value[:, part * own : (part + 1) * own]


def unpack(at, mine, other, mine_qkv, other_qkv, units, features):
    count, half, _ = mine.shape
    return pl.pallas_call(
        unpack_kernel,
        in_specs=[pl.BlockSpec(memory_space=pltpu.SMEM)]
        + [pl.BlockSpec(memory_space=pltpu.VMEM)] * 4,
        out_shape=[
            jax.ShapeDtypeStruct((2 * half, count * units), wide),
            jax.ShapeDtypeStruct((units, features), wide),
            jax.ShapeDtypeStruct((2 * half, 3 * features), wide),
            jax.ShapeDtypeStruct((2 * half, features), wide),
        ],
        compiler_params=pltpu.CompilerParams(vmem_limit_bytes=40 * 1024 * 1024),
        name="unpack",
    )(at, mine, other, mine_qkv, other_qkv)


def shift_chip(value, dx, dz):
    pairs = [(x * 4 + z, ((x + dx) % 2) * 4 + (z + dz) % 4) for x in range(2) for z in range(4)]
    return lax.ppermute(value, CHIPS, pairs)


def reduce_chips(value, far, deep):
    total = None
    for turn in range(8):
        dx, dz = turn // 4, turn % 4
        target = ((far + dx) % 2) * 4 + (deep + dz) % 4
        block = lax.dynamic_index_in_dim(value, target, 0, keepdims=False)
        block = (block if turn == 0 else shift_chip(block, dx, dz)).astype(wide)
        total = block if total is None else total + block
    return total.astype(low)


def gather_chips(value):
    return jnp.stack(
        [value if turn == 0 else shift_chip(value, turn // 4, turn % 4) for turn in range(8)]
    )


def swap_add(value, core):
    keep = lax.dynamic_index_in_dim(value, core, 0, keepdims=False)
    give = lax.dynamic_index_in_dim(value, 1 - core, 0, keepdims=False)
    return (keep.astype(wide) + swap_core(give).astype(wide)).astype(low)


def shift_to(value, dx, dy):
    pairs = [(x * 4 + y, ((x + dx) % 2) * 4 + (y + dy) % 4) for x in range(2) for y in range(4)]
    return lax.ppermute(value, SHARD, pairs)


def scatter_sum(total, value, place, offsets):
    for dx, dy in offsets:
        target = ((place // 4 + dx) % 2) * 4 + (place + dy) % 4
        block = lax.dynamic_index_in_dim(value, target, 0, keepdims=False)
        total = total + shift_to(block, dx, dy).astype(wide)
    return total


def gather_small(value, place):
    for bit in (1, 2, 4):
        other = lax.ppermute(value, SHARD, [(k, k ^ bit) for k in range(8)])
        upper = (place // bit) % 2 == 1
        value = jnp.concatenate(
            [jnp.where(upper, other, value), jnp.where(upper, value, other)], axis=0
        )
    return value


def join_rows(mine, other, core):
    first = jnp.where(core == 0, mine, other)
    second = jnp.where(core == 0, other, mine)
    return jnp.concatenate([first, second], axis=1).reshape(-1, mine.shape[-1])


def core_half(value, core):
    keep = lax.dynamic_index_in_dim(value, core, 1, keepdims=False)
    give = lax.dynamic_index_in_dim(value, 1 - core, 1, keepdims=False).astype(low)
    return (keep.astype(wide) + swap_core(give).astype(wide)).astype(low)


def on_device(
    latents, cond, cotangent, w_qkv, bias_qv, w_proj, b_proj, w_fc1, b_fc1, w_fc2, b_fc2, w_ada, b_ada
):
    stream_low = latents[0]
    upstream_low = cotangent[0]
    rows, features = stream_low.shape
    shards = 8
    length = shards * rows
    own = features // shards
    half = own // 2
    units = w_fc2.shape[0]
    ada_width = w_ada.shape[1]
    ada_rows = ada_width // LANES
    place = lax.axis_index(SHARD)
    core = lax.axis_index("core")

    cond_value = cond.astype(wide)
    cond_silu, silu_pull = jax.vjp(silu, cond_value)
    cond_low = cond_silu.astype(low)
    cond_own = lax.dynamic_slice_in_dim(cond_low, place * own, own, 1)
    mod_part = mul(cond_own, w_ada)[0]
    blocks = jnp.arange(shards)[:, None] == place
    mod_part = mod_part + jnp.where(blocks, b_ada.astype(wide)[None, :], 0.0).reshape(ada_width)
    small = jnp.concatenate([mod_part.astype(low), bias_qv, b_proj, b_fc2])

    def halved(value):
        return lax.dynamic_slice_in_dim(value, core * half, half, 0)

    qkv_mine = halved(w_qkv)

    def qkv_part(part):
        return jnp.stack(
            [
                qkv_mine[:, part * features + k * own : part * features + (k + 1) * own]
                for k in range(shards)
            ]
        )

    first_sent = jnp.concatenate(
        [
            copies(stream_low),
            jnp.concatenate([qkv_part(0), qkv_part(1)], axis=1),
            jnp.concatenate([qkv_part(2), copies(as_rows(small, half))], axis=1),
        ],
        axis=2,
    )
    first_got = exchange(first_sent)
    weights_sent = jnp.concatenate(
        [
            halved(w_fc1).reshape(half, shards, units).transpose(1, 0, 2),
            copies(halved(w_proj)),
        ],
        axis=2,
    )
    weights_sent, first_got = lax.optimization_barrier((weights_sent, first_got))
    weights_got = exchange(weights_sent)
    near = first_got[:, :, features : features + own]
    far = first_got[:, :, features + own :]
    qkv_got = jnp.concatenate([near[:, :half], near[:, half:], far[:, :half]], axis=2)
    wq = join_rows(qkv_got, swap_core(qkv_got), core)
    small_got = far[:, half:].astype(wide)
    modulation = jnp.sum(small_got[:, :ada_rows], axis=0).reshape(1, ada_width)
    shift_first, scale_first, gate_first, shift_second, scale_second, gate_second = jnp.split(
        modulation, 6, axis=1
    )
    at = ada_rows
    bias_wide = small_got[:, at : at + 2].reshape(1, 2 * features)
    proj_bias = small_got[:, at + 2].reshape(1, features)
    second_bias = small_got[:, at + 3].reshape(1, features)

    query_bias = lax.dynamic_slice_in_dim(bias_wide, place * own, own, 1)
    value_bias = lax.dynamic_slice_in_dim(bias_wide, features + place * own, own, 1)
    attend_in, queries, keyset, valueset, mixed, log_total = attend(
        first_got, wq, scale_first, shift_first, query_bias, value_bias
    )
    mixed, weights_got = lax.optimization_barrier((mixed, weights_got))
    mixed_got = exchange(
        jnp.concatenate([mixed.reshape(shards, rows, own), copies(upstream_low)], axis=2)
    )
    weights_other = swap_core(weights_got)
    w1 = join_rows(weights_got[:, :, :units], weights_other[:, :, :units], core)
    wp = join_rows(weights_got[:, :, units:], weights_other[:, :, units:], core)
    mixed_tok = mixed_got[:, :, :own].transpose(1, 0, 2).reshape(rows, features)
    upstream_all = mixed_got[:, :, own:].reshape(length, features)
    branch = mul(mixed_tok, wp) + proj_bias
    stream = stream_low.astype(wide)
    middle = stream + gate_first * branch
    norm_second, inverse_second = normalize(middle)
    feed_in = (norm_second * (1.0 + scale_second) + shift_second).astype(low)
    feed_got = exchange(copies(feed_in))
    (
        feed_part,
        second_low,
        active,
        grad_hidden,
        grad_branch_second,
        gate_sums,
        second_bias_sums,
        hidden_sums,
    ) = gated(feed_got, w1, b_fc1.astype(wide)[None, :], w_fc2, mixed_got, gate_second)
    feed_back = exchange(feed_part)
    term_first, term_second = weights_back(
        feed_got.reshape(length, features), grad_hidden, active, grad_branch_second, shards
    )
    term_first = swap_add(term_first, core)
    feed_back, term_first, term_second = lax.optimization_barrier(
        (feed_back, term_first, term_second)
    )
    grad_feed = jnp.sum(feed_back.astype(wide), axis=0)

    upstream = upstream_low.astype(wide)
    grad_gate_second = gate_sums[0] + second_bias[0] * jnp.sum(upstream, axis=0)
    grad_scale_second = jnp.sum(grad_feed * norm_second, axis=0)
    grad_shift_second = jnp.sum(grad_feed, axis=0)
    grad_middle = upstream + normalize_back(
        norm_second, inverse_second, grad_feed * (1.0 + scale_second)
    )
    grad_gate_first = jnp.sum(grad_middle * branch, axis=0)
    grad_branch = (grad_middle * gate_first).astype(low)
    grad_mixed_tok = mul_t(grad_branch, wp).astype(low)
    grad_mixed = exchange(grad_mixed_tok.reshape(rows, shards, own).transpose(1, 0, 2))
    term_proj = proj_back(mixed_got, grad_branch, own)
    term_proj, grad_mixed = lax.optimization_barrier((term_proj, grad_mixed))
    pair_got = exchange(jnp.concatenate([term_first, swap_add(term_proj, core)], axis=2))
    attend_part, term_qkv, attend_sums, packed_sums = attend_back(
        queries, grad_mixed.reshape(length, own), log_total, keyset, valueset, wq, attend_in, first_got
    )
    attend_part, term_qkv, attend_sums, packed_sums, pair_got = lax.optimization_barrier(
        (attend_part, term_qkv, attend_sums, packed_sums, pair_got)
    )
    packed_sums = packed_sums[0]
    grad_shift_first = attend_sums[0]
    grad_scale_first = attend_sums[1]
    mod_terms = jnp.concatenate(
        [
            grad_shift_first,
            grad_scale_first,
            grad_gate_first,
            grad_shift_second,
            grad_scale_second,
            grad_gate_second,
            jnp.sum(grad_branch.astype(wide), axis=0),
            packed_sums[:own],
            packed_sums[2 * own :],
        ]
    ).astype(low)
    term_qkv = core_half(term_qkv.reshape(shards, 2, half, 3 * own), core)
    last_sent = jnp.concatenate(
        [
            attend_part,
            jnp.concatenate([term_qkv[:, :, :own], term_qkv[:, :, own : 2 * own]], axis=1),
            jnp.concatenate(
                [term_qkv[:, :, 2 * own :], copies(as_rows(mod_terms, half))], axis=1
            ),
        ],
        axis=2,
    )
    last_got = exchange(last_sent)
    term_proj = jnp.sum(pair_got[:, :, units:].astype(wide), axis=0).astype(low)
    term_second = swap_add(term_second.reshape(2, units // 2, features), core)
    piece = units // 2 // shards
    term_second = term_second.reshape(shards, piece, features)
    fold = features // 2
    early = jnp.concatenate(
        [
            pair_got[:, :, :units],
            jnp.concatenate([term_second[:, :, :fold], term_second[:, :, fold:]], axis=1),
            term_proj.reshape(half, shards, own).transpose(1, 0, 2),
        ],
        axis=2,
    )
    chip_x, chip_z = lax.axis_index("xl"), lax.axis_index("z")
    early_got = gather_chips(reduce_chips(early, chip_x, chip_z))
    last_got, early_got = lax.optimization_barrier((last_got, early_got))
    early_other = swap_core(early_got)
    second_low, last_got = lax.optimization_barrier((second_low, last_got))
    second_own = lax.dynamic_index_in_dim(second_low, place, 0, keepdims=False).astype(wide)
    second_near = scatter_sum(second_own, second_low, place, ((0, 1), (0, 3), (0, 2)))
    grad_attend = jnp.sum(last_got[:, :, :features].astype(wide), axis=0)
    near = last_got[:, :, features : features + own]
    far = last_got[:, :, features + own :]
    term_qkv = jnp.concatenate([near[:, :half], near[:, half:], far[:, :half]], axis=2)
    mod_got = far[:, half:].astype(wide)
    head_rows = ada_rows + features // LANES
    mod_sums = jnp.sum(mod_got[:, :head_rows], axis=0)
    bias_qv_all = jnp.concatenate(
        [mod_got[:, head_rows].reshape(features), mod_got[:, head_rows + 1].reshape(features)]
    )
    norm_own, inverse_own = normalize(stream)
    grad_stream = grad_middle + normalize_back(
        norm_own, inverse_own, grad_attend * (1.0 + scale_first)
    )
    grad_latents = grad_stream.astype(low)

    grad_modulation = mod_sums[:ada_rows].reshape(ada_width)
    proj_bias_term = lax.dynamic_slice_in_dim(mod_sums, ada_rows + place, 1, 0)
    cond_term = jnp.sum(w_ada.astype(wide) * grad_modulation[None, :], axis=1)
    cond_total = gather_small(cond_term[None], place).reshape(1, features)
    grad_cond = silu_pull(cond_total)[0]

    second_bias_sums = second_bias_sums[0]
    rep_terms = jnp.concatenate(
        [
            mod_sums[:ada_rows],
            cond_own.astype(wide),
            proj_bias_term,
            hidden_sums.reshape(units // LANES, LANES),
            lax.dynamic_slice_in_dim(second_bias_sums, place * own, own, 0)[None],
            lax.dynamic_slice_in_dim(bias_qv_all, place * 2 * own, 2 * own, 0).reshape(2, own),
        ]
    )
    rep_terms = jnp.pad(rep_terms, ((0, half - rep_terms.shape[0]), (0, 0))).astype(low)
    rep_terms = jnp.concatenate([rep_terms, swap_core(rep_terms)], axis=1)

    rep_sent = jnp.concatenate([term_qkv, copies(rep_terms)], axis=2)
    rep_got = exchange(rep_sent, CHIPS)
    width = 3 * own
    owned = jnp.sum(rep_got[:, :, :width].astype(wide), axis=0).astype(low)
    rep_small = jnp.concatenate(
        [rep_got[:, :, width : width + own], rep_got[:, :, width + own :]], axis=0
    )
    grad_w_ada = t_mul(
        rep_small[:, ada_rows], rep_small[:, :ada_rows].reshape(2 * shards, ada_width)
    )
    rep_sums = jnp.sum(rep_small.astype(wide), axis=0)
    ada_own = ada_rows // shards
    grad_b_ada = lax.dynamic_slice_in_dim(rep_sums, place * ada_own, ada_own, 0)
    grad_b_ada = grad_b_ada.reshape(ada_width // shards)
    at = ada_rows + 1
    grad_b_proj = rep_sums[at]
    at += 1
    grad_b_fc1 = rep_sums[at : at + units // LANES].reshape(units)
    at += units // LANES
    grad_b_fc2 = rep_sums[at]
    grad_bias_qv = rep_sums[at + 1 : at + 3].reshape(2 * own)

    owned, second_near = lax.optimization_barrier((owned, second_near))
    whole_mine = exchange(copies(owned), CHIPS)
    branch_second = (
        scatter_sum(second_near, second_low, place, ((1, 0), (1, 1), (1, 3), (1, 2)))
        + second_bias
    )
    output = (middle + gate_second * branch_second).astype(low)
    whole_mine, grad_w_ada = lax.optimization_barrier((whole_mine, grad_w_ada))
    grad_w_fc1, grad_w_fc2, grad_w_qkv, grad_w_proj = unpack(
        jnp.stack([core, chip_x, chip_z]).astype(jnp.int32),
        early_got,
        early_other,
        whole_mine,
        swap_core(whole_mine),
        units,
        features,
    )

    return (
        output[None],
        grad_latents[None],
        grad_cond,
        grad_w_qkv,
        grad_bias_qv,
        grad_w_proj,
        grad_b_proj,
        grad_w_fc1,
        grad_b_fc1,
        grad_w_fc2,
        grad_b_fc2,
        grad_w_ada,
        grad_b_ada,
    )


def solution(mesh):
    fine = Mesh(mesh.devices.reshape(2, 4, 2, 2, 4), REP + SHARD)
    tokens = P(REP, SHARD, None)
    matrix = P(SHARD, None)
    vector = P(SHARD)
    params = (matrix, vector) * 5
    return jax.shard_map(
        on_device,
        mesh=fine,
        in_specs=(tokens, P(REP, None), tokens) + params,
        out_specs=(tokens, tokens, P(REP, None)) + params,
        check_vma=False,
    )
```

```python
import jax
import jax.numpy as jnp
from jax import lax
from jax.experimental import pallas as pl
from jax.experimental.pallas import tpu as pltpu
from jax.sharding import Mesh, PartitionSpec as P

HEAD = 64
SHARD = ("xh", "y")
CHIPS = ("xl", "z")
REP = ("xl", "z", "core")
LANES = 128
QUERY_BLOCK = 256
SCALE = HEAD ** (-0.5)

epsilon = 1e-06
highest = lax.Precision.HIGHEST
low = jnp.bfloat16
wide = jnp.float32


def swap_core(value):
    return lax.ppermute(value, "core", [(0, 1), (1, 0)])


def exchange(value, axes=SHARD):
    return lax.all_to_all(value, axes, 0, 0, tiled=True)


def copies(value):
    return jnp.broadcast_to(value[None], (8,) + value.shape)


def as_rows(value, count):
    rows = value.reshape(-1, LANES)
    return jnp.pad(rows, ((0, count - rows.shape[0]), (0, 0)))


def normalize(values):
    centered = values - jnp.mean(values, axis=-1, keepdims=True)
    inverse = lax.rsqrt(jnp.mean(centered * centered, axis=-1, keepdims=True) + epsilon)
    return centered * inverse, inverse


def normalize_back(norm, inverse, grad):
    return inverse * (
        grad
        - jnp.mean(grad, axis=-1, keepdims=True)
        - norm * jnp.mean(grad * norm, axis=-1, keepdims=True)
    )


def silu(values):
    return values / (1.0 + jnp.exp(-values))


def gelu_tanh(values):
    return (
        0.5
        * values
        * (1.0 + jnp.tanh(0.7978845608028654 * (values + 0.044715 * values * values * values)))
    )


def mul(left, right):
    return lax.dot_general(left, right, (((1,), (0,)), ((), ())), preferred_element_type=wide)


def mul_t(left, right):
    return lax.dot_general(left, right, (((1,), (1,)), ((), ())), preferred_element_type=wide)


def t_mul(left, right):
    return lax.dot_general(left, right, (((0,), (0,)), ((), ())), preferred_element_type=wide)


def head_of(value, index):
    lane = lax.broadcasted_iota(jnp.int32, value.shape, 1)
    return jnp.where((lane >= HEAD) == (index == 1), value, jnp.zeros_like(value))


def attend_kernel(
    got_ref, wq_ref, scale_ref, shift_ref, qb_ref, vb_ref, in_ref, q_ref, k_ref, v_ref, mixed_ref, log_ref
):
    count, rows, _ = got_ref.shape
    features = scale_ref.shape[1]
    own = qb_ref.shape[1]
    gain = 1.0 + scale_ref[...]
    for block in range(count):
        at = pl.ds(block * rows, rows)
        norm, _ = normalize(got_ref[block, :, 0:features].astype(wide))
        attend_in = (norm * gain + shift_ref[...]).astype(low)
        in_ref[at, :] = attend_in
        packed = mul(attend_in, wq_ref[...])
        q_ref[at, :] = (packed[:, :own] + qb_ref[...]).astype(low)
        k_ref[at, :] = packed[:, own : 2 * own].astype(low)
        v_ref[at, :] = (packed[:, 2 * own :] + vb_ref[...]).astype(low)
    for block in range(count * rows // QUERY_BLOCK):
        at = pl.ds(block * QUERY_BLOCK, QUERY_BLOCK)
        total = None
        logs = None
        for index in range(2):
            scores = mul_t(head_of(q_ref[at, :], index), k_ref[...]) * SCALE
            peak = jnp.max(scores, axis=1, keepdims=True)
            powered = jnp.exp(scores - peak)
            row_total = jnp.sum(powered, axis=1, keepdims=True)
            probs = (powered / row_total).astype(low)
            part = mul(probs, head_of(v_ref[...], index))
            log = head_of(jnp.broadcast_to(peak + jnp.log(row_total), part.shape), index)
            total = part if total is None else total + part
            logs = log if logs is None else logs + log
        mixed_ref[at, :] = total.astype(low)
        log_ref[at, :] = logs


def attend(got, wq, scale, shift, query_bias, value_bias):
    length, features = wq.shape
    length = got.shape[0] * got.shape[1]
    features = wq.shape[0]
    own = wq.shape[1] // 3
    head = jax.ShapeDtypeStruct((length, own), low)
    return pl.pallas_call(
        attend_kernel,
        out_shape=[
            jax.ShapeDtypeStruct((length, features), low),
            head,
            head,
            head,
            head,
            jax.ShapeDtypeStruct((length, own), wide),
        ],
        compiler_params=pltpu.CompilerParams(vmem_limit_bytes=40 * 1024 * 1024),
        cost_estimate=pl.CostEstimate(
            flops=16 * length * length * own,
            transcendentals=2 * length * length,
            bytes_accessed=8 * length * features,
        ),
        name="attend",
    )(got, wq, scale, shift, query_bias, value_bias)


def attend_back_kernel(
    q_ref, g_ref, log_ref, k_ref, v_ref, wq_ref, in_ref, got_ref,
    part_ref, term_ref, sums_ref, packed_sums_ref, packed, key_acc, value_acc,
):
    length, own = q_ref.shape
    count, rows, _ = got_ref.shape
    features = in_ref.shape[1]
    for block in range(length // QUERY_BLOCK):
        at = pl.ds(block * QUERY_BLOCK, QUERY_BLOCK)
        grad_query = None
        for index in range(2):
            query = head_of(q_ref[at, :], index)
            grad = head_of(g_ref[at, :], index)
            log = log_ref[at, index * HEAD : index * HEAD + 1]
            probs = jnp.exp(mul_t(query, k_ref[...]) * SCALE - log)
            grad_probs = mul_t(grad, v_ref[...])
            delta = jnp.sum(probs * grad_probs, axis=1, keepdims=True)
            grad_scores = (probs * (grad_probs - delta)).astype(low)
            part = mul(grad_scores, head_of(k_ref[...], index))
            grad_query = part if grad_query is None else grad_query + part
            key_part = t_mul(grad_scores, query)
            value_part = t_mul(probs.astype(low), grad)
            if block == 0 and index == 0:
                key_acc[...] = key_part
                value_acc[...] = value_part
            else:
                key_acc[...] += key_part
                value_acc[...] += value_part
        packed[at, 0:own] = (grad_query * SCALE).astype(low)
    packed[:, own : 2 * own] = (key_acc[...] * SCALE).astype(low)
    packed[:, 2 * own : 3 * own] = value_acc[...].astype(low)
    packed_sums_ref[...] = jnp.sum(packed[...].astype(wide), axis=0, keepdims=True)
    shift_sum = None
    scale_sum = None
    for block in range(count):
        at = pl.ds(block * rows, rows)
        part = mul_t(packed[at, :], wq_ref[...])
        norm, _ = normalize(got_ref[block, :, 0:features].astype(wide))
        part_ref[block] = part.astype(low)
        one = jnp.sum(part, axis=0, keepdims=True)
        two = jnp.sum(part * norm, axis=0, keepdims=True)
        shift_sum = one if shift_sum is None else shift_sum + one
        scale_sum = two if scale_sum is None else scale_sum + two
    sums_ref[0:1, :] = shift_sum
    sums_ref[1:2, :] = scale_sum
    for block in range(features // QUERY_BLOCK):
        at = pl.ds(block * QUERY_BLOCK, QUERY_BLOCK)
        term_ref[at, :] = t_mul(in_ref[:, at], packed[...]).astype(low)


def attend_back(queries, grad_mixed, logs, keyset, valueset, wq, attend_in, got):
    length, own = queries.shape
    features = attend_in.shape[1]
    count, rows, _ = got.shape
    return pl.pallas_call(
        attend_back_kernel,
        out_shape=[
            jax.ShapeDtypeStruct((count, rows, features), low),
            jax.ShapeDtypeStruct((features, 3 * own), low),
            jax.ShapeDtypeStruct((2, features), wide),
            jax.ShapeDtypeStruct((1, 3 * own), wide),
        ],
        scratch_shapes=[
            pltpu.VMEM((length, 3 * own), low),
            pltpu.VMEM((length, own), wide),
            pltpu.VMEM((length, own), wide),
        ],
        compiler_params=pltpu.CompilerParams(vmem_limit_bytes=40 * 1024 * 1024),
        cost_estimate=pl.CostEstimate(
            flops=32 * length * length * own,
            transcendentals=2 * length * length,
            bytes_accessed=12 * length * features,
        ),
        name="attend_back",
    )(queries, grad_mixed, logs, keyset, valueset, wq, attend_in, got)


def gated_kernel(
    feed_ref, w1_ref, b1_ref, w2_ref, got_ref, gate_ref,
    grad_ref, second_ref, active_ref, hidden_ref, branch_ref, gate_sum, branch_sum, hidden_sum,
):
    count, rows, features = feed_ref.shape
    units = w1_ref.shape[1]
    skip = got_ref.shape[2] - features
    sums = [None, None, None]

    def add(slot, value):
        one = jnp.sum(value, axis=0, keepdims=True)
        sums[slot] = one if sums[slot] is None else sums[slot] + one

    pair = 2
    for block in range(count // pair):
        at = pl.ds(block * pair * rows, pair * rows)
        both = slice(block * pair, (block + 1) * pair)
        feed = feed_ref[both].reshape(pair * rows, features)
        upstream = got_ref[both, :, skip:].reshape(pair * rows, features).astype(wide)
        hidden = mul(feed, w1_ref[...]) + b1_ref[...]
        square = hidden * hidden
        bent = jnp.tanh(0.7978845608028654 * (hidden + 0.044715 * square * hidden))
        rise = 0.5 * (1.0 + bent)
        slope = rise + 0.5 * hidden * (1.0 - bent * bent) * (
            0.7978845608028654 * (1.0 + 3.0 * 0.044715 * square)
        )
        active = (hidden * rise).astype(low)
        active_ref[at, :] = active
        second = mul(active, w2_ref[...])
        second_ref[both] = second.astype(low).reshape(pair, rows, features)
        add(0, upstream * second)
        grad_branch = (upstream * gate_ref[...]).astype(low)
        branch_ref[at, :] = grad_branch
        add(1, grad_branch.astype(wide))
        grad_hidden = (mul_t(grad_branch, w2_ref[...]) * slope).astype(low)
        hidden_ref[at, :] = grad_hidden
        add(2, grad_hidden.astype(wide))
        grad_feed = mul_t(grad_hidden, w1_ref[...]).astype(low)
        grad_ref[both] = grad_feed.reshape(pair, rows, features)
    gate_sum[...] = sums[0]
    branch_sum[...] = sums[1]
    hidden_sum[...] = sums[2]


def gated(feed, w1, b1, w2, got, gate):
    count, rows, features = feed.shape
    units = w1.shape[1]
    length = count * rows
    return pl.pallas_call(
        gated_kernel,
        out_shape=[
            pltpu.HBM((count, rows, features), low),
            pltpu.HBM((count, rows, features), low),
            pltpu.HBM((length, units), low),
            pltpu.HBM((length, units), low),
            pltpu.HBM((length, features), low),
            jax.ShapeDtypeStruct((1, features), wide),
            jax.ShapeDtypeStruct((1, features), wide),
            jax.ShapeDtypeStruct((1, units), wide),
        ],
        compiler_params=pltpu.CompilerParams(vmem_limit_bytes=40 * 1024 * 1024),
        cost_estimate=pl.CostEstimate(
            flops=8 * length * features * units,
            transcendentals=length * units,
            bytes_accessed=16 * length * features,
        ),
        name="gated",
    )(feed, w1, b1, w2, got, gate)


def weights_kernel(feed_ref, hidden_ref, active_ref, branch_ref, first_ref, second_ref):
    features = feed_ref.shape[1]
    units = hidden_ref.shape[1]
    own = 2 * first_ref.shape[2]
    half = own // 2
    for block in range(features // QUERY_BLOCK):
        at = pl.ds(block * QUERY_BLOCK, QUERY_BLOCK)
        term = t_mul(feed_ref[:, at], hidden_ref[...]).astype(low)
        for piece in range(QUERY_BLOCK // own):
            target = block * (QUERY_BLOCK // own) + piece
            first_ref[0, target] = term[piece * own : piece * own + half]
            first_ref[1, target] = term[piece * own + half : (piece + 1) * own]
    for block in range(units // QUERY_BLOCK):
        at = pl.ds(block * QUERY_BLOCK, QUERY_BLOCK)
        second_ref[at, :] = t_mul(active_ref[:, at], branch_ref[...]).astype(low)


def weights_back(feed, grad_hidden, active, grad_branch, shards):
    length, features = feed.shape
    units = active.shape[1]
    return pl.pallas_call(
        weights_kernel,
        out_shape=[
            jax.ShapeDtypeStruct((2, shards, features // shards // 2, units), low),
            jax.ShapeDtypeStruct((units, features), low),
        ],
        compiler_params=pltpu.CompilerParams(vmem_limit_bytes=40 * 1024 * 1024),
        cost_estimate=pl.CostEstimate(
            flops=4 * length * features * units,
            transcendentals=0,
            bytes_accessed=10 * length * features,
        ),
        name="weights_back",
    )(feed, grad_hidden, active, grad_branch)


def proj_kernel(core_ref, got_ref, got_other_ref, grad_ref, grad_other_ref, out_ref):
    count, half, _ = out_ref.shape
    for block in range(count):
        term = t_mul(got_ref[block, :, 0 : 2 * half], grad_ref[...])
        term = term + t_mul(got_other_ref[block], grad_other_ref[...])
        out_ref[block] = jnp.where(core_ref[0] == 0, term[:half], term[half:]).astype(low)


def proj_back(core, got, got_other, grad, grad_other):
    count, rows, own = got_other.shape
    features = grad.shape[1]
    return pl.pallas_call(
        proj_kernel,
        in_specs=[pl.BlockSpec(memory_space=pltpu.SMEM)]
        + [pl.BlockSpec(memory_space=pltpu.VMEM)] * 4,
        out_shape=jax.ShapeDtypeStruct((count, own // 2, features), low),
        compiler_params=pltpu.CompilerParams(vmem_limit_bytes=40 * 1024 * 1024),
        name="proj_back",
    )(core, got, got_other, grad, grad_other)


def unpack_kernel(
    core_ref, mine_ref, other_ref, mine_qkv_ref, other_qkv_ref, first_ref, second_ref, qkv_ref, proj_ref
):
    count, half, _ = mine_ref.shape
    units = first_ref.shape[1] // count
    features = second_ref.shape[1]
    fold = features // 2
    own = proj_ref.shape[1] // count
    piece = half // 2
    for side in range(2):
        rows = pl.ds(side * half, half)
        here = core_ref[0] == side
        for block in range(count):
            value = jnp.where(here, mine_ref[block], other_ref[block]).astype(wide)
            first_ref[rows, block * units : (block + 1) * units] = value[:, :units]
            at = pl.ds((side * count + block) * piece, piece)
            second_ref[at, :fold] = value[:piece, units : units + fold]
            second_ref[at, fold:] = value[piece:, units : units + fold]
            proj_ref[rows, block * own : (block + 1) * own] = value[:, units + fold :]
            value = jnp.where(here, mine_qkv_ref[block], other_qkv_ref[block]).astype(wide)
            for part in range(3):
                lane = part * features + block * own
                qkv_ref[rows, lane : lane + own] = value[:, part * own : (part + 1) * own]


def unpack(core, mine, other, mine_qkv, other_qkv, units, features):
    count, half, _ = mine.shape
    return pl.pallas_call(
        unpack_kernel,
        in_specs=[pl.BlockSpec(memory_space=pltpu.SMEM)]
        + [pl.BlockSpec(memory_space=pltpu.VMEM)] * 4,
        out_shape=[
            jax.ShapeDtypeStruct((2 * half, count * units), wide),
            jax.ShapeDtypeStruct((units, features), wide),
            jax.ShapeDtypeStruct((2 * half, 3 * features), wide),
            jax.ShapeDtypeStruct((2 * half, features), wide),
        ],
        compiler_params=pltpu.CompilerParams(vmem_limit_bytes=40 * 1024 * 1024),
        name="unpack",
    )(core, mine, other, mine_qkv, other_qkv)


def swap_add(value, core):
    keep = lax.dynamic_index_in_dim(value, core, 0, keepdims=False)
    give = lax.dynamic_index_in_dim(value, 1 - core, 0, keepdims=False)
    return (keep.astype(wide) + swap_core(give).astype(wide)).astype(low)


def shift_to(value, dx, dy):
    pairs = [(x * 4 + y, ((x + dx) % 2) * 4 + (y + dy) % 4) for x in range(2) for y in range(4)]
    return lax.ppermute(value, SHARD, pairs)


def scatter_sum(total, value, place, offsets):
    for dx, dy in offsets:
        target = ((place // 4 + dx) % 2) * 4 + (place + dy) % 4
        block = lax.dynamic_index_in_dim(value, target, 0, keepdims=False)
        total = total + shift_to(block, dx, dy).astype(wide)
    return total


def gather_small(value, place):
    for bit in (1, 2, 4):
        other = lax.ppermute(value, SHARD, [(k, k ^ bit) for k in range(8)])
        upper = (place // bit) % 2 == 1
        value = jnp.concatenate(
            [jnp.where(upper, other, value), jnp.where(upper, value, other)], axis=0
        )
    return value


def join_rows(mine, other, core):
    first = jnp.where(core == 0, mine, other)
    second = jnp.where(core == 0, other, mine)
    return jnp.concatenate([first, second], axis=1).reshape(-1, mine.shape[-1])


def core_half(value, core):
    keep = lax.dynamic_index_in_dim(value, core, 1, keepdims=False)
    give = lax.dynamic_index_in_dim(value, 1 - core, 1, keepdims=False).astype(low)
    return (keep.astype(wide) + swap_core(give).astype(wide)).astype(low)


def on_device(
    latents, cond, cotangent, w_qkv, bias_qv, w_proj, b_proj, w_fc1, b_fc1, w_fc2, b_fc2, w_ada, b_ada
):
    stream_low = latents[0]
    upstream_low = cotangent[0]
    rows, features = stream_low.shape
    shards = 8
    length = shards * rows
    own = features // shards
    half = own // 2
    units = w_fc2.shape[0]
    ada_width = w_ada.shape[1]
    ada_rows = ada_width // LANES
    place = lax.axis_index(SHARD)
    core = lax.axis_index("core")

    cond_value = cond.astype(wide)
    cond_silu, silu_pull = jax.vjp(silu, cond_value)
    cond_low = cond_silu.astype(low)
    cond_own = lax.dynamic_slice_in_dim(cond_low, place * own, own, 1)
    mod_part = mul(cond_own, w_ada)[0]
    blocks = jnp.arange(shards)[:, None] == place
    mod_part = mod_part + jnp.where(blocks, b_ada.astype(wide)[None, :], 0.0).reshape(ada_width)
    small = jnp.concatenate([mod_part.astype(low), bias_qv, b_proj, b_fc2])

    def halved(value):
        return lax.dynamic_slice_in_dim(value, core * half, half, 0)

    qkv_mine = halved(w_qkv)

    def qkv_part(part):
        return jnp.stack(
            [
                qkv_mine[:, part * features + k * own : part * features + (k + 1) * own]
                for k in range(shards)
            ]
        )

    first_sent = jnp.concatenate(
        [
            copies(stream_low),
            jnp.concatenate([qkv_part(0), qkv_part(1)], axis=1),
            jnp.concatenate([qkv_part(2), copies(as_rows(small, half))], axis=1),
        ],
        axis=2,
    )
    first_got = exchange(first_sent)
    weights_sent = jnp.concatenate(
        [
            halved(w_fc1).reshape(half, shards, units).transpose(1, 0, 2),
            copies(halved(w_proj)),
        ],
        axis=2,
    )
    weights_sent, first_got = lax.optimization_barrier((weights_sent, first_got))
    weights_got = exchange(weights_sent)
    near = first_got[:, :, features : features + own]
    far = first_got[:, :, features + own :]
    qkv_got = jnp.concatenate([near[:, :half], near[:, half:], far[:, :half]], axis=2)
    wq = join_rows(qkv_got, swap_core(qkv_got), core)
    small_got = far[:, half:].astype(wide)
    modulation = jnp.sum(small_got[:, :ada_rows], axis=0).reshape(1, ada_width)
    shift_first, scale_first, gate_first, shift_second, scale_second, gate_second = jnp.split(
        modulation, 6, axis=1
    )
    at = ada_rows
    bias_wide = small_got[:, at : at + 2].reshape(1, 2 * features)
    proj_bias = small_got[:, at + 2].reshape(1, features)
    second_bias = small_got[:, at + 3].reshape(1, features)

    query_bias = lax.dynamic_slice_in_dim(bias_wide, place * own, own, 1)
    value_bias = lax.dynamic_slice_in_dim(bias_wide, features + place * own, own, 1)
    attend_in, queries, keyset, valueset, mixed, log_total = attend(
        first_got, wq, scale_first, shift_first, query_bias, value_bias
    )
    mixed, weights_got = lax.optimization_barrier((mixed, weights_got))
    mixed_got = exchange(
        jnp.concatenate([mixed.reshape(shards, rows, own), copies(upstream_low)], axis=2)
    )
    weights_other = swap_core(weights_got)
    w1 = join_rows(weights_got[:, :, :units], weights_other[:, :, :units], core)
    wp = join_rows(weights_got[:, :, units:], weights_other[:, :, units:], core)
    mixed_other = swap_core(mixed_got[:, :, :own])
    mixed_tok = mixed_got[:, :, :own].transpose(1, 0, 2).reshape(rows, features)
    upstream_all = mixed_got[:, :, own:].reshape(length, features)
    branch = mul(mixed_tok, wp) + proj_bias
    stream = stream_low.astype(wide)
    middle = stream + gate_first * branch
    norm_second, inverse_second = normalize(middle)
    feed_in = (norm_second * (1.0 + scale_second) + shift_second).astype(low)
    feed_got = exchange(copies(feed_in))
    (
        feed_part,
        second_low,
        active,
        grad_hidden,
        grad_branch_second,
        gate_sums,
        second_bias_sums,
        hidden_sums,
    ) = gated(feed_got, w1, b_fc1.astype(wide)[None, :], w_fc2, mixed_got, gate_second)
    feed_back = exchange(feed_part)
    term_first, term_second = weights_back(
        feed_got.reshape(length, features), grad_hidden, active, grad_branch_second, shards
    )
    term_first = swap_add(term_first, core)
    feed_back, term_first, term_second = lax.optimization_barrier(
        (feed_back, term_first, term_second)
    )
    grad_feed = jnp.sum(feed_back.astype(wide), axis=0)

    upstream = upstream_low.astype(wide)
    grad_gate_second = gate_sums[0] + second_bias[0] * jnp.sum(upstream, axis=0)
    grad_scale_second = jnp.sum(grad_feed * norm_second, axis=0)
    grad_shift_second = jnp.sum(grad_feed, axis=0)
    grad_middle = upstream + normalize_back(
        norm_second, inverse_second, grad_feed * (1.0 + scale_second)
    )
    grad_gate_first = jnp.sum(grad_middle * branch, axis=0)
    grad_branch = (grad_middle * gate_first).astype(low)
    grad_mixed_tok = mul_t(grad_branch, wp).astype(low)
    grad_mixed = exchange(grad_mixed_tok.reshape(rows, shards, own).transpose(1, 0, 2))
    term_proj = proj_back(
        core.astype(jnp.int32)[None], mixed_got, mixed_other, grad_branch, swap_core(grad_branch)
    )
    term_proj, grad_mixed = lax.optimization_barrier((term_proj, grad_mixed))
    pair_got = exchange(jnp.concatenate([term_first, term_proj], axis=2))
    attend_part, term_qkv, attend_sums, packed_sums = attend_back(
        queries, grad_mixed.reshape(length, own), log_total, keyset, valueset, wq, attend_in, first_got
    )
    attend_part, term_qkv, attend_sums, packed_sums, pair_got = lax.optimization_barrier(
        (attend_part, term_qkv, attend_sums, packed_sums, pair_got)
    )
    packed_sums = packed_sums[0]
    grad_shift_first = attend_sums[0]
    grad_scale_first = attend_sums[1]
    mod_terms = jnp.concatenate(
        [
            grad_shift_first,
            grad_scale_first,
            grad_gate_first,
            grad_shift_second,
            grad_scale_second,
            grad_gate_second,
            jnp.sum(grad_branch.astype(wide), axis=0),
            packed_sums[:own],
            packed_sums[2 * own :],
        ]
    ).astype(low)
    term_qkv = core_half(term_qkv.reshape(shards, 2, half, 3 * own), core)
    last_sent = jnp.concatenate(
        [
            attend_part,
            jnp.concatenate([term_qkv[:, :, :own], term_qkv[:, :, own : 2 * own]], axis=1),
            jnp.concatenate(
                [term_qkv[:, :, 2 * own :], copies(as_rows(mod_terms, half))], axis=1
            ),
        ],
        axis=2,
    )
    last_got = exchange(last_sent)
    term_proj = jnp.sum(pair_got[:, :, units:].astype(wide), axis=0).astype(low)
    term_second = swap_add(term_second.reshape(2, units // 2, features), core)
    piece = units // 2 // shards
    term_second = term_second.reshape(shards, piece, features)
    fold = features // 2
    early = jnp.concatenate(
        [
            pair_got[:, :, :units],
            jnp.concatenate([term_second[:, :, :fold], term_second[:, :, fold:]], axis=1),
            term_proj.reshape(half, shards, own).transpose(1, 0, 2),
        ],
        axis=2,
    )
    early_sum = lax.psum_scatter(
        early.reshape(shards * half, early.shape[2]), CHIPS, scatter_dimension=0, tiled=True
    )
    last_got, early_sum = lax.optimization_barrier((last_got, early_sum))
    early_got = lax.all_gather(early_sum, CHIPS, axis=0, tiled=True)
    second_low, last_got = lax.optimization_barrier((second_low, last_got))
    second_own = lax.dynamic_index_in_dim(second_low, place, 0, keepdims=False).astype(wide)
    second_near = scatter_sum(second_own, second_low, place, ((0, 1), (0, 3), (0, 2)))
    grad_attend = jnp.sum(last_got[:, :, :features].astype(wide), axis=0)
    near = last_got[:, :, features : features + own]
    far = last_got[:, :, features + own :]
    term_qkv = jnp.concatenate([near[:, :half], near[:, half:], far[:, :half]], axis=2)
    mod_got = far[:, half:].astype(wide)
    head_rows = ada_rows + features // LANES
    mod_sums = jnp.sum(mod_got[:, :head_rows], axis=0)
    bias_qv_all = jnp.concatenate(
        [mod_got[:, head_rows].reshape(features), mod_got[:, head_rows + 1].reshape(features)]
    )
    norm_own, inverse_own = normalize(stream)
    grad_stream = grad_middle + normalize_back(
        norm_own, inverse_own, grad_attend * (1.0 + scale_first)
    )
    grad_latents = grad_stream.astype(low)

    grad_modulation = mod_sums[:ada_rows].reshape(ada_width)
    proj_bias_term = lax.dynamic_slice_in_dim(mod_sums, ada_rows + place, 1, 0)
    cond_term = jnp.sum(w_ada.astype(wide) * grad_modulation[None, :], axis=1)
    second_bias_sums = second_bias_sums[0]
    rep_terms = jnp.concatenate(
        [
            mod_sums[:ada_rows],
            cond_own.astype(wide),
            proj_bias_term,
            hidden_sums.reshape(units // LANES, LANES),
            lax.dynamic_slice_in_dim(second_bias_sums, place * own, own, 0)[None],
            lax.dynamic_slice_in_dim(bias_qv_all, place * 2 * own, 2 * own, 0).reshape(2, own),
        ]
    )
    rep_terms = jnp.pad(rep_terms, ((0, half - rep_terms.shape[0]), (0, 0))).astype(low)
    rep_terms = jnp.concatenate([rep_terms, swap_core(rep_terms)], axis=1)

    rep_sent = jnp.concatenate([term_qkv, copies(rep_terms)], axis=2)
    rep_got = exchange(rep_sent, CHIPS)
    rep_got, cond_term = lax.optimization_barrier((rep_got, cond_term))
    cond_total = gather_small(cond_term[None], place).reshape(1, features)
    grad_cond = silu_pull(cond_total)[0]
    width = 3 * own
    owned = jnp.sum(rep_got[:, :, :width].astype(wide), axis=0).astype(low)
    rep_small = jnp.concatenate(
        [rep_got[:, :, width : width + own], rep_got[:, :, width + own :]], axis=0
    )
    grad_w_ada = t_mul(
        rep_small[:, ada_rows], rep_small[:, :ada_rows].reshape(2 * shards, ada_width)
    )
    rep_sums = jnp.sum(rep_small.astype(wide), axis=0)
    ada_own = ada_rows // shards
    grad_b_ada = lax.dynamic_slice_in_dim(rep_sums, place * ada_own, ada_own, 0)
    grad_b_ada = grad_b_ada.reshape(ada_width // shards)
    at = ada_rows + 1
    grad_b_proj = rep_sums[at]
    at += 1
    grad_b_fc1 = rep_sums[at : at + units // LANES].reshape(units)
    at += units // LANES
    grad_b_fc2 = rep_sums[at]
    grad_bias_qv = rep_sums[at + 1 : at + 3].reshape(2 * own)

    owned, second_near = lax.optimization_barrier((owned, second_near))
    whole_mine = exchange(copies(owned), CHIPS)
    branch_second = (
        scatter_sum(second_near, second_low, place, ((1, 0), (1, 1), (1, 3), (1, 2)))
        + second_bias
    )
    output = (middle + gate_second * branch_second).astype(low)
    whole_mine, grad_w_ada = lax.optimization_barrier((whole_mine, grad_w_ada))
    grad_w_fc1, grad_w_fc2, grad_w_qkv, grad_w_proj = unpack(
        core.astype(jnp.int32)[None],
        early_got.reshape(early.shape),
        swap_core(early_got).reshape(early.shape),
        whole_mine,
        swap_core(whole_mine),
        units,
        features,
    )

    return (
        output[None],
        grad_latents[None],
        grad_cond,
        grad_w_qkv,
        grad_bias_qv,
        grad_w_proj,
        grad_b_proj,
        grad_w_fc1,
        grad_b_fc1,
        grad_w_fc2,
        grad_b_fc2,
        grad_w_ada,
        grad_b_ada,
    )


def solution(mesh):
    fine = Mesh(mesh.devices.reshape(2, 4, 2, 2, 4), REP + SHARD)
    tokens = P(REP, SHARD, None)
    matrix = P(SHARD, None)
    vector = P(SHARD)
    params = (matrix, vector) * 5
    return jax.shard_map(
        on_device,
        mesh=fine,
        in_specs=(tokens, P(REP, None), tokens) + params,
        out_specs=(tokens, tokens, P(REP, None)) + params,
        check_vma=False,
    )
```

```python
import jax
import jax.numpy as jnp
from jax import lax
from jax.experimental import pallas as pl
from jax.experimental.pallas import tpu as pltpu
from jax.sharding import Mesh, PartitionSpec as P

HEAD = 64
SHARD = ("xh", "y")
CHIPS = ("xl", "z")
REP = ("xl", "z", "core")
LANES = 128
QUERY_BLOCK = 256
SCALE = HEAD ** (-0.5)

epsilon = 1e-06
highest = lax.Precision.HIGHEST
low = jnp.bfloat16
wide = jnp.float32


def swap_core(value):
    return lax.ppermute(value, "core", [(0, 1), (1, 0)])


def exchange(value, axes=SHARD):
    return lax.all_to_all(value, axes, 0, 0, tiled=True)


def copies(value):
    return jnp.broadcast_to(value[None], (8,) + value.shape)


def as_rows(value, count):
    rows = value.reshape(-1, LANES)
    return jnp.pad(rows, ((0, count - rows.shape[0]), (0, 0)))


def normalize(values):
    centered = values - jnp.mean(values, axis=-1, keepdims=True)
    inverse = lax.rsqrt(jnp.mean(centered * centered, axis=-1, keepdims=True) + epsilon)
    return centered * inverse, inverse


def normalize_back(norm, inverse, grad):
    return inverse * (
        grad
        - jnp.mean(grad, axis=-1, keepdims=True)
        - norm * jnp.mean(grad * norm, axis=-1, keepdims=True)
    )


def silu(values):
    return values / (1.0 + jnp.exp(-values))


def gelu_tanh(values):
    return (
        0.5
        * values
        * (1.0 + jnp.tanh(0.7978845608028654 * (values + 0.044715 * values * values * values)))
    )


def mul(left, right):
    return lax.dot_general(left, right, (((1,), (0,)), ((), ())), preferred_element_type=wide)


def mul_t(left, right):
    return lax.dot_general(left, right, (((1,), (1,)), ((), ())), preferred_element_type=wide)


def t_mul(left, right):
    return lax.dot_general(left, right, (((0,), (0,)), ((), ())), preferred_element_type=wide)


def head_of(value, index):
    lane = lax.broadcasted_iota(jnp.int32, value.shape, 1)
    return jnp.where((lane >= HEAD) == (index == 1), value, jnp.zeros_like(value))


def attend_kernel(
    got_ref, wq_ref, scale_ref, shift_ref, qb_ref, vb_ref, in_ref, q_ref, k_ref, v_ref, mixed_ref, log_ref
):
    count, rows, _ = got_ref.shape
    features = scale_ref.shape[1]
    own = qb_ref.shape[1]
    gain = 1.0 + scale_ref[...]
    for block in range(count):
        at = pl.ds(block * rows, rows)
        norm, _ = normalize(got_ref[block, :, 0:features].astype(wide))
        attend_in = (norm * gain + shift_ref[...]).astype(low)
        in_ref[at, :] = attend_in
        packed = mul(attend_in, wq_ref[...])
        q_ref[at, :] = (packed[:, :own] + qb_ref[...]).astype(low)
        k_ref[at, :] = packed[:, own : 2 * own].astype(low)
        v_ref[at, :] = (packed[:, 2 * own :] + vb_ref[...]).astype(low)
    for block in range(count * rows // QUERY_BLOCK):
        at = pl.ds(block * QUERY_BLOCK, QUERY_BLOCK)
        total = None
        logs = None
        for index in range(2):
            scores = mul_t(head_of(q_ref[at, :], index), k_ref[...]) * SCALE
            peak = jnp.max(scores, axis=1, keepdims=True)
            powered = jnp.exp(scores - peak)
            row_total = jnp.sum(powered, axis=1, keepdims=True)
            probs = (powered / row_total).astype(low)
            part = mul(probs, head_of(v_ref[...], index))
            log = head_of(jnp.broadcast_to(peak + jnp.log(row_total), part.shape), index)
            total = part if total is None else total + part
            logs = log if logs is None else logs + log
        mixed_ref[at, :] = total.astype(low)
        log_ref[at, :] = logs


def attend(got, wq, scale, shift, query_bias, value_bias):
    length, features = wq.shape
    length = got.shape[0] * got.shape[1]
    features = wq.shape[0]
    own = wq.shape[1] // 3
    head = jax.ShapeDtypeStruct((length, own), low)
    return pl.pallas_call(
        attend_kernel,
        out_shape=[
            jax.ShapeDtypeStruct((length, features), low),
            head,
            head,
            head,
            head,
            jax.ShapeDtypeStruct((length, own), wide),
        ],
        compiler_params=pltpu.CompilerParams(vmem_limit_bytes=40 * 1024 * 1024),
        cost_estimate=pl.CostEstimate(
            flops=16 * length * length * own,
            transcendentals=2 * length * length,
            bytes_accessed=8 * length * features,
        ),
        name="attend",
    )(got, wq, scale, shift, query_bias, value_bias)


def attend_back_kernel(
    q_ref, g_ref, log_ref, k_ref, v_ref, wq_far, in_far, got_far,
    part_ref, term_ref, sums_ref, packed_sums_ref, packed, key_acc, value_acc,
    wq_ref, in_ref, got_ref, sems,
):
    loads = [
        pltpu.make_async_copy(source, target, sems.at[slot])
        for slot, (source, target) in enumerate(
            ((wq_far, wq_ref), (got_far, got_ref), (in_far, in_ref))
        )
    ]
    for load in loads:
        load.start()
    length, own = q_ref.shape
    count, rows, _ = got_ref.shape
    features = in_ref.shape[1]
    for block in range(length // QUERY_BLOCK):
        at = pl.ds(block * QUERY_BLOCK, QUERY_BLOCK)
        grad_query = None
        for index in range(2):
            query = head_of(q_ref[at, :], index)
            grad = head_of(g_ref[at, :], index)
            log = log_ref[at, index * HEAD : index * HEAD + 1]
            probs = jnp.exp(mul_t(query, k_ref[...]) * SCALE - log)
            grad_probs = mul_t(grad, v_ref[...])
            delta = jnp.sum(probs * grad_probs, axis=1, keepdims=True)
            grad_scores = (probs * (grad_probs - delta)).astype(low)
            part = mul(grad_scores, head_of(k_ref[...], index))
            grad_query = part if grad_query is None else grad_query + part
            key_part = t_mul(grad_scores, query)
            value_part = t_mul(probs.astype(low), grad)
            if block == 0 and index == 0:
                key_acc[...] = key_part
                value_acc[...] = value_part
            else:
                key_acc[...] += key_part
                value_acc[...] += value_part
        packed[at, 0:own] = (grad_query * SCALE).astype(low)
    packed[:, own : 2 * own] = (key_acc[...] * SCALE).astype(low)
    packed[:, 2 * own : 3 * own] = value_acc[...].astype(low)
    for load in loads:
        load.wait()
    packed_sums_ref[...] = jnp.sum(packed[...].astype(wide), axis=0, keepdims=True)
    shift_sum = None
    scale_sum = None
    for block in range(count):
        at = pl.ds(block * rows, rows)
        part = mul_t(packed[at, :], wq_ref[...])
        norm, _ = normalize(got_ref[block, :, 0:features].astype(wide))
        part_ref[block] = part.astype(low)
        one = jnp.sum(part, axis=0, keepdims=True)
        two = jnp.sum(part * norm, axis=0, keepdims=True)
        shift_sum = one if shift_sum is None else shift_sum + one
        scale_sum = two if scale_sum is None else scale_sum + two
    sums_ref[0:1, :] = shift_sum
    sums_ref[1:2, :] = scale_sum
    for block in range(features // QUERY_BLOCK):
        at = pl.ds(block * QUERY_BLOCK, QUERY_BLOCK)
        term_ref[at, :] = t_mul(in_ref[:, at], packed[...]).astype(low)


def attend_back(queries, grad_mixed, logs, keyset, valueset, wq, attend_in, got):
    length, own = queries.shape
    features = attend_in.shape[1]
    count, rows, _ = got.shape
    return pl.pallas_call(
        attend_back_kernel,
        in_specs=[pl.BlockSpec(memory_space=pltpu.VMEM)] * 5
        + [pl.BlockSpec(memory_space=pltpu.HBM)] * 3,
        out_shape=[
            jax.ShapeDtypeStruct((count, rows, features), low),
            jax.ShapeDtypeStruct((features, 3 * own), low),
            jax.ShapeDtypeStruct((2, features), wide),
            jax.ShapeDtypeStruct((1, 3 * own), wide),
        ],
        scratch_shapes=[
            pltpu.VMEM((length, 3 * own), low),
            pltpu.VMEM((length, own), wide),
            pltpu.VMEM((length, own), wide),
            pltpu.VMEM(wq.shape, low),
            pltpu.VMEM(attend_in.shape, low),
            pltpu.VMEM(got.shape, low),
            pltpu.SemaphoreType.DMA((3,)),
        ],
        compiler_params=pltpu.CompilerParams(vmem_limit_bytes=40 * 1024 * 1024),
        cost_estimate=pl.CostEstimate(
            flops=32 * length * length * own,
            transcendentals=2 * length * length,
            bytes_accessed=12 * length * features,
        ),
        name="attend_back",
    )(queries, grad_mixed, logs, keyset, valueset, wq, attend_in, got)


def gated_kernel(
    feed_ref, w1_ref, b1_ref, w2_ref, got_ref, gate_ref,
    grad_ref, second_ref, active_ref, hidden_ref, branch_ref, gate_sum, branch_sum, hidden_sum,
):
    count, rows, features = feed_ref.shape
    skip = got_ref.shape[2] - features

    @pl.when(pl.program_id(0) == 0)
    def _():
        for ref in (gate_sum, branch_sum, hidden_sum):
            ref[...] = jnp.zeros_like(ref)

    feed = feed_ref[...].reshape(count * rows, features)
    upstream = got_ref[:, :, skip:].reshape(count * rows, features).astype(wide)
    hidden = mul(feed, w1_ref[...]) + b1_ref[...]
    square = hidden * hidden
    bent = jnp.tanh(0.7978845608028654 * (hidden + 0.044715 * square * hidden))
    rise = 0.5 * (1.0 + bent)
    slope = rise + 0.5 * hidden * (1.0 - bent * bent) * (
        0.7978845608028654 * (1.0 + 3.0 * 0.044715 * square)
    )
    active = (hidden * rise).astype(low)
    active_ref[...] = active
    second = mul(active, w2_ref[...])
    second_ref[...] = second.astype(low).reshape(count, rows, features)
    gate_sum[...] += jnp.sum(upstream * second, axis=0, keepdims=True)
    grad_branch = (upstream * gate_ref[...]).astype(low)
    branch_ref[...] = grad_branch
    branch_sum[...] += jnp.sum(grad_branch.astype(wide), axis=0, keepdims=True)
    grad_hidden = (mul_t(grad_branch, w2_ref[...]) * slope).astype(low)
    hidden_ref[...] = grad_hidden
    hidden_sum[...] += jnp.sum(grad_hidden.astype(wide), axis=0, keepdims=True)
    grad_feed = mul_t(grad_hidden, w1_ref[...]).astype(low)
    grad_ref[...] = grad_feed.reshape(count, rows, features)


def gated(feed, w1, b1, w2, got, gate):
    count, rows, features = feed.shape
    units = w1.shape[1]
    length = count * rows
    pair = 2

    def fixed(*shape):
        return pl.BlockSpec(shape, lambda i: (0,) * len(shape))

    def blocks(width):
        return pl.BlockSpec((pair, rows, width), lambda i: (i, 0, 0))

    def flat(width):
        return pl.BlockSpec((pair * rows, width), lambda i: (i, 0))

    return pl.pallas_call(
        gated_kernel,
        grid=(count // pair,),
        in_specs=[
            blocks(features),
            fixed(features, units),
            fixed(1, units),
            fixed(units, features),
            blocks(got.shape[2]),
            fixed(1, features),
        ],
        out_specs=[
            blocks(features),
            blocks(features),
            flat(units),
            flat(units),
            flat(features),
            fixed(1, features),
            fixed(1, features),
            fixed(1, units),
        ],
        out_shape=[
            pltpu.HBM((count, rows, features), low),
            pltpu.HBM((count, rows, features), low),
            pltpu.HBM((length, units), low),
            pltpu.HBM((length, units), low),
            pltpu.HBM((length, features), low),
            jax.ShapeDtypeStruct((1, features), wide),
            jax.ShapeDtypeStruct((1, features), wide),
            jax.ShapeDtypeStruct((1, units), wide),
        ],
        compiler_params=pltpu.CompilerParams(vmem_limit_bytes=40 * 1024 * 1024),
        cost_estimate=pl.CostEstimate(
            flops=8 * length * features * units,
            transcendentals=length * units,
            bytes_accessed=16 * length * features,
        ),
        name="gated",
    )(feed, w1, b1, w2, got, gate)


def weights_kernel(feed_ref, hidden_ref, active_ref, branch_ref, first_ref, second_ref):
    features = feed_ref.shape[1]
    units = hidden_ref.shape[1]
    own = 2 * first_ref.shape[2]
    half = own // 2
    for block in range(features // QUERY_BLOCK):
        at = pl.ds(block * QUERY_BLOCK, QUERY_BLOCK)
        term = t_mul(feed_ref[:, at], hidden_ref[...]).astype(low)
        for piece in range(QUERY_BLOCK // own):
            target = block * (QUERY_BLOCK // own) + piece
            first_ref[0, target] = term[piece * own : piece * own + half]
            first_ref[1, target] = term[piece * own + half : (piece + 1) * own]
    for block in range(units // QUERY_BLOCK):
        at = pl.ds(block * QUERY_BLOCK, QUERY_BLOCK)
        second_ref[at, :] = t_mul(active_ref[:, at], branch_ref[...]).astype(low)


def weights_back(feed, grad_hidden, active, grad_branch, shards):
    length, features = feed.shape
    units = active.shape[1]
    return pl.pallas_call(
        weights_kernel,
        out_shape=[
            jax.ShapeDtypeStruct((2, shards, features // shards // 2, units), low),
            jax.ShapeDtypeStruct((units, features), low),
        ],
        compiler_params=pltpu.CompilerParams(vmem_limit_bytes=40 * 1024 * 1024),
        cost_estimate=pl.CostEstimate(
            flops=4 * length * features * units,
            transcendentals=0,
            bytes_accessed=10 * length * features,
        ),
        name="weights_back",
    )(feed, grad_hidden, active, grad_branch)


def proj_kernel(got_ref, grad_ref, out_ref):
    count = got_ref.shape[0]
    half = out_ref.shape[2]
    for block in range(count):
        term = t_mul(got_ref[block, :, 0 : 2 * half], grad_ref[...]).astype(low)
        out_ref[0, block] = term[:half]
        out_ref[1, block] = term[half:]


def proj_back(got, grad, own):
    count, rows, _ = got.shape
    features = grad.shape[1]
    return pl.pallas_call(
        proj_kernel,
        out_shape=jax.ShapeDtypeStruct((2, count, own // 2, features), low),
        compiler_params=pltpu.CompilerParams(vmem_limit_bytes=40 * 1024 * 1024),
        name="proj_back",
    )(got, grad)


def unpack_kernel(core_ref, mine_ref, other_ref, first_ref, second_ref, qkv_ref, proj_ref):
    count, half, _ = mine_ref.shape
    units = first_ref.shape[1] // count
    features = second_ref.shape[1]
    fold = features // 2
    own = proj_ref.shape[1] // count
    piece = half // 2
    for side in range(2):
        rows = pl.ds(side * half, half)
        for block in range(count):
            value = jnp.where(
                core_ref[0] == side, mine_ref[block], other_ref[block]
            ).astype(wide)
            first_ref[rows, block * units : (block + 1) * units] = value[:, :units]
            at = pl.ds((side * count + block) * piece, piece)
            second_ref[at, :fold] = value[:piece, units : units + fold]
            second_ref[at, fold:] = value[piece:, units : units + fold]
            for part in range(3):
                lane = part * features + block * own
                start = units + fold + part * own
                qkv_ref[rows, lane : lane + own] = value[:, start : start + own]
            proj_ref[rows, block * own : (block + 1) * own] = value[:, units + fold + 3 * own :]


def unpack(core, mine, other, units, features):
    count, half, _ = mine.shape
    return pl.pallas_call(
        unpack_kernel,
        in_specs=[
            pl.BlockSpec(memory_space=pltpu.SMEM),
            pl.BlockSpec(memory_space=pltpu.VMEM),
            pl.BlockSpec(memory_space=pltpu.VMEM),
        ],
        out_shape=[
            jax.ShapeDtypeStruct((2 * half, count * units), wide),
            jax.ShapeDtypeStruct((units, features), wide),
            jax.ShapeDtypeStruct((2 * half, 3 * features), wide),
            jax.ShapeDtypeStruct((2 * half, features), wide),
        ],
        compiler_params=pltpu.CompilerParams(vmem_limit_bytes=40 * 1024 * 1024),
        name="unpack",
    )(core, mine, other)


def swap_add(value, core):
    keep = lax.dynamic_index_in_dim(value, core, 0, keepdims=False)
    give = lax.dynamic_index_in_dim(value, 1 - core, 0, keepdims=False)
    return (keep.astype(wide) + swap_core(give).astype(wide)).astype(low)


def shift_to(value, dx, dy):
    pairs = [(x * 4 + y, ((x + dx) % 2) * 4 + (y + dy) % 4) for x in range(2) for y in range(4)]
    return lax.ppermute(value, SHARD, pairs)


def scatter_sum(total, value, place, offsets):
    for dx, dy in offsets:
        target = ((place // 4 + dx) % 2) * 4 + (place + dy) % 4
        block = lax.dynamic_index_in_dim(value, target, 0, keepdims=False)
        total = total + shift_to(block, dx, dy).astype(wide)
    return total


def gather_small(value, place):
    for bit in (1, 2, 4):
        other = lax.ppermute(value, SHARD, [(k, k ^ bit) for k in range(8)])
        upper = (place // bit) % 2 == 1
        value = jnp.concatenate(
            [jnp.where(upper, other, value), jnp.where(upper, value, other)], axis=0
        )
    return value


def join_rows(mine, other, core):
    first = jnp.where(core == 0, mine, other)
    second = jnp.where(core == 0, other, mine)
    return jnp.concatenate([first, second], axis=1).reshape(-1, mine.shape[-1])


def core_half(value, core):
    keep = lax.dynamic_index_in_dim(value, core, 1, keepdims=False)
    give = lax.dynamic_index_in_dim(value, 1 - core, 1, keepdims=False).astype(low)
    return (keep.astype(wide) + swap_core(give).astype(wide)).astype(low)


def on_device(
    latents, cond, cotangent, w_qkv, bias_qv, w_proj, b_proj, w_fc1, b_fc1, w_fc2, b_fc2, w_ada, b_ada
):
    stream_low = latents[0]
    upstream_low = cotangent[0]
    rows, features = stream_low.shape
    shards = 8
    length = shards * rows
    own = features // shards
    half = own // 2
    units = w_fc2.shape[0]
    ada_width = w_ada.shape[1]
    ada_rows = ada_width // LANES
    place = lax.axis_index(SHARD)
    core = lax.axis_index("core")

    cond_value = cond.astype(wide)
    cond_silu, silu_pull = jax.vjp(silu, cond_value)
    cond_low = cond_silu.astype(low)
    cond_own = lax.dynamic_slice_in_dim(cond_low, place * own, own, 1)
    mod_part = mul(cond_own, w_ada)[0]
    blocks = jnp.arange(shards)[:, None] == place
    mod_part = mod_part + jnp.where(blocks, b_ada.astype(wide)[None, :], 0.0).reshape(ada_width)
    small = jnp.concatenate([mod_part.astype(low), bias_qv, b_proj, b_fc2])

    def halved(value):
        return lax.dynamic_slice_in_dim(value, core * half, half, 0)

    qkv_mine = halved(w_qkv)

    def qkv_part(part):
        return jnp.stack(
            [
                qkv_mine[:, part * features + k * own : part * features + (k + 1) * own]
                for k in range(shards)
            ]
        )

    first_sent = jnp.concatenate(
        [
            copies(stream_low),
            jnp.concatenate([qkv_part(0), qkv_part(1)], axis=1),
            jnp.concatenate([qkv_part(2), copies(as_rows(small, half))], axis=1),
        ],
        axis=2,
    )
    first_got = exchange(first_sent)
    weights_sent = jnp.concatenate(
        [
            halved(w_fc1).reshape(half, shards, units).transpose(1, 0, 2),
            copies(halved(w_proj)),
        ],
        axis=2,
    )
    weights_sent, first_got = lax.optimization_barrier((weights_sent, first_got))
    weights_got = exchange(weights_sent)
    near = first_got[:, :, features : features + own]
    far = first_got[:, :, features + own :]
    qkv_got = jnp.concatenate([near[:, :half], near[:, half:], far[:, :half]], axis=2)
    wq = join_rows(qkv_got, swap_core(qkv_got), core)
    small_got = far[:, half:].astype(wide)
    modulation = jnp.sum(small_got[:, :ada_rows], axis=0).reshape(1, ada_width)
    shift_first, scale_first, gate_first, shift_second, scale_second, gate_second = jnp.split(
        modulation, 6, axis=1
    )
    at = ada_rows
    bias_wide = small_got[:, at : at + 2].reshape(1, 2 * features)
    proj_bias = small_got[:, at + 2].reshape(1, features)
    second_bias = small_got[:, at + 3].reshape(1, features)

    query_bias = lax.dynamic_slice_in_dim(bias_wide, place * own, own, 1)
    value_bias = lax.dynamic_slice_in_dim(bias_wide, features + place * own, own, 1)
    attend_in, queries, keyset, valueset, mixed, log_total = attend(
        first_got, wq, scale_first, shift_first, query_bias, value_bias
    )
    mixed, weights_got = lax.optimization_barrier((mixed, weights_got))
    mixed_got = exchange(
        jnp.concatenate([mixed.reshape(shards, rows, own), copies(upstream_low)], axis=2)
    )
    weights_other = swap_core(weights_got)
    w1 = join_rows(weights_got[:, :, :units], weights_other[:, :, :units], core)
    wp = join_rows(weights_got[:, :, units:], weights_other[:, :, units:], core)
    mixed_tok = mixed_got[:, :, :own].transpose(1, 0, 2).reshape(rows, features)
    upstream_all = mixed_got[:, :, own:].reshape(length, features)
    branch = mul(mixed_tok, wp) + proj_bias
    stream = stream_low.astype(wide)
    middle = stream + gate_first * branch
    norm_second, inverse_second = normalize(middle)
    feed_in = (norm_second * (1.0 + scale_second) + shift_second).astype(low)
    feed_got = exchange(copies(feed_in))
    (
        feed_part,
        second_low,
        active,
        grad_hidden,
        grad_branch_second,
        gate_sums,
        second_bias_sums,
        hidden_sums,
    ) = gated(feed_got, w1, b_fc1.astype(wide)[None, :], w_fc2, mixed_got, gate_second)
    feed_back = exchange(feed_part)
    term_first, term_second = weights_back(
        feed_got.reshape(length, features), grad_hidden, active, grad_branch_second, shards
    )
    term_first = swap_add(term_first, core)
    feed_back, term_first, term_second = lax.optimization_barrier(
        (feed_back, term_first, term_second)
    )
    grad_feed = jnp.sum(feed_back.astype(wide), axis=0)

    upstream = upstream_low.astype(wide)
    grad_gate_second = gate_sums[0] + second_bias[0] * jnp.sum(upstream, axis=0)
    grad_scale_second = jnp.sum(grad_feed * norm_second, axis=0)
    grad_shift_second = jnp.sum(grad_feed, axis=0)
    grad_middle = upstream + normalize_back(
        norm_second, inverse_second, grad_feed * (1.0 + scale_second)
    )
    grad_gate_first = jnp.sum(grad_middle * branch, axis=0)
    grad_branch = (grad_middle * gate_first).astype(low)
    grad_mixed_tok = mul_t(grad_branch, wp).astype(low)
    grad_mixed = exchange(grad_mixed_tok.reshape(rows, shards, own).transpose(1, 0, 2))
    term_proj = proj_back(mixed_got, grad_branch, own)
    term_proj, grad_mixed = lax.optimization_barrier((term_proj, grad_mixed))
    pair_got = exchange(jnp.concatenate([term_first, swap_add(term_proj, core)], axis=2))
    attend_part, term_qkv, attend_sums, packed_sums = attend_back(
        queries, grad_mixed.reshape(length, own), log_total, keyset, valueset, wq, attend_in, first_got
    )
    attend_part, term_qkv, attend_sums, packed_sums, pair_got = lax.optimization_barrier(
        (attend_part, term_qkv, attend_sums, packed_sums, pair_got)
    )
    packed_sums = packed_sums[0]
    grad_shift_first = attend_sums[0]
    grad_scale_first = attend_sums[1]
    mod_terms = jnp.concatenate(
        [
            grad_shift_first,
            grad_scale_first,
            grad_gate_first,
            grad_shift_second,
            grad_scale_second,
            grad_gate_second,
            jnp.sum(grad_branch.astype(wide), axis=0),
            packed_sums[:own],
            packed_sums[2 * own :],
        ]
    ).astype(low)
    term_qkv = core_half(term_qkv.reshape(shards, 2, half, 3 * own), core)
    last_sent = jnp.concatenate(
        [
            attend_part,
            jnp.concatenate([term_qkv[:, :, :own], term_qkv[:, :, own : 2 * own]], axis=1),
            jnp.concatenate(
                [term_qkv[:, :, 2 * own :], copies(as_rows(mod_terms, half))], axis=1
            ),
        ],
        axis=2,
    )
    last_got = exchange(last_sent)
    second_low, last_got = lax.optimization_barrier((second_low, last_got))
    second_own = lax.dynamic_index_in_dim(second_low, place, 0, keepdims=False).astype(wide)
    second_near = scatter_sum(second_own, second_low, place, ((0, 1), (0, 3), (0, 2)))
    grad_attend = jnp.sum(last_got[:, :, :features].astype(wide), axis=0)
    near = last_got[:, :, features : features + own]
    far = last_got[:, :, features + own :]
    term_qkv = jnp.concatenate([near[:, :half], near[:, half:], far[:, :half]], axis=2)
    mod_got = far[:, half:].astype(wide)
    head_rows = ada_rows + features // LANES
    mod_sums = jnp.sum(mod_got[:, :head_rows], axis=0)
    bias_qv_all = jnp.concatenate(
        [mod_got[:, head_rows].reshape(features), mod_got[:, head_rows + 1].reshape(features)]
    )
    norm_own, inverse_own = normalize(stream)
    grad_stream = grad_middle + normalize_back(
        norm_own, inverse_own, grad_attend * (1.0 + scale_first)
    )
    grad_latents = grad_stream.astype(low)

    grad_modulation = mod_sums[:ada_rows].reshape(ada_width)
    proj_bias_term = lax.dynamic_slice_in_dim(mod_sums, ada_rows + place, 1, 0)
    cond_term = jnp.sum(w_ada.astype(wide) * grad_modulation[None, :], axis=1)
    cond_total = gather_small(cond_term[None], place).reshape(1, features)
    grad_cond = silu_pull(cond_total)[0]

    second_bias_sums = second_bias_sums[0]
    rep_terms = jnp.concatenate(
        [
            mod_sums[:ada_rows],
            cond_own.astype(wide),
            proj_bias_term,
            hidden_sums.reshape(units // LANES, LANES),
            lax.dynamic_slice_in_dim(second_bias_sums, place * own, own, 0)[None],
            lax.dynamic_slice_in_dim(bias_qv_all, place * 2 * own, 2 * own, 0).reshape(2, own),
        ]
    )
    rep_terms = jnp.pad(rep_terms, ((0, half - rep_terms.shape[0]), (0, 0))).astype(low)
    rep_terms = jnp.concatenate([rep_terms, swap_core(rep_terms)], axis=1)

    term_first = pair_got[:, :, :units]
    term_proj = jnp.sum(pair_got[:, :, units:].astype(wide), axis=0).astype(low)
    term_second = swap_add(term_second.reshape(2, units // 2, features), core)
    piece = units // 2 // shards
    term_second = term_second.reshape(shards, piece, features)
    fold = features // 2

    rep_sent = jnp.concatenate(
        [
            term_first,
            jnp.concatenate([term_second[:, :, :fold], term_second[:, :, fold:]], axis=1),
            term_qkv,
            term_proj.reshape(half, shards, own).transpose(1, 0, 2),
            copies(rep_terms),
        ],
        axis=2,
    )
    rep_got = exchange(rep_sent, CHIPS)
    width = units + fold + 4 * own
    owned = jnp.sum(rep_got[:, :, :width].astype(wide), axis=0).astype(low)
    rep_small = jnp.concatenate(
        [rep_got[:, :, width : width + own], rep_got[:, :, width + own :]], axis=0
    )
    grad_w_ada = t_mul(
        rep_small[:, ada_rows], rep_small[:, :ada_rows].reshape(2 * shards, ada_width)
    )
    rep_sums = jnp.sum(rep_small.astype(wide), axis=0)
    ada_own = ada_rows // shards
    grad_b_ada = lax.dynamic_slice_in_dim(rep_sums, place * ada_own, ada_own, 0)
    grad_b_ada = grad_b_ada.reshape(ada_width // shards)
    at = ada_rows + 1
    grad_b_proj = rep_sums[at]
    at += 1
    grad_b_fc1 = rep_sums[at : at + units // LANES].reshape(units)
    at += units // LANES
    grad_b_fc2 = rep_sums[at]
    grad_bias_qv = rep_sums[at + 1 : at + 3].reshape(2 * own)

    owned, second_near = lax.optimization_barrier((owned, second_near))
    whole_mine = exchange(copies(owned), CHIPS)
    branch_second = (
        scatter_sum(second_near, second_low, place, ((1, 0), (1, 1), (1, 3), (1, 2)))
        + second_bias
    )
    output = (middle + gate_second * branch_second).astype(low)
    whole_mine, grad_w_ada = lax.optimization_barrier((whole_mine, grad_w_ada))
    grad_w_fc1, grad_w_fc2, grad_w_qkv, grad_w_proj = unpack(
        core.astype(jnp.int32)[None], whole_mine, swap_core(whole_mine), units, features
    )

    return (
        output[None],
        grad_latents[None],
        grad_cond,
        grad_w_qkv,
        grad_bias_qv,
        grad_w_proj,
        grad_b_proj,
        grad_w_fc1,
        grad_b_fc1,
        grad_w_fc2,
        grad_b_fc2,
        grad_w_ada,
        grad_b_ada,
    )


def solution(mesh):
    fine = Mesh(mesh.devices.reshape(2, 4, 2, 2, 4), REP + SHARD)
    tokens = P(REP, SHARD, None)
    matrix = P(SHARD, None)
    vector = P(SHARD)
    params = (matrix, vector) * 5
    return jax.shard_map(
        on_device,
        mesh=fine,
        in_specs=(tokens, P(REP, None), tokens) + params,
        out_specs=(tokens, tokens, P(REP, None)) + params,
        check_vma=False,
    )
```

```python
import jax
import jax.numpy as jnp
from jax import lax
from jax.experimental import pallas as pl
from jax.experimental.pallas import tpu as pltpu
from jax.sharding import Mesh, PartitionSpec as P

HEAD = 64
SHARD = ("xh", "y")
CHIPS = ("xl", "z")
REP = ("xl", "z", "core")
LANES = 128
QUERY_BLOCK = 256
SCALE = HEAD ** (-0.5)

epsilon = 1e-06
highest = lax.Precision.HIGHEST
low = jnp.bfloat16
wide = jnp.float32


def swap_core(value):
    return lax.ppermute(value, "core", [(0, 1), (1, 0)])


def exchange(value, axes=SHARD):
    return lax.all_to_all(value, axes, 0, 0, tiled=True)


def copies(value):
    return jnp.broadcast_to(value[None], (8,) + value.shape)


def as_rows(value, count):
    rows = value.reshape(-1, LANES)
    return jnp.pad(rows, ((0, count - rows.shape[0]), (0, 0)))


def normalize(values):
    centered = values - jnp.mean(values, axis=-1, keepdims=True)
    inverse = lax.rsqrt(jnp.mean(centered * centered, axis=-1, keepdims=True) + epsilon)
    return centered * inverse, inverse


def normalize_back(norm, inverse, grad):
    return inverse * (
        grad
        - jnp.mean(grad, axis=-1, keepdims=True)
        - norm * jnp.mean(grad * norm, axis=-1, keepdims=True)
    )


def silu(values):
    return values / (1.0 + jnp.exp(-values))


def gelu_tanh(values):
    return (
        0.5
        * values
        * (1.0 + jnp.tanh(0.7978845608028654 * (values + 0.044715 * values * values * values)))
    )


def mul(left, right):
    return lax.dot_general(left, right, (((1,), (0,)), ((), ())), preferred_element_type=wide)


def mul_t(left, right):
    return lax.dot_general(left, right, (((1,), (1,)), ((), ())), preferred_element_type=wide)


def t_mul(left, right):
    return lax.dot_general(left, right, (((0,), (0,)), ((), ())), preferred_element_type=wide)


def head_of(value, index):
    lane = lax.broadcasted_iota(jnp.int32, value.shape, 1)
    return jnp.where((lane >= HEAD) == (index == 1), value, jnp.zeros_like(value))


def attend_kernel(
    got_ref, wq_ref, scale_ref, shift_ref, qb_ref, vb_ref, in_ref, q_ref, k_ref, v_ref, mixed_ref, log_ref
):
    count, rows, _ = got_ref.shape
    features = scale_ref.shape[1]
    own = qb_ref.shape[1]
    gain = 1.0 + scale_ref[...]
    for block in range(count):
        at = pl.ds(block * rows, rows)
        norm, _ = normalize(got_ref[block, :, 0:features].astype(wide))
        attend_in = (norm * gain + shift_ref[...]).astype(low)
        in_ref[at, :] = attend_in
        packed = mul(attend_in, wq_ref[...])
        q_ref[at, :] = (packed[:, :own] + qb_ref[...]).astype(low)
        k_ref[at, :] = packed[:, own : 2 * own].astype(low)
        v_ref[at, :] = (packed[:, 2 * own :] + vb_ref[...]).astype(low)
    for block in range(count * rows // QUERY_BLOCK):
        at = pl.ds(block * QUERY_BLOCK, QUERY_BLOCK)
        total = None
        logs = None
        for index in range(2):
            scores = mul_t(head_of(q_ref[at, :], index), k_ref[...]) * SCALE
            peak = jnp.max(scores, axis=1, keepdims=True)
            powered = jnp.exp(scores - peak)
            row_total = jnp.sum(powered, axis=1, keepdims=True)
            probs = (powered / row_total).astype(low)
            part = mul(probs, head_of(v_ref[...], index))
            log = head_of(jnp.broadcast_to(peak + jnp.log(row_total), part.shape), index)
            total = part if total is None else total + part
            logs = log if logs is None else logs + log
        mixed_ref[at, :] = total.astype(low)
        log_ref[at, :] = logs


def attend(got, wq, scale, shift, query_bias, value_bias):
    length, features = wq.shape
    length = got.shape[0] * got.shape[1]
    features = wq.shape[0]
    own = wq.shape[1] // 3
    head = jax.ShapeDtypeStruct((length, own), low)
    return pl.pallas_call(
        attend_kernel,
        out_shape=[
            jax.ShapeDtypeStruct((length, features), low),
            head,
            head,
            head,
            head,
            jax.ShapeDtypeStruct((length, own), wide),
        ],
        compiler_params=pltpu.CompilerParams(vmem_limit_bytes=40 * 1024 * 1024),
        cost_estimate=pl.CostEstimate(
            flops=16 * length * length * own,
            transcendentals=2 * length * length,
            bytes_accessed=8 * length * features,
        ),
        name="attend",
    )(got, wq, scale, shift, query_bias, value_bias)


def attend_back_kernel(
    q_far, g_far, log_far, k_far, v_far, wq_far, in_far, got_far,
    part_ref, term_ref, sums_ref, packed_sums_ref, packed, key_acc, value_acc,
    q_ref, g_ref, log_ref, k_ref, v_ref, wq_ref, in_ref, got_ref, sems,
):
    loads = [
        pltpu.make_async_copy(source, target, sems.at[slot])
        for slot, (source, target) in enumerate(
            (
                (q_far, q_ref),
                (k_far, k_ref),
                (log_far, log_ref),
                (g_far, g_ref),
                (v_far, v_ref),
                (wq_far, wq_ref),
                (got_far, got_ref),
                (in_far, in_ref),
            )
        )
    ]
    for load in loads:
        load.start()
    for load in loads[:5]:
        load.wait()
    length, own = q_ref.shape
    count, rows, _ = got_ref.shape
    features = in_ref.shape[1]
    for block in range(length // QUERY_BLOCK):
        at = pl.ds(block * QUERY_BLOCK, QUERY_BLOCK)
        grad_query = None
        for index in range(2):
            query = head_of(q_ref[at, :], index)
            grad = head_of(g_ref[at, :], index)
            log = log_ref[at, index * HEAD : index * HEAD + 1]
            probs = jnp.exp(mul_t(query, k_ref[...]) * SCALE - log)
            grad_probs = mul_t(grad, v_ref[...])
            delta = jnp.sum(probs * grad_probs, axis=1, keepdims=True)
            grad_scores = (probs * (grad_probs - delta)).astype(low)
            part = mul(grad_scores, head_of(k_ref[...], index))
            grad_query = part if grad_query is None else grad_query + part
            key_part = t_mul(grad_scores, query)
            value_part = t_mul(probs.astype(low), grad)
            if block == 0 and index == 0:
                key_acc[...] = key_part
                value_acc[...] = value_part
            else:
                key_acc[...] += key_part
                value_acc[...] += value_part
        packed[at, 0:own] = (grad_query * SCALE).astype(low)
    packed[:, own : 2 * own] = (key_acc[...] * SCALE).astype(low)
    packed[:, 2 * own : 3 * own] = value_acc[...].astype(low)
    for load in loads[5:]:
        load.wait()
    packed_sums_ref[...] = jnp.sum(packed[...].astype(wide), axis=0, keepdims=True)
    shift_sum = None
    scale_sum = None
    for block in range(count):
        at = pl.ds(block * rows, rows)
        part = mul_t(packed[at, :], wq_ref[...])
        norm, _ = normalize(got_ref[block, :, 0:features].astype(wide))
        part_ref[block] = part.astype(low)
        one = jnp.sum(part, axis=0, keepdims=True)
        two = jnp.sum(part * norm, axis=0, keepdims=True)
        shift_sum = one if shift_sum is None else shift_sum + one
        scale_sum = two if scale_sum is None else scale_sum + two
    sums_ref[0:1, :] = shift_sum
    sums_ref[1:2, :] = scale_sum
    for block in range(features // QUERY_BLOCK):
        at = pl.ds(block * QUERY_BLOCK, QUERY_BLOCK)
        term_ref[at, :] = t_mul(in_ref[:, at], packed[...]).astype(low)


def attend_back(queries, grad_mixed, logs, keyset, valueset, wq, attend_in, got):
    length, own = queries.shape
    features = attend_in.shape[1]
    count, rows, _ = got.shape
    return pl.pallas_call(
        attend_back_kernel,
        in_specs=[pl.BlockSpec(memory_space=pltpu.HBM)] * 8,
        out_shape=[
            jax.ShapeDtypeStruct((count, rows, features), low),
            jax.ShapeDtypeStruct((features, 3 * own), low),
            jax.ShapeDtypeStruct((2, features), wide),
            jax.ShapeDtypeStruct((1, 3 * own), wide),
        ],
        scratch_shapes=[
            pltpu.VMEM((length, 3 * own), low),
            pltpu.VMEM((length, own), wide),
            pltpu.VMEM((length, own), wide),
            pltpu.VMEM((length, own), low),
            pltpu.VMEM((length, own), low),
            pltpu.VMEM((length, own), wide),
            pltpu.VMEM((length, own), low),
            pltpu.VMEM((length, own), low),
            pltpu.VMEM(wq.shape, low),
            pltpu.VMEM(attend_in.shape, low),
            pltpu.VMEM(got.shape, low),
            pltpu.SemaphoreType.DMA((8,)),
        ],
        compiler_params=pltpu.CompilerParams(vmem_limit_bytes=40 * 1024 * 1024),
        cost_estimate=pl.CostEstimate(
            flops=32 * length * length * own,
            transcendentals=2 * length * length,
            bytes_accessed=12 * length * features,
        ),
        name="attend_back",
    )(queries, grad_mixed, logs, keyset, valueset, wq, attend_in, got)


def gated_kernel(
    feed_ref, w1_ref, b1_ref, w2_ref, got_ref, gate_ref,
    grad_ref, second_ref, active_ref, hidden_ref, branch_ref, gate_sum, branch_sum, hidden_sum,
):
    count, rows, features = feed_ref.shape
    skip = got_ref.shape[2] - features

    @pl.when(pl.program_id(0) == 0)
    def _():
        for ref in (gate_sum, branch_sum, hidden_sum):
            ref[...] = jnp.zeros_like(ref)

    feed = feed_ref[...].reshape(count * rows, features)
    upstream = got_ref[:, :, skip:].reshape(count * rows, features).astype(wide)
    hidden = mul(feed, w1_ref[...]) + b1_ref[...]
    square = hidden * hidden
    bent = jnp.tanh(0.7978845608028654 * (hidden + 0.044715 * square * hidden))
    rise = 0.5 * (1.0 + bent)
    slope = rise + 0.5 * hidden * (1.0 - bent * bent) * (
        0.7978845608028654 * (1.0 + 3.0 * 0.044715 * square)
    )
    active = (hidden * rise).astype(low)
    active_ref[...] = active
    second = mul(active, w2_ref[...])
    second_ref[...] = second.astype(low).reshape(count, rows, features)
    gate_sum[...] += jnp.sum(upstream * second, axis=0, keepdims=True)
    grad_branch = (upstream * gate_ref[...]).astype(low)
    branch_ref[...] = grad_branch
    branch_sum[...] += jnp.sum(grad_branch.astype(wide), axis=0, keepdims=True)
    grad_hidden = (mul_t(grad_branch, w2_ref[...]) * slope).astype(low)
    hidden_ref[...] = grad_hidden
    hidden_sum[...] += jnp.sum(grad_hidden.astype(wide), axis=0, keepdims=True)
    grad_feed = mul_t(grad_hidden, w1_ref[...]).astype(low)
    grad_ref[...] = grad_feed.reshape(count, rows, features)


def gated(feed, w1, b1, w2, got, gate):
    count, rows, features = feed.shape
    units = w1.shape[1]
    length = count * rows
    pair = 2

    def fixed(*shape):
        return pl.BlockSpec(shape, lambda i: (0,) * len(shape))

    def blocks(width):
        return pl.BlockSpec((pair, rows, width), lambda i: (i, 0, 0))

    def flat(width):
        return pl.BlockSpec((pair * rows, width), lambda i: (i, 0))

    return pl.pallas_call(
        gated_kernel,
        grid=(count // pair,),
        in_specs=[
            blocks(features),
            fixed(features, units),
            fixed(1, units),
            fixed(units, features),
            blocks(got.shape[2]),
            fixed(1, features),
        ],
        out_specs=[
            blocks(features),
            blocks(features),
            flat(units),
            flat(units),
            flat(features),
            fixed(1, features),
            fixed(1, features),
            fixed(1, units),
        ],
        out_shape=[
            pltpu.HBM((count, rows, features), low),
            pltpu.HBM((count, rows, features), low),
            pltpu.HBM((length, units), low),
            pltpu.HBM((length, units), low),
            pltpu.HBM((length, features), low),
            jax.ShapeDtypeStruct((1, features), wide),
            jax.ShapeDtypeStruct((1, features), wide),
            jax.ShapeDtypeStruct((1, units), wide),
        ],
        compiler_params=pltpu.CompilerParams(vmem_limit_bytes=40 * 1024 * 1024),
        cost_estimate=pl.CostEstimate(
            flops=8 * length * features * units,
            transcendentals=length * units,
            bytes_accessed=16 * length * features,
        ),
        name="gated",
    )(feed, w1, b1, w2, got, gate)


def weights_kernel(feed_ref, hidden_ref, active_ref, branch_ref, first_ref, second_ref):
    features = feed_ref.shape[1]
    units = hidden_ref.shape[1]
    own = 2 * first_ref.shape[2]
    half = own // 2
    for block in range(features // QUERY_BLOCK):
        at = pl.ds(block * QUERY_BLOCK, QUERY_BLOCK)
        term = t_mul(feed_ref[:, at], hidden_ref[...]).astype(low)
        for piece in range(QUERY_BLOCK // own):
            target = block * (QUERY_BLOCK // own) + piece
            first_ref[0, target] = term[piece * own : piece * own + half]
            first_ref[1, target] = term[piece * own + half : (piece + 1) * own]
    for block in range(units // QUERY_BLOCK):
        at = pl.ds(block * QUERY_BLOCK, QUERY_BLOCK)
        second_ref[at, :] = t_mul(active_ref[:, at], branch_ref[...]).astype(low)


def weights_back(feed, grad_hidden, active, grad_branch, shards):
    length, features = feed.shape
    units = active.shape[1]
    return pl.pallas_call(
        weights_kernel,
        out_shape=[
            jax.ShapeDtypeStruct((2, shards, features // shards // 2, units), low),
            jax.ShapeDtypeStruct((units, features), low),
        ],
        compiler_params=pltpu.CompilerParams(vmem_limit_bytes=40 * 1024 * 1024),
        cost_estimate=pl.CostEstimate(
            flops=4 * length * features * units,
            transcendentals=0,
            bytes_accessed=10 * length * features,
        ),
        name="weights_back",
    )(feed, grad_hidden, active, grad_branch)


def proj_kernel(got_ref, grad_ref, out_ref):
    count = got_ref.shape[0]
    half = out_ref.shape[2]
    for block in range(count):
        term = t_mul(got_ref[block, :, 0 : 2 * half], grad_ref[...]).astype(low)
        out_ref[0, block] = term[:half]
        out_ref[1, block] = term[half:]


def proj_back(got, grad, own):
    count, rows, _ = got.shape
    features = grad.shape[1]
    return pl.pallas_call(
        proj_kernel,
        out_shape=jax.ShapeDtypeStruct((2, count, own // 2, features), low),
        compiler_params=pltpu.CompilerParams(vmem_limit_bytes=40 * 1024 * 1024),
        name="proj_back",
    )(got, grad)


def unpack_kernel(core_ref, mine_ref, other_ref, first_ref, second_ref, qkv_ref, proj_ref):
    count, half, _ = mine_ref.shape
    units = first_ref.shape[1] // count
    features = second_ref.shape[1]
    fold = features // 2
    own = proj_ref.shape[1] // count
    piece = half // 2
    for side in range(2):
        rows = pl.ds(side * half, half)
        for block in range(count):
            value = jnp.where(
                core_ref[0] == side, mine_ref[block], other_ref[block]
            ).astype(wide)
            first_ref[rows, block * units : (block + 1) * units] = value[:, :units]
            at = pl.ds((side * count + block) * piece, piece)
            second_ref[at, :fold] = value[:piece, units : units + fold]
            second_ref[at, fold:] = value[piece:, units : units + fold]
            for part in range(3):
                lane = part * features + block * own
                start = units + fold + part * own
                qkv_ref[rows, lane : lane + own] = value[:, start : start + own]
            proj_ref[rows, block * own : (block + 1) * own] = value[:, units + fold + 3 * own :]


def unpack(core, mine, other, units, features):
    count, half, _ = mine.shape
    return pl.pallas_call(
        unpack_kernel,
        in_specs=[
            pl.BlockSpec(memory_space=pltpu.SMEM),
            pl.BlockSpec(memory_space=pltpu.VMEM),
            pl.BlockSpec(memory_space=pltpu.VMEM),
        ],
        out_shape=[
            jax.ShapeDtypeStruct((2 * half, count * units), wide),
            jax.ShapeDtypeStruct((units, features), wide),
            jax.ShapeDtypeStruct((2 * half, 3 * features), wide),
            jax.ShapeDtypeStruct((2 * half, features), wide),
        ],
        compiler_params=pltpu.CompilerParams(vmem_limit_bytes=40 * 1024 * 1024),
        name="unpack",
    )(core, mine, other)


def swap_add(value, core):
    keep = lax.dynamic_index_in_dim(value, core, 0, keepdims=False)
    give = lax.dynamic_index_in_dim(value, 1 - core, 0, keepdims=False)
    return (keep.astype(wide) + swap_core(give).astype(wide)).astype(low)


def shift_to(value, dx, dy):
    pairs = [(x * 4 + y, ((x + dx) % 2) * 4 + (y + dy) % 4) for x in range(2) for y in range(4)]
    return lax.ppermute(value, SHARD, pairs)


def scatter_sum(total, value, place, offsets):
    for dx, dy in offsets:
        target = ((place // 4 + dx) % 2) * 4 + (place + dy) % 4
        block = lax.dynamic_index_in_dim(value, target, 0, keepdims=False)
        total = total + shift_to(block, dx, dy).astype(wide)
    return total


def gather_small(value, place):
    for bit in (1, 2, 4):
        other = lax.ppermute(value, SHARD, [(k, k ^ bit) for k in range(8)])
        upper = (place // bit) % 2 == 1
        value = jnp.concatenate(
            [jnp.where(upper, other, value), jnp.where(upper, value, other)], axis=0
        )
    return value


def join_rows(mine, other, core):
    first = jnp.where(core == 0, mine, other)
    second = jnp.where(core == 0, other, mine)
    return jnp.concatenate([first, second], axis=1).reshape(-1, mine.shape[-1])


def core_half(value, core):
    keep = lax.dynamic_index_in_dim(value, core, 1, keepdims=False)
    give = lax.dynamic_index_in_dim(value, 1 - core, 1, keepdims=False).astype(low)
    return (keep.astype(wide) + swap_core(give).astype(wide)).astype(low)


def on_device(
    latents, cond, cotangent, w_qkv, bias_qv, w_proj, b_proj, w_fc1, b_fc1, w_fc2, b_fc2, w_ada, b_ada
):
    stream_low = latents[0]
    upstream_low = cotangent[0]
    rows, features = stream_low.shape
    shards = 8
    length = shards * rows
    own = features // shards
    half = own // 2
    units = w_fc2.shape[0]
    ada_width = w_ada.shape[1]
    ada_rows = ada_width // LANES
    place = lax.axis_index(SHARD)
    core = lax.axis_index("core")

    cond_value = cond.astype(wide)
    cond_silu, silu_pull = jax.vjp(silu, cond_value)
    cond_low = cond_silu.astype(low)
    cond_own = lax.dynamic_slice_in_dim(cond_low, place * own, own, 1)
    mod_part = mul(cond_own, w_ada)[0]
    blocks = jnp.arange(shards)[:, None] == place
    mod_part = mod_part + jnp.where(blocks, b_ada.astype(wide)[None, :], 0.0).reshape(ada_width)
    small = jnp.concatenate([mod_part.astype(low), bias_qv, b_proj, b_fc2])

    def halved(value):
        return lax.dynamic_slice_in_dim(value, core * half, half, 0)

    qkv_mine = halved(w_qkv)

    def qkv_part(part):
        return jnp.stack(
            [
                qkv_mine[:, part * features + k * own : part * features + (k + 1) * own]
                for k in range(shards)
            ]
        )

    first_sent = jnp.concatenate(
        [
            copies(stream_low),
            jnp.concatenate([qkv_part(0), qkv_part(1)], axis=1),
            jnp.concatenate([qkv_part(2), copies(as_rows(small, half))], axis=1),
        ],
        axis=2,
    )
    first_got = exchange(first_sent)
    weights_sent = jnp.concatenate(
        [
            halved(w_fc1).reshape(half, shards, units).transpose(1, 0, 2),
            copies(halved(w_proj)),
        ],
        axis=2,
    )
    weights_sent, first_got = lax.optimization_barrier((weights_sent, first_got))
    weights_got = exchange(weights_sent)
    near = first_got[:, :, features : features + own]
    far = first_got[:, :, features + own :]
    qkv_got = jnp.concatenate([near[:, :half], near[:, half:], far[:, :half]], axis=2)
    wq = join_rows(qkv_got, swap_core(qkv_got), core)
    small_got = far[:, half:].astype(wide)
    modulation = jnp.sum(small_got[:, :ada_rows], axis=0).reshape(1, ada_width)
    shift_first, scale_first, gate_first, shift_second, scale_second, gate_second = jnp.split(
        modulation, 6, axis=1
    )
    at = ada_rows
    bias_wide = small_got[:, at : at + 2].reshape(1, 2 * features)
    proj_bias = small_got[:, at + 2].reshape(1, features)
    second_bias = small_got[:, at + 3].reshape(1, features)

    query_bias = lax.dynamic_slice_in_dim(bias_wide, place * own, own, 1)
    value_bias = lax.dynamic_slice_in_dim(bias_wide, features + place * own, own, 1)
    attend_in, queries, keyset, valueset, mixed, log_total = attend(
        first_got, wq, scale_first, shift_first, query_bias, value_bias
    )
    mixed, weights_got = lax.optimization_barrier((mixed, weights_got))
    mixed_got = exchange(
        jnp.concatenate([mixed.reshape(shards, rows, own), copies(upstream_low)], axis=2)
    )
    weights_other = swap_core(weights_got)
    w1 = join_rows(weights_got[:, :, :units], weights_other[:, :, :units], core)
    wp = join_rows(weights_got[:, :, units:], weights_other[:, :, units:], core)
    mixed_tok = mixed_got[:, :, :own].transpose(1, 0, 2).reshape(rows, features)
    upstream_all = mixed_got[:, :, own:].reshape(length, features)
    branch = mul(mixed_tok, wp) + proj_bias
    stream = stream_low.astype(wide)
    middle = stream + gate_first * branch
    norm_second, inverse_second = normalize(middle)
    feed_in = (norm_second * (1.0 + scale_second) + shift_second).astype(low)
    feed_got = exchange(copies(feed_in))
    (
        feed_part,
        second_low,
        active,
        grad_hidden,
        grad_branch_second,
        gate_sums,
        second_bias_sums,
        hidden_sums,
    ) = gated(feed_got, w1, b_fc1.astype(wide)[None, :], w_fc2, mixed_got, gate_second)
    feed_back = exchange(feed_part)
    term_first, term_second = weights_back(
        feed_got.reshape(length, features), grad_hidden, active, grad_branch_second, shards
    )
    term_first = swap_add(term_first, core)
    feed_back, term_first, term_second = lax.optimization_barrier(
        (feed_back, term_first, term_second)
    )
    grad_feed = jnp.sum(feed_back.astype(wide), axis=0)

    upstream = upstream_low.astype(wide)
    grad_gate_second = gate_sums[0] + second_bias[0] * jnp.sum(upstream, axis=0)
    grad_scale_second = jnp.sum(grad_feed * norm_second, axis=0)
    grad_shift_second = jnp.sum(grad_feed, axis=0)
    grad_middle = upstream + normalize_back(
        norm_second, inverse_second, grad_feed * (1.0 + scale_second)
    )
    grad_gate_first = jnp.sum(grad_middle * branch, axis=0)
    grad_branch = (grad_middle * gate_first).astype(low)
    grad_mixed_tok = mul_t(grad_branch, wp).astype(low)
    grad_mixed = exchange(grad_mixed_tok.reshape(rows, shards, own).transpose(1, 0, 2))
    term_proj = proj_back(mixed_got, grad_branch, own)
    term_proj, grad_mixed = lax.optimization_barrier((term_proj, grad_mixed))
    pair_got = exchange(jnp.concatenate([term_first, swap_add(term_proj, core)], axis=2))
    attend_part, term_qkv, attend_sums, packed_sums = attend_back(
        queries, grad_mixed.reshape(length, own), log_total, keyset, valueset, wq, attend_in, first_got
    )
    attend_part, term_qkv, attend_sums, packed_sums, pair_got = lax.optimization_barrier(
        (attend_part, term_qkv, attend_sums, packed_sums, pair_got)
    )
    packed_sums = packed_sums[0]
    grad_shift_first = attend_sums[0]
    grad_scale_first = attend_sums[1]
    mod_terms = jnp.concatenate(
        [
            grad_shift_first,
            grad_scale_first,
            grad_gate_first,
            grad_shift_second,
            grad_scale_second,
            grad_gate_second,
            jnp.sum(grad_branch.astype(wide), axis=0),
            packed_sums[:own],
            packed_sums[2 * own :],
        ]
    ).astype(low)
    term_qkv = core_half(term_qkv.reshape(shards, 2, half, 3 * own), core)
    last_sent = jnp.concatenate(
        [
            attend_part,
            jnp.concatenate([term_qkv[:, :, :own], term_qkv[:, :, own : 2 * own]], axis=1),
            jnp.concatenate(
                [term_qkv[:, :, 2 * own :], copies(as_rows(mod_terms, half))], axis=1
            ),
        ],
        axis=2,
    )
    last_got = exchange(last_sent)
    second_low, last_got = lax.optimization_barrier((second_low, last_got))
    second_own = lax.dynamic_index_in_dim(second_low, place, 0, keepdims=False).astype(wide)
    second_near = scatter_sum(second_own, second_low, place, ((0, 1), (0, 3), (0, 2)))
    grad_attend = jnp.sum(last_got[:, :, :features].astype(wide), axis=0)
    near = last_got[:, :, features : features + own]
    far = last_got[:, :, features + own :]
    term_qkv = jnp.concatenate([near[:, :half], near[:, half:], far[:, :half]], axis=2)
    mod_got = far[:, half:].astype(wide)
    head_rows = ada_rows + features // LANES
    mod_sums = jnp.sum(mod_got[:, :head_rows], axis=0)
    bias_qv_all = jnp.concatenate(
        [mod_got[:, head_rows].reshape(features), mod_got[:, head_rows + 1].reshape(features)]
    )
    norm_own, inverse_own = normalize(stream)
    grad_stream = grad_middle + normalize_back(
        norm_own, inverse_own, grad_attend * (1.0 + scale_first)
    )
    grad_latents = grad_stream.astype(low)

    grad_modulation = mod_sums[:ada_rows].reshape(ada_width)
    proj_bias_term = lax.dynamic_slice_in_dim(mod_sums, ada_rows + place, 1, 0)
    cond_term = jnp.sum(w_ada.astype(wide) * grad_modulation[None, :], axis=1)
    cond_total = gather_small(cond_term[None], place).reshape(1, features)
    grad_cond = silu_pull(cond_total)[0]

    second_bias_sums = second_bias_sums[0]
    rep_terms = jnp.concatenate(
        [
            mod_sums[:ada_rows],
            cond_own.astype(wide),
            proj_bias_term,
            hidden_sums.reshape(units // LANES, LANES),
            lax.dynamic_slice_in_dim(second_bias_sums, place * own, own, 0)[None],
            lax.dynamic_slice_in_dim(bias_qv_all, place * 2 * own, 2 * own, 0).reshape(2, own),
        ]
    )
    rep_terms = jnp.pad(rep_terms, ((0, half - rep_terms.shape[0]), (0, 0))).astype(low)
    rep_terms = jnp.concatenate([rep_terms, swap_core(rep_terms)], axis=1)

    term_first = pair_got[:, :, :units]
    term_proj = jnp.sum(pair_got[:, :, units:].astype(wide), axis=0).astype(low)
    term_second = swap_add(term_second.reshape(2, units // 2, features), core)
    piece = units // 2 // shards
    term_second = term_second.reshape(shards, piece, features)
    fold = features // 2

    rep_sent = jnp.concatenate(
        [
            term_first,
            jnp.concatenate([term_second[:, :, :fold], term_second[:, :, fold:]], axis=1),
            term_qkv,
            term_proj.reshape(half, shards, own).transpose(1, 0, 2),
            copies(rep_terms),
        ],
        axis=2,
    )
    rep_got = exchange(rep_sent, CHIPS)
    width = units + fold + 4 * own
    owned = jnp.sum(rep_got[:, :, :width].astype(wide), axis=0).astype(low)
    rep_small = jnp.concatenate(
        [rep_got[:, :, width : width + own], rep_got[:, :, width + own :]], axis=0
    )
    grad_w_ada = t_mul(
        rep_small[:, ada_rows], rep_small[:, :ada_rows].reshape(2 * shards, ada_width)
    )
    rep_sums = jnp.sum(rep_small.astype(wide), axis=0)
    ada_own = ada_rows // shards
    grad_b_ada = lax.dynamic_slice_in_dim(rep_sums, place * ada_own, ada_own, 0)
    grad_b_ada = grad_b_ada.reshape(ada_width // shards)
    at = ada_rows + 1
    grad_b_proj = rep_sums[at]
    at += 1
    grad_b_fc1 = rep_sums[at : at + units // LANES].reshape(units)
    at += units // LANES
    grad_b_fc2 = rep_sums[at]
    grad_bias_qv = rep_sums[at + 1 : at + 3].reshape(2 * own)

    owned, second_near = lax.optimization_barrier((owned, second_near))
    whole_mine = exchange(copies(owned), CHIPS)
    branch_second = (
        scatter_sum(second_near, second_low, place, ((1, 0), (1, 1), (1, 3), (1, 2)))
        + second_bias
    )
    output = (middle + gate_second * branch_second).astype(low)
    whole_mine, grad_w_ada = lax.optimization_barrier((whole_mine, grad_w_ada))
    grad_w_fc1, grad_w_fc2, grad_w_qkv, grad_w_proj = unpack(
        core.astype(jnp.int32)[None], whole_mine, swap_core(whole_mine), units, features
    )

    return (
        output[None],
        grad_latents[None],
        grad_cond,
        grad_w_qkv,
        grad_bias_qv,
        grad_w_proj,
        grad_b_proj,
        grad_w_fc1,
        grad_b_fc1,
        grad_w_fc2,
        grad_b_fc2,
        grad_w_ada,
        grad_b_ada,
    )


def solution(mesh):
    fine = Mesh(mesh.devices.reshape(2, 4, 2, 2, 4), REP + SHARD)
    tokens = P(REP, SHARD, None)
    matrix = P(SHARD, None)
    vector = P(SHARD)
    params = (matrix, vector) * 5
    return jax.shard_map(
        on_device,
        mesh=fine,
        in_specs=(tokens, P(REP, None), tokens) + params,
        out_specs=(tokens, tokens, P(REP, None)) + params,
        check_vma=False,
    )
```
